32 devices in a mesh: ctx: 8 (over y, x, core), batch: 4 (over z).
Axes of the slice: x: 2, y: 2, z: 4, core: 2. Of those that a mesh axis runs over, the one named last changes fastest.
Arguments:
- queries: bfloat16 [4, 2048, 2048], P('batch', 'ctx'), may hold values from -120 to 120
- keys: bfloat16 [4, 2048, 512], P('batch', 'ctx'), may hold values from -6 to 6
- values: bfloat16 [4, 2048, 512], P('batch', 'ctx'), may hold values from -6 to 6
- tau: float32 [16], replicated, may hold values from 0.5 to 2
- out_grad: bfloat16 [4, 2048, 2048], P('batch', 'ctx'), may hold values from -18 to 18
- key_blocks: int32 [4, 16, 13], replicated, may hold values from 0 to 15, as said below
Outputs:
- attended: bfloat16 [4, 2048, 2048], P('batch', 'ctx')
- query_grad: bfloat16 [4, 2048, 2048], P('batch', 'ctx')
- key_grad: bfloat16 [4, 2048, 512], P('batch', 'ctx')
- value_grad: bfloat16 [4, 2048, 512], P('batch', 'ctx')
- tau_grad: float32 [16], replicated
The draws below stay inside these ranges and needn't reach their ends.
Inputs may be any that keep to these rules, and one draw needn't show every extreme that they name: `key_blocks`: row a of head group g lists a - 1, a, a + 1, then a + m s and a - m s for m = 1 to 5, all modulo 16, with a stride s of 2 or 3 drawn for each group and row.
All inputs are finite; a program needn't handle non-finite values.
Results may differ from the reference program's by a relative error of at most 0.0051.
Values may be sent and summed in bfloat16 or wider, within the bound.
No kernel may reach another device: no remote copies, remote signals or barrier semaphores. Data moves between devices by JAX's collectives and lax.ppermute only.
A program may use at most 192 MiB of HBM per device.

```python
import math
import jax
import jax.numpy as jnp
from jax import lax

HEADS = 16
KV_HEADS = 4
HD = 128
BLOCK = 128
KMAX = 13
QPG = 4
BATCHES = 4
SEQ = 2048
NB = 16


def paired(key):
    base_keys = jnp.clip(jax.random.normal(jax.random.fold_in(key, 11), (BATCHES, SEQ, KV_HEADS, HD), jnp.float32), -6.0, 6.0)
    base_queries = jnp.clip(jax.random.normal(jax.random.fold_in(key, 12), (BATCHES, SEQ, KV_HEADS, QPG, HD), jnp.float32), -6.0, 6.0)
    return (base_keys, base_queries)


def draw_keys(key, part):
    base_keys, base_queries = paired(key)
    return base_keys.reshape(BATCHES, SEQ, KV_HEADS * HD).astype(jnp.bfloat16)


def draw_queries(key, part):
    base_keys, base_queries = paired(key)
    return base_queries.reshape(BATCHES, SEQ, HEADS * HD).astype(jnp.bfloat16)


def draw_out_grad(key, part):
    ramp = 1.0 + 2.0 * jnp.arange(SEQ, dtype=jnp.float32) / SEQ
    noise = jnp.clip(jax.random.normal(jax.random.fold_in(key, 22), (BATCHES, SEQ, HEADS * HD), jnp.float32), -6.0, 6.0)
    return (noise * ramp[None, :, None]).astype(jnp.bfloat16)


def draw_key_blocks(key, part):
    stride = jax.random.randint(jax.random.fold_in(key, 31), (KV_HEADS, NB, 1), 2, 4)
    rows = jnp.arange(NB, dtype=jnp.int32)[None, :, None]
    band = jnp.array([-1, 0, 1], jnp.int32)[None, None, :] + jnp.zeros((KV_HEADS, NB, 1), jnp.int32)
    multiples = jnp.arange(1, (KMAX - 3) // 2 + 1, dtype=jnp.int32)[None, None, :]
    offsets = jnp.concatenate([band, stride * multiples, -stride * multiples], axis=2)
    return ((rows + offsets) % NB).astype(jnp.int32)


def block_scale(own_key, shape, shards, least, high):
    def one(dim, blocks):
        steps = jax.random.uniform(jax.random.fold_in(jax.random.fold_in(own_key, 6), dim), (blocks,), jnp.float32, least / len(shards), high / len(shards))
        return jnp.repeat(jnp.exp(steps), shape[dim] // blocks).reshape((-1,) + (1,) * (len(shape) - dim - 1))

    level = one(*shards[0])
    for cut in shards[1:]:
        level = level * one(*cut)
    return level


def centred(rng, extent, deviation, bound, pieces=(), held_as=jnp.bfloat16):
    gain = block_scale(rng, extent, pieces, -0.22, 0.18) if pieces else 1.0
    values = jax.random.normal(rng, extent, jnp.float32) * deviation * gain
    return jnp.minimum(jnp.maximum(values, -bound), bound).astype(held_as)


def setup_inputs(seed: int = 0) -> dict:
    splits = jax.random.split(jax.random.key(seed), 7)
    queries = draw_queries(jax.random.fold_in(splits[6], 71), 0)
    keys = draw_keys(jax.random.fold_in(splits[6], 71), 0)
    values = centred(splits[2], (BATCHES, SEQ, KV_HEADS * HD), 1.0, 6.0, ((0, 4), (1, 8)))
    tau = jnp.clip(jnp.exp(jax.random.uniform(splits[3], (HEADS,), jnp.float32, math.log(0.5), math.log(2.0))), 0.5, 2.0)
    out_grad = draw_out_grad(jax.random.fold_in(splits[6], 71), 0)
    key_blocks = draw_key_blocks(jax.random.fold_in(splits[6], 71), 0)
    return {"queries": queries, "keys": keys, "values": values, "tau": tau, "out_grad": out_grad, "key_blocks": key_blocks}


highest = lax.Precision.HIGHEST

def low_round(array):
    return lax.optimization_barrier(array.astype(jnp.bfloat16)).astype(jnp.float32)

def one_group(query_block, grad_block, key_group, value_group, listed, scale_row):
    key_rows = jnp.take(key_group, listed, axis=0).reshape(KMAX * BLOCK, HD).astype(jnp.float32)
    value_rows = jnp.take(value_group, listed, axis=0).reshape(KMAX * BLOCK, HD).astype(jnp.float32)
    query_rows = query_block.astype(jnp.float32)
    grad_rows = grad_block.astype(jnp.float32)
    raw_scores = jnp.einsum('qhd,kd->hqk', query_rows, key_rows, precision=highest)
    weights = jax.nn.softmax(raw_scores * scale_row[:, None, None], axis=-1)
    probs_low = low_round(weights)
    result = jnp.einsum('hqk,kd->qhd', probs_low, value_rows, precision=highest)
    row_dot = lax.optimization_barrier(jnp.sum(grad_rows * result, axis=-1))
    dweights = jnp.einsum('qhd,kd->hqk', grad_rows, value_rows, precision=highest)
    dscores = weights * (dweights - row_dot.T[:, :, None])
    scale_part = lax.optimization_barrier(jnp.sum(dscores * raw_scores, axis=(1, 2))) / math.sqrt(HD)
    scaled = low_round(dscores * scale_row[:, None, None])
    query_part = jnp.einsum('hqk,kd->qhd', scaled, key_rows, precision=highest)
    key_part = jnp.einsum('hqk,qhd->kd', scaled, query_rows, precision=highest)
    value_part = jnp.einsum('hqk,qhd->kd', probs_low, grad_rows, precision=highest)
    return (result, query_part, key_part.reshape(KMAX, BLOCK, HD), value_part.reshape(KMAX, BLOCK, HD), scale_part)

def reference(queries, keys, values, tau, out_grad, key_blocks):
    nblocks = SEQ // BLOCK
    scale_all = (tau.astype(jnp.float32) / math.sqrt(HD)).reshape(KV_HEADS, QPG)
    group_ids = jnp.arange(KV_HEADS, dtype=jnp.int32)
    outputs = []
    query_grads = []
    key_grads = []
    value_grads = []
    scale_total = jnp.zeros((KV_HEADS, QPG), jnp.float32)
    for seq_index in range(BATCHES):
        query_seq = queries[seq_index].reshape(nblocks, BLOCK, KV_HEADS, QPG, HD)
        grad_seq = out_grad[seq_index].reshape(nblocks, BLOCK, KV_HEADS, QPG, HD)
        key_seq = keys[seq_index].reshape(nblocks, BLOCK, KV_HEADS, HD).transpose(2, 0, 1, 3)
        value_seq = values[seq_index].reshape(nblocks, BLOCK, KV_HEADS, HD).transpose(2, 0, 1, 3)

        def step_fn(state_in, index):
            key_acc, value_acc, scale_acc = state_in
            query_block = query_seq[index].transpose(1, 0, 2, 3)
            grad_block = grad_seq[index].transpose(1, 0, 2, 3)
            listed = key_blocks[:, index, :].astype(jnp.int32)
            result, query_part, key_part, value_part, scale_part = jax.vmap(one_group)(query_block, grad_block, key_seq, value_seq, listed, scale_all)
            key_acc = key_acc.at[group_ids[:, None], listed].add(key_part)
            value_acc = value_acc.at[group_ids[:, None], listed].add(value_part)
            return ((key_acc, value_acc, scale_acc + scale_part), (result, query_part))
        zeros = jnp.zeros((KV_HEADS, nblocks, BLOCK, HD), jnp.float32)
        start = (zeros, zeros, jnp.zeros((KV_HEADS, QPG), jnp.float32))
        (key_acc, value_acc, scale_acc), (results, query_parts) = lax.scan(step_fn, start, jnp.arange(nblocks, dtype=jnp.int32))
        outputs.append(results.transpose(0, 2, 1, 3, 4).reshape(SEQ, HEADS * HD).astype(jnp.bfloat16))
        query_grads.append(query_parts.transpose(0, 2, 1, 3, 4).reshape(SEQ, HEADS * HD).astype(jnp.bfloat16))
        key_grads.append(key_acc.transpose(1, 2, 0, 3).reshape(SEQ, KV_HEADS * HD).astype(jnp.bfloat16))
        value_grads.append(value_acc.transpose(1, 2, 0, 3).reshape(SEQ, KV_HEADS * HD).astype(jnp.bfloat16))
        scale_total = scale_total + scale_acc
    tau_grad = scale_total.reshape(HEADS) / math.sqrt(BATCHES * SEQ)
    return (jnp.stack(outputs), jnp.stack(query_grads), jnp.stack(key_grads), jnp.stack(value_grads), tau_grad)
```

```python
import functools
import math

import jax
import jax.numpy as jnp
from jax import lax
from jax.experimental import pallas as pl
from jax.experimental.pallas import tpu as pltpu
from jax.sharding import PartitionSpec as P

HEADS = 16
KV_HEADS = 4
HD = 128
BLOCK = 128
QPG = HEADS // KV_HEADS
ROWS = QPG * BLOCK
STRIDES = (2, 3)
CHUNK = 3
LOG2E = math.log2(math.e)
NEVER = -1e30


def distinct_bound(block_count, listed_count):
    most = 0
    for stride in STRIDES:
        steps = range(1, (listed_count - 3) // 2 + 1)
        offsets = [-1, 0, 1] + [stride * m for m in steps] + [-stride * m for m in steps]
        most = max(most, len({o % block_count for o in offsets}))
    return most


def nt(a, b):
    return jnp.dot(a, b, preferred_element_type=jnp.float32)


def group_kernel(listed, pieces, *refs):
    slots, bias, _ = refs[:3]
    q_own, q_sib, g_own, g_sib, coef = refs[3:8]
    kv_in = refs[8 : 8 + pieces]
    att_own, dq_own, sib_out, tau_out = refs[8 + pieces : 12 + pieces]
    kv_out = refs[12 + pieces : 12 + 2 * pieces]
    k_s, v_s, kt_s, vt_s, dk_s, dv_s, e_s, dp_s, p_s, ds_s = refs[12 + 2 * pieces :]
    unit = pl.program_id(0)

    @pl.when(unit == 0)
    def _():
        for i in range(pieces):
            for half in range(2):
                rows = slice(half * BLOCK, (half + 1) * BLOCK)
                k_block = kv_in[i][0, rows, :]
                v_block = kv_in[i][1, rows, :]
                k_s[2 * i + half] = k_block
                v_s[2 * i + half] = v_block
                kt_s[2 * i + half] = k_block.T
                vt_s[2 * i + half] = v_block.T
        dk_s[...] = jnp.zeros_like(dk_s)
        dv_s[...] = jnp.zeros_like(dv_s)
        tau_out[...] = jnp.zeros_like(tau_out)

    own = unit < 2
    q_here = jnp.where(own, q_own[...], q_sib[0])
    g_here = jnp.where(own, g_own[...], g_sib[0])

    def per_head(x):
        return [x[:, h * HD : (h + 1) * HD] for h in range(QPG)]

    q_rows = jnp.concatenate(per_head(q_here), axis=0)
    g_rows = jnp.concatenate(per_head(g_here), axis=0)
    q_t = jnp.concatenate([x.T for x in per_head(q_here)], axis=1)
    g_t = jnp.concatenate([x.T for x in per_head(g_here)], axis=1)
    factor = coef[0:1, :]
    scale = coef[1:2, :]
    ids = [slots[unit, j] for j in range(listed)]
    chunks = [range(c, min(c + CHUNK, listed)) for c in range(0, listed, CHUNK)]

    def rows_of(c):
        return slice(c[0] * BLOCK, (c[-1] + 1) * BLOCK)

    most = None
    for c in chunks:
        raw = nt(jnp.concatenate([k_s[ids[j]] for j in c], axis=0), q_t)
        e_s[rows_of(c), :] = raw
        top = jnp.max(raw.reshape(-1, 8, ROWS), axis=0)
        most = top if most is None else jnp.maximum(most, top)
    top_row = jnp.max(most, axis=0, keepdims=True) * factor

    total = jnp.zeros((8, ROWS), jnp.float32)
    for c in chunks:
        dp_s[rows_of(c), :] = nt(jnp.concatenate([v_s[ids[j]] for j in c], axis=0), g_t)
        for j in c:
            rows = slice(j * BLOCK, (j + 1) * BLOCK)
            e = jnp.exp2(e_s[rows, :] * factor - (top_row - bias[unit, j]))
            e_s[rows, :] = e
            total = total + jnp.sum(e.reshape(-1, 8, ROWS), axis=0)
    inverse = 1.0 / jnp.sum(total, axis=0, keepdims=True)

    for c in chunks:
        probs = (e_s[rows_of(c), :] * inverse).astype(jnp.bfloat16)
        p_s[rows_of(c), :] = probs
        part = nt(probs, g_rows)
        for n, j in enumerate(c):
            dv_s[ids[j]] += part[n * BLOCK : (n + 1) * BLOCK, :]
    o_t = nt(jnp.concatenate([vt_s[s] for s in ids], axis=1), p_s[...])
    row_dot = jnp.sum(g_t.astype(jnp.float32) * o_t, axis=0, keepdims=True)

    weight_scale = inverse * scale
    for c in chunks:
        scaled = (e_s[rows_of(c), :] * weight_scale * (dp_s[rows_of(c), :] - row_dot)).astype(
            jnp.bfloat16
        )
        ds_s[rows_of(c), :] = scaled
        part = nt(scaled, q_rows)
        for n, j in enumerate(c):
            dk_s[ids[j]] += part[n * BLOCK : (n + 1) * BLOCK, :]
    dq_t = nt(jnp.concatenate([kt_s[s] for s in ids], axis=1), ds_s[...])
    tau_out[...] += jnp.sum(q_t.astype(jnp.float32) * dq_t, axis=0, keepdims=True)

    def back(x):
        low = x.astype(jnp.bfloat16)
        return jnp.concatenate([y.T for y in per_head(low)], axis=1)

    att = back(o_t)
    dq = back(dq_t)

    @pl.when(own)
    def _():
        att_own[...] = att
        dq_own[...] = dq

    @pl.when(jnp.logical_not(own))
    def _():
        sib_out[0] = att
        sib_out[1] = dq

    @pl.when(unit == 3)
    def _():
        for i in range(pieces):
            for half in range(2):
                rows = slice(half * BLOCK, (half + 1) * BLOCK)
                kv_out[i][0, rows, :] = dk_s[2 * i + half].astype(jnp.bfloat16)
                kv_out[i][1, rows, :] = dv_s[2 * i + half].astype(jnp.bfloat16)


def run_group(gi, slots, bias, column, queries, q_sib, out_grad, g_sib, coef, pieces_in):
    listed = slots.shape[1]
    pieces = len(pieces_in)
    tokens = queries.shape[0]
    width = QPG * HD
    own_map = lambda u, s, b, c: (jnp.minimum(u, 1), c[0])
    sib_map = lambda u, s, b, c: (0, jnp.maximum(u - 2, 0), 0)
    whole3 = pl.BlockSpec((2, tokens, HD), lambda u, s, b, c: (0, 0, 0))
    block_own = pl.BlockSpec((BLOCK, width), own_map)
    out_own = pl.BlockSpec((BLOCK, width), lambda u, s, b, c: (jnp.minimum(u, 1), 0))
    bf = lambda *shape: jax.ShapeDtypeStruct(shape, jnp.bfloat16)
    slot_count = 2 * pieces
    keys_wide = listed * BLOCK
    qs = pl.BlockSpec((1, BLOCK, width), lambda u, s, b, c: (0, jnp.maximum(u - 2, 0), 0))
    gs = pl.BlockSpec((1, BLOCK, width), lambda u, s, b, c: (1, jnp.maximum(u - 2, 0), 0))
    macs = 4 * ROWS * keys_wide * HD * 6
    return pl.pallas_call(
        functools.partial(group_kernel, listed, pieces),
        grid_spec=pltpu.PrefetchScalarGridSpec(
            num_scalar_prefetch=3,
            grid=(4,),
            in_specs=[block_own, qs, block_own, gs, pl.BlockSpec((8, ROWS), lambda u, s, b, c: (0, 0))]
            + [whole3] * pieces,
            out_specs=[
                out_own,
                out_own,
                pl.BlockSpec((2, BLOCK, width), sib_map),
                pl.BlockSpec((1, ROWS), lambda u, s, b, c: (0, 0)),
            ]
            + [whole3] * pieces,
            scratch_shapes=[pltpu.VMEM((slot_count, BLOCK, HD), jnp.bfloat16)] * 4
            + [pltpu.VMEM((slot_count, BLOCK, HD), jnp.float32)] * 2
            + [pltpu.VMEM((keys_wide, ROWS), jnp.float32)] * 2
            + [pltpu.VMEM((keys_wide, ROWS), jnp.bfloat16)] * 2,
        ),
        out_shape=[bf(tokens, width), bf(tokens, width), bf(2, tokens, width)]
        + [jax.ShapeDtypeStruct((1, ROWS), jnp.float32)]
        + [bf(2, tokens, HD)] * pieces,
        compiler_params=pltpu.CompilerParams(
            dimension_semantics=("arbitrary",), vmem_limit_bytes=48 * 2**20
        ),
        cost_estimate=pl.CostEstimate(
            flops=2 * macs, bytes_accessed=6 * 2**20, transcendentals=4 * ROWS * keys_wide
        ),
        name="group_attention",
    )(slots, bias, column, queries, q_sib, out_grad, g_sib, coef, *pieces_in)


def body(queries, keys, values, tau, out_grad, key_blocks):
    ctx = lax.axis_size("ctx")
    me = lax.axis_index("ctx")
    pair, core = me // 2, me % 2
    pairs = ctx // 2
    tokens = queries.shape[1]
    local_blocks = tokens // BLOCK
    pair_blocks = 2 * local_blocks
    block_count = ctx * local_blocks
    listed_count = key_blocks.shape[2]
    block_reach = max(STRIDES) * ((listed_count - 3) // 2)
    reach = (block_reach + pair_blocks - 1) // pair_blocks
    everyone = 2 * reach + 1 >= pairs
    by_xor = everyone and pairs & (pairs - 1) == 0
    if everyone:
        offsets = list(range(pairs))
    else:
        offsets = [o % pairs for o in range(-reach, reach + 1)]
        offsets.remove(0)
        offsets.insert(0, 0)

    def moved(p, r, sign):
        return p ^ r if by_xor else (p + sign * r) % pairs

    def route(r, cx, sign):
        return [
            (2 * p + k, 2 * moved(p, r, sign) + (k ^ cx)) for p in range(pairs) for k in range(2)
        ]

    def send(x, r, cx, sign):
        return lax.ppermute(x, "ctx", route(r, cx, sign))

    def columns(x, group, width):
        return lax.dynamic_slice_in_dim(x, group * width, width, 1)

    q0, k0, v0, g0 = queries[0], keys[0], values[0], out_grad[0]
    wide = QPG * HD
    order = [(r, cx) for r in offsets for cx in range(2)]

    units = jnp.arange(4)
    unit_block = pair * pair_blocks + (core ^ (units // 2)) * local_blocks + units % 2
    rel_of = jnp.array([offsets.index(r) if r in offsets else 0 for r in range(pairs)], jnp.int32)
    block_pair = key_blocks // pair_blocks
    relative = block_pair ^ pair if by_xor else (pair - block_pair) % pairs
    rel_index = jnp.sum(
        jnp.where(relative[..., None] == jnp.arange(pairs), rel_of, 0), axis=-1
    )
    slot = (
        rel_index * pair_blocks
        + ((key_blocks // local_blocks) % 2 ^ core) * local_blocks
        + key_blocks % local_blocks
    )
    listed = distinct_bound(block_count, listed_count)

    def lists(group):
        rows = jnp.take(lax.dynamic_index_in_dim(slot, group, 0, keepdims=False), unit_block, axis=0)
        same = rows[:, :, None] == rows[:, None, :]
        times = jnp.sum(same, axis=2)
        earlier = jnp.tril(jnp.ones((listed_count, listed_count), bool), -1)
        first = jnp.logical_not(jnp.any(same & earlier, axis=2))
        rank = jnp.sum(
            first[:, None, :] & jnp.tril(jnp.ones((listed_count, listed_count), bool)), axis=2
        ) - 1
        place = (rank[:, None, :] == jnp.arange(listed)[:, None]) & first[:, None, :]
        used = jnp.any(place, axis=2)
        chosen = jnp.where(used, jnp.sum(jnp.where(place, rows[:, None, :], 0), axis=2), rows[:, :1])
        count = jnp.sum(jnp.where(place, times[:, None, :], 0), axis=2)
        bias = jnp.where(
            count == 0,
            NEVER,
            jnp.where(count == 1, 0.0, jnp.where(count == 2, 1.0, jnp.log2(count.astype(jnp.float32)))),
        )
        return chosen.astype(jnp.int32), bias.astype(jnp.float32)

    att_parts, dq_parts, grads, tau_parts = [], [], [], []
    for gi in range(2):
        mine = 2 * core + gi
        theirs = 2 * (1 - core) + gi
        kv_same = jnp.stack([columns(k0, mine, HD), columns(v0, mine, HD)])
        kv_other = jnp.stack([columns(k0, theirs, HD), columns(v0, theirs, HD)])
        pieces = [
            kv_same if (r, cx) == (0, 0) else send((kv_same, kv_other)[cx], r, cx, 1)
            for r, cx in order
        ]
        qg_sib = send(jnp.stack([columns(q0, theirs, wide), columns(g0, theirs, wide)]), 0, 1, 1)
        tau_group = lax.dynamic_slice_in_dim(tau, mine * QPG, QPG, 0)
        scale = jnp.repeat(tau_group / math.sqrt(HD), BLOCK)[None]
        coef = jnp.concatenate([scale * LOG2E, scale, jnp.zeros((6, ROWS), jnp.float32)], axis=0)
        slots, bias = lists(mine)
        out = run_group(
            gi, slots, bias, mine[None].astype(jnp.int32), q0, qg_sib, g0, qg_sib, coef, pieces
        )
        att_own, dq_own, sib, tau_rows = out[:4]
        kv_grads = out[4:]
        sib = send(sib, 0, 1, 1)
        att_parts.append((att_own, sib[0]))
        dq_parts.append((dq_own, sib[1]))
        received = [
            x if (r, cx) == (0, 0) else send(x, r, cx, -1) for (r, cx), x in zip(order, kv_grads)
        ]
        grads.append([[x for (r, c), x in zip(order, received) if c == cx] for cx in range(2)])
        tau_parts.append(jnp.sum(tau_rows.reshape(QPG, BLOCK), axis=1) / tau_group)

    def by_group(parts):
        return jnp.concatenate(
            [jnp.where(core == c // 2, parts[c % 2][0], parts[c % 2][1]) for c in range(4)], axis=1
        )

    attended = by_group(att_parts)[None]
    query_grad = by_group(dq_parts)[None]

    def summed(which):
        cols = []
        for c in range(4):
            total = None
            for a, b in zip(*grads[c % 2]):
                term = jnp.where(core == c // 2, a[which], b[which]).astype(jnp.float32)
                total = term if total is None else total + term
            cols.append(total.astype(jnp.bfloat16))
        return jnp.concatenate(cols, axis=1)[None]

    key_grad, value_grad = summed(0), summed(1)
    mine = jnp.concatenate(tau_parts)
    placed = lax.dynamic_update_slice_in_dim(
        jnp.zeros((HEADS,), jnp.float32), mine, core * 2 * QPG, 0
    )
    scale_total = jnp.sum(lax.all_gather(placed, ("ctx", "batch")), axis=0)
    tau_grad = scale_total / math.sqrt(lax.axis_size("batch") * ctx * tokens)
    return (attended, query_grad, key_grad, value_grad, tau_grad)


def solution(mesh):
    rows = P("batch", "ctx", None)
    return jax.shard_map(
        body,
        mesh=mesh,
        in_specs=(rows, rows, rows, P(), rows, P()),
        out_specs=(rows, rows, rows, rows, P()),
        check_vma=False,
    )
```

```python
import functools
import math

import jax
import jax.numpy as jnp
from jax import lax
from jax.experimental import pallas as pl
from jax.experimental.pallas import tpu as pltpu
from jax.sharding import PartitionSpec as P

HEADS = 16
KV_HEADS = 4
HD = 128
BLOCK = 128
QPG = HEADS // KV_HEADS
ROWS = QPG * BLOCK
STRIDES = (2, 3)
CHUNK = 3
LOG2E = math.log2(math.e)
NEVER = -1e30


def distinct_offsets(block_count, listed_count):
    tables = []
    for stride in STRIDES:
        steps = range(1, (listed_count - 3) // 2 + 1)
        listed = [-1, 0, 1] + [stride * m for m in steps] + [-stride * m for m in steps]
        times = {}
        for o in listed:
            times[o % block_count] = times.get(o % block_count, 0) + 1
        tables.append(sorted(times.items()))
    most = max(len(t) for t in tables)
    return [t + [(0, 0)] * (most - len(t)) for t in tables]


def nt(a, b):
    return jnp.dot(a, b, preferred_element_type=jnp.float32)


def group_kernel(gi, devices, local_blocks, listed, offsets, *refs):
    place, strides, taus = refs[:3]
    q_own, q_sib, g_own, g_sib, kv_in, tau_in = refs[3:9]
    att_own, dq_own, sib_out, tau_out, kv_out = refs[9:14]
    k_s, v_s, kt_s, vt_s, dk_s, dv_s, s_s, e_s, dp_s, p_s, ds_s, tau_s = refs[14:]
    unit = pl.program_id(0)
    blocks = devices * local_blocks
    me = place[0]
    core = me % 2
    group = 2 * core + gi

    @pl.when(unit == 0)
    def _():
        def fill(b, carry):
            for half in range(local_blocks):
                rows = slice(half * BLOCK, (half + 1) * BLOCK)
                k_block = kv_in[b, 0, rows, :]
                v_block = kv_in[b, 1, rows, :]
                at = b * local_blocks + half
                k_s[at] = k_block
                v_s[at] = v_block
                kt_s[at] = k_block.T
                vt_s[at] = v_block.T
            return carry

        lax.fori_loop(0, devices, fill, 0, unroll=2)
        dk_s[...] = jnp.zeros_like(dk_s)
        dv_s[...] = jnp.zeros_like(dv_s)
        tau_s[...] = jnp.zeros_like(tau_s)

    own = unit < local_blocks
    q_here = jnp.where(own, q_own[...], q_sib[0])
    g_here = jnp.where(own, g_own[...], g_sib[0])

    def per_head(x):
        return [x[:, h * HD : (h + 1) * HD] for h in range(QPG)]

    q_rows = jnp.concatenate(per_head(q_here), axis=0)
    g_rows = jnp.concatenate(per_head(g_here), axis=0)
    q_t = jnp.concatenate([x.T for x in per_head(q_here)], axis=1)
    g_t = jnp.concatenate([x.T for x in per_head(g_here)], axis=1)
    scale = jnp.concatenate(
        [jnp.full((1, BLOCK), taus[group * QPG + h], jnp.float32) for h in range(QPG)], axis=1
    ) / math.sqrt(HD)
    factor = scale * LOG2E

    query_block = (me ^ (unit // local_blocks)) * local_blocks + unit % local_blocks
    wide = strides[group * blocks + query_block] == STRIDES[1]
    ids, bias = [], []
    for (narrow_off, narrow_times), (wide_off, wide_times) in zip(*offsets):
        ids.append((query_block + jnp.where(wide, wide_off, narrow_off)) % blocks)
        bias.append(
            times_bias(narrow_times)
            if narrow_times == wide_times
            else jnp.where(wide, times_bias(wide_times), times_bias(narrow_times))
        )
    chunks = [range(c, min(c + CHUNK, listed)) for c in range(0, listed, CHUNK)]

    def rows_of(c):
        return slice(c[0] * BLOCK, (c[-1] + 1) * BLOCK)

    most = None
    for c in chunks:
        raw = nt(jnp.concatenate([k_s[ids[j]] for j in c], axis=0), q_t)
        s_s[rows_of(c), :] = raw
        top = jnp.max(raw.reshape(-1, 8, ROWS), axis=0)
        most = top if most is None else jnp.maximum(most, top)
    top_row = jnp.max(most, axis=0, keepdims=True) * factor

    total = jnp.zeros((8, ROWS), jnp.float32)
    for c in chunks:
        dp_s[rows_of(c), :] = nt(jnp.concatenate([v_s[ids[j]] for j in c], axis=0), g_t)
        for j in c:
            rows = slice(j * BLOCK, (j + 1) * BLOCK)
            e = jnp.exp2(s_s[rows, :] * factor - (top_row - bias[j]))
            e_s[rows, :] = e
            total = total + jnp.sum(e.reshape(-1, 8, ROWS), axis=0)
    inverse = 1.0 / jnp.sum(total, axis=0, keepdims=True)

    for c in chunks:
        probs = (e_s[rows_of(c), :] * inverse).astype(jnp.bfloat16)
        p_s[rows_of(c), :] = probs
        part = nt(probs, g_rows)
        for n, j in enumerate(c):
            dv_s[ids[j]] += part[n * BLOCK : (n + 1) * BLOCK, :]
    o_t = nt(jnp.concatenate([vt_s[s] for s in ids], axis=1), p_s[...])
    row_dot = jnp.sum(g_t.astype(jnp.float32) * o_t, axis=0, keepdims=True)

    weight_scale = inverse * scale
    tau_rows = jnp.zeros((8, ROWS), jnp.float32)
    for c in chunks:
        scaled = e_s[rows_of(c), :] * weight_scale * (dp_s[rows_of(c), :] - row_dot)
        tau_rows = tau_rows + jnp.sum((scaled * s_s[rows_of(c), :]).reshape(-1, 8, ROWS), axis=0)
        low = scaled.astype(jnp.bfloat16)
        ds_s[rows_of(c), :] = low
        part = nt(low, q_rows)
        for n, j in enumerate(c):
            dk_s[ids[j]] += part[n * BLOCK : (n + 1) * BLOCK, :]
    dq_t = nt(jnp.concatenate([kt_s[s] for s in ids], axis=1), ds_s[...])
    tau_s[...] += tau_rows

    def back(x):
        low = x.astype(jnp.bfloat16)
        return jnp.concatenate([y.T for y in per_head(low)], axis=1)

    att = back(o_t)
    dq = back(dq_t)

    @pl.when(own)
    def _():
        att_own[...] = att
        dq_own[...] = dq

    @pl.when(jnp.logical_not(own))
    def _():
        sib_out[0] = att
        sib_out[1] = dq

    @pl.when(unit == 2 * local_blocks - 1)
    def _():
        def drain(b, carry):
            for half in range(local_blocks):
                rows = slice(half * BLOCK, (half + 1) * BLOCK)
                at = b * local_blocks + half
                kv_out[b, 0, rows, :] = dk_s[at].astype(jnp.bfloat16)
                kv_out[b, 1, rows, :] = dv_s[at].astype(jnp.bfloat16)
            return carry

        lax.fori_loop(0, devices, drain, 0, unroll=2)
        lane = lax.broadcasted_iota(jnp.int32, (8, HD), 1)
        sums = tau_in[...]
        for h in range(QPG):
            head = group * QPG + h
            share = jnp.sum(tau_s[:, h * BLOCK : (h + 1) * BLOCK]) / taus[head]
            sums = sums + jnp.where(lane == head, share, 0.0)
        tau_out[...] = sums


def times_bias(times):
    return math.log2(times) if times else NEVER


def run_group(gi, devices, place, strides, tau, queries, out_grad, qg_sib, kv_in, tau_in, offsets):
    listed = len(offsets[0])
    tokens = queries.shape[0]
    local_blocks = tokens // BLOCK
    units = 2 * local_blocks
    blocks = devices * local_blocks
    width = QPG * HD
    last = local_blocks - 1
    mine = lambda u, p, s, t: (jnp.minimum(u, last), 2 * (p[0] % 2) + gi)
    qs = pl.BlockSpec((1, BLOCK, width), lambda u, p, s, t: (0, jnp.maximum(u - local_blocks, 0), gi))
    gs = pl.BlockSpec((1, BLOCK, width), lambda u, p, s, t: (1, jnp.maximum(u - local_blocks, 0), gi))
    block_own = pl.BlockSpec((BLOCK, width), mine)
    out_own = pl.BlockSpec((BLOCK, width), lambda u, p, s, t: (jnp.minimum(u, last), 0))
    out_sib = pl.BlockSpec((2, BLOCK, width), lambda u, p, s, t: (0, jnp.maximum(u - local_blocks, 0), 0))
    kv_all = pl.BlockSpec((devices, 2, tokens, HD), lambda u, p, s, t: (0, 0, 0, 0))
    small = pl.BlockSpec((8, HD), lambda u, p, s, t: (0, 0))
    bf = lambda *shape: jax.ShapeDtypeStruct(shape, jnp.bfloat16)
    keys_wide = listed * BLOCK
    macs = units * ROWS * keys_wide * HD * 6
    return pl.pallas_call(
        functools.partial(group_kernel, gi, devices, local_blocks, listed, offsets),
        grid_spec=pltpu.PrefetchScalarGridSpec(
            num_scalar_prefetch=3,
            grid=(units,),
            in_specs=[block_own, qs, block_own, gs, kv_all, small],
            out_specs=[out_own, out_own, out_sib, small, kv_all],
            scratch_shapes=[pltpu.VMEM((blocks, BLOCK, HD), jnp.bfloat16)] * 4
            + [pltpu.VMEM((blocks, BLOCK, HD), jnp.float32)] * 2
            + [pltpu.VMEM((keys_wide, ROWS), jnp.float32)] * 3
            + [pltpu.VMEM((keys_wide, ROWS), jnp.bfloat16)] * 2
            + [pltpu.VMEM((8, ROWS), jnp.float32)],
        ),
        out_shape=[bf(tokens, width), bf(tokens, width), bf(2, tokens, width)]
        + [jax.ShapeDtypeStruct((8, HD), jnp.float32), bf(devices, 2, tokens, HD)],
        compiler_params=pltpu.CompilerParams(
            dimension_semantics=("arbitrary",), vmem_limit_bytes=60 * 2**20
        ),
        cost_estimate=pl.CostEstimate(
            flops=2 * macs, bytes_accessed=6 * 2**20, transcendentals=units * ROWS * keys_wide
        ),
        name="group_attention",
    )(place, strides, tau, queries, qg_sib, out_grad, qg_sib, kv_in, tau_in)


def total_over(x, axis):
    size = lax.axis_size(axis)
    if size & (size - 1):
        return lax.psum(x, axis)

    def partner(distance):
        return lax.ppermute(x, axis, [(i, i ^ distance) for i in range(size)])

    step = 1
    while step < size:
        if size // step % 4 == 0 and size // step != 8:
            x = (x + partner(step)) + (partner(2 * step) + partner(3 * step))
            step *= 4
        else:
            x = x + partner(step)
            step *= 2
    return x


def body(queries, keys, values, tau, out_grad, key_blocks):
    ctx = lax.axis_size("ctx")
    me = lax.axis_index("ctx").astype(jnp.int32)
    core = me % 2
    tokens = queries.shape[1]
    local_blocks = tokens // BLOCK
    block_count = ctx * local_blocks
    listed_count = key_blocks.shape[2]
    offsets = distinct_offsets(block_count, listed_count)
    swap = [(d, d ^ 1) for d in range(ctx)]
    wide = 2 * QPG * HD

    q0, k0, v0, g0 = queries[0], keys[0], values[0], out_grad[0]
    place = me[None]
    strides = ((key_blocks[:, :, 3] - jnp.arange(block_count, dtype=jnp.int32)) % block_count).reshape(-1)

    def kv_for(gi):
        halves = [
            jnp.stack([x[:, g * HD : (g + 1) * HD] for x in (k0, v0)]) for g in (gi, 2 + gi)
        ]
        return lax.all_to_all(jnp.stack(halves * (ctx // 2)), "ctx", 0, 0)

    def theirs(x):
        return lax.dynamic_slice_in_dim(x, (1 - core) * wide, wide, 1)

    kv_in = [kv_for(gi) for gi in range(2)]
    qg_sib = lax.ppermute(jnp.stack([theirs(q0), theirs(g0)]), "ctx", swap)

    att_parts, dq_parts, grads = [], [], []
    tau_rows = jnp.zeros((8, HD), jnp.float32)
    for gi in range(2):
        att_own, dq_own, sib, tau_rows, kv_grads = run_group(
            gi, ctx, place, strides, tau, q0, g0, qg_sib, kv_in[gi], tau_rows, offsets
        )
        sib = lax.ppermute(sib, "ctx", swap)
        att_parts.append((att_own, sib[0]))
        dq_parts.append((dq_own, sib[1]))
        grads.append(lax.all_to_all(kv_grads, "ctx", 0, 0))

    def by_group(parts):
        return jnp.concatenate(
            [jnp.where(core == c // 2, parts[c % 2][0], parts[c % 2][1]) for c in range(4)], axis=1
        )

    attended = by_group(att_parts)[None]
    query_grad = by_group(dq_parts)[None]

    def summed(which):
        cols = []
        for c in range(4):
            total = None
            for src in range(c // 2, ctx, 2):
                term = grads[c % 2][src, which].astype(jnp.float32)
                total = term if total is None else total + term
            cols.append(total.astype(jnp.bfloat16))
        return jnp.concatenate(cols, axis=1)[None]

    key_grad, value_grad = summed(0), summed(1)
    scale_total = total_over(total_over(tau_rows, "ctx"), "batch")[0, :HEADS]
    tau_grad = scale_total / math.sqrt(lax.axis_size("batch") * ctx * tokens)
    return (attended, query_grad, key_grad, value_grad, tau_grad)


def solution(mesh):
    rows = P("batch", "ctx", None)
    return jax.shard_map(
        body,
        mesh=mesh,
        in_specs=(rows, rows, rows, P(), rows, P()),
        out_specs=(rows, rows, rows, rows, P()),
        check_vma=False,
    )
```

```python
import functools
import math

import jax
import jax.numpy as jnp
from jax import lax
from jax.experimental import pallas as pl
from jax.experimental.pallas import tpu as pltpu
from jax.sharding import PartitionSpec as P

HEADS = 16
KV_HEADS = 4
HD = 128
BLOCK = 128
QPG = HEADS // KV_HEADS
SPLIT = 2
HEADS_EACH = QPG // SPLIT
ROWS = HEADS_EACH * BLOCK
TAIL = 16
STRIDES = (2, 3)
LOG2E = math.log2(math.e)
NEVER = -1e30


def distinct_offsets(block_count, listed_count):
    tables = []
    for stride in STRIDES:
        steps = range(1, (listed_count - 3) // 2 + 1)
        listed = [-1, 0, 1] + [stride * m for m in steps] + [-stride * m for m in steps]
        times = {}
        for o in listed:
            times[o % block_count] = times.get(o % block_count, 0) + 1
        tables.append(sorted(times.items()))
    most = max(len(t) for t in tables)
    return [t + [(0, 0)] * (most - len(t)) for t in tables]


def nt(a, b):
    return jnp.dot(a, b, preferred_element_type=jnp.float32)


def group_kernel(gi, devices, local_blocks, listed, offsets, *refs):
    place, strides, taus = refs[:3]
    q_own, q_sib, g_own, g_sib, kv_in, tau_in = refs[3:9]
    att_own, dq_own, sib_out, tau_out, kv_out = refs[9:14]
    k_s, v_s, kt_s, vt_s, dk_s, dv_s, s_s, e_s, dp_s, p_s, ds_s, tau_s = refs[14:]
    unit = pl.program_id(0)
    blocks = devices * local_blocks
    tokens = local_blocks * BLOCK
    me = place[0]
    core = me % 2
    group = 2 * core + gi

    @pl.when(unit == 0)
    def _():
        def fill(b, carry):
            for half in range(local_blocks):
                rows = slice(half * BLOCK, (half + 1) * BLOCK)
                k_block = kv_in[b, 0, rows, :]
                v_block = kv_in[b, 1, rows, :]
                at = b * local_blocks + half
                k_s[at] = k_block
                v_s[at] = v_block
                kt_s[at] = k_block.T
                vt_s[at] = v_block.T
            return carry

        lax.fori_loop(0, devices, fill, 0, unroll=2)
        dk_s[...] = jnp.zeros_like(dk_s)
        dv_s[...] = jnp.zeros_like(dv_s)
        tau_s[...] = jnp.zeros_like(tau_s)

    own = unit < local_blocks
    query_block = (me ^ (unit // local_blocks)) * local_blocks + unit % local_blocks
    wide = strides[group * blocks + query_block] == STRIDES[1]
    ids, bias = [], []
    for (narrow_off, narrow_times), (wide_off, wide_times) in zip(*offsets):
        ids.append((query_block + jnp.where(wide, wide_off, narrow_off)) % blocks)
        bias.append(
            times_bias(narrow_times)
            if narrow_times == wide_times
            else jnp.where(wide, times_bias(wide_times), times_bias(narrow_times))
        )
    keys_all = jnp.concatenate([k_s[i] for i in ids], axis=0)
    values_all = jnp.concatenate([v_s[i] for i in ids], axis=0)
    keys_t = jnp.concatenate([kt_s[i] for i in ids], axis=1)
    values_t = jnp.concatenate([vt_s[i] for i in ids], axis=1)
    span = [slice(j * BLOCK, (j + 1) * BLOCK) for j in range(listed)]

    def in_rows(x):
        return x.reshape(-1, 8, ROWS)

    def part(n):
        cols = slice(n * HEADS_EACH * HD, (n + 1) * HEADS_EACH * HD)
        s_n, e_n, dp_n, p_n, ds_n = (x.at[n] for x in (s_s, e_s, dp_s, p_s, ds_s))
        q_here = jnp.where(own, q_own[:, cols], q_sib[0, :, cols])
        g_here = jnp.where(own, g_own[:, cols], g_sib[0, :, cols])

        def per_head(x):
            return [x[:, h * HD : (h + 1) * HD] for h in range(HEADS_EACH)]

        q_rows = jnp.concatenate(per_head(q_here), axis=0)
        g_rows = jnp.concatenate(per_head(g_here), axis=0)
        q_t = jnp.concatenate([x.T for x in per_head(q_here)], axis=1)
        g_t = jnp.concatenate([x.T for x in per_head(g_here)], axis=1)
        first = group * QPG + n * HEADS_EACH
        scale = jnp.concatenate(
            [jnp.full((1, BLOCK), taus[first + h], jnp.float32) for h in range(HEADS_EACH)], axis=1
        ) / math.sqrt(HD)
        factor = scale * LOG2E

        s_n[...] = nt(keys_all, q_t)
        yield
        dp_n[...] = nt(values_all, g_t)
        most = jnp.max(in_rows(s_n[span[0], :]), axis=0)
        for j in range(1, listed):
            most = jnp.maximum(most, jnp.max(in_rows(s_n[span[j], :]), axis=0))
        top_row = jnp.max(most, axis=0, keepdims=True) * factor
        total = jnp.zeros((8, ROWS), jnp.float32)
        for j in range(listed):
            e = jnp.exp2(s_n[span[j], :] * factor - (top_row - bias[j]))
            e_n[span[j], :] = e
            total = total + jnp.sum(in_rows(e), axis=0)
        inverse = 1.0 / jnp.sum(total, axis=0, keepdims=True)
        yield
        for j in range(listed):
            p_n[span[j], :] = (e_n[span[j], :] * inverse).astype(jnp.bfloat16)
        o_t = nt(values_t, p_n[...])
        dv = nt(p_n[...], g_rows)
        for j in range(listed):
            dv_s[ids[j]] += dv[span[j], :]
        row_dot = jnp.sum(g_t.astype(jnp.float32) * o_t, axis=0, keepdims=True)
        write(n, 0, o_t)
        yield
        weight_scale = inverse * scale
        tau_rows = jnp.zeros((8, ROWS), jnp.float32)
        for j in range(listed):
            scaled = e_n[span[j], :] * weight_scale * (dp_n[span[j], :] - row_dot)
            tau_rows = tau_rows + jnp.sum(in_rows(scaled * s_n[span[j], :]), axis=0)
            ds_n[span[j], :] = scaled.astype(jnp.bfloat16)
        tau_s[n] += tau_rows
        yield
        dq_t = nt(keys_t, ds_n[...])
        dk = nt(ds_n[...], q_rows)
        for j in range(listed):
            dk_s[ids[j]] += dk[span[j], :]
        write(n, 1, dq_t)

    def write(n, which, x_t):
        low = x_t.astype(jnp.bfloat16)
        out = jnp.concatenate([low[:, h * HD : (h + 1) * HD].T for h in range(HEADS_EACH)], axis=1)
        cols = slice(n * HEADS_EACH * HD, (n + 1) * HEADS_EACH * HD)
        (att_own, dq_own)[which][:, cols] = out
        sib_out[which, :, cols] = out

    shares = [part(n) for n in range(SPLIT)]
    live = []
    while shares or live:
        if shares:
            live.append(shares.pop(0))
        for share in list(live):
            if next(share, 1) == 1:
                live.remove(share)

    @pl.when(unit == 2 * local_blocks - 1)
    def _():
        lane = lax.broadcasted_iota(jnp.int32, (TAIL, HD), 1)
        row = lax.broadcasted_iota(jnp.int32, (TAIL, HD), 0)
        sums = tau_in[...]
        for h in range(QPG):
            head = group * QPG + h
            rows = tau_s[h // HEADS_EACH, :, (h % HEADS_EACH) * BLOCK : (h % HEADS_EACH + 1) * BLOCK]
            sums = sums + jnp.where(lane == head, jnp.sum(rows) / taus[head], 0.0)
        tau_out[...] = sums
        high = sums.astype(jnp.bfloat16).astype(jnp.float32)
        mid = (sums - high).astype(jnp.bfloat16).astype(jnp.float32)
        low = sums - high - mid
        tail = jnp.where(
            row == 0, high, jnp.where(row == 1, mid, jnp.where(row == 2, low, 0.0))
        ).astype(jnp.bfloat16)

        def drain(b, carry):
            for half in range(local_blocks):
                at = b * local_blocks + half
                low, high = half * BLOCK, (half + 1) * BLOCK
                kv_out[b, low:high, :] = dk_s[at].astype(jnp.bfloat16)
                kv_out[b, tokens + low : tokens + high, :] = dv_s[at].astype(jnp.bfloat16)
            kv_out[b, 2 * tokens :, :] = tail
            return carry

        lax.fori_loop(0, devices, drain, 0, unroll=2)


def times_bias(times):
    return math.log2(times) if times else NEVER


def run_group(gi, devices, place, strides, tau, queries, out_grad, qg_sib, kv_in, tau_in, offsets):
    listed = len(offsets[0])
    tokens = queries.shape[0]
    local_blocks = tokens // BLOCK
    units = 2 * local_blocks
    blocks = devices * local_blocks
    width = QPG * HD
    last = local_blocks - 1
    mine = lambda u, p, s, t: (jnp.minimum(u, last), 2 * (p[0] % 2) + gi)
    qs = pl.BlockSpec((1, BLOCK, width), lambda u, p, s, t: (0, jnp.maximum(u - local_blocks, 0), gi))
    gs = pl.BlockSpec((1, BLOCK, width), lambda u, p, s, t: (1, jnp.maximum(u - local_blocks, 0), gi))
    block_own = pl.BlockSpec((BLOCK, width), mine)
    out_own = pl.BlockSpec((BLOCK, width), lambda u, p, s, t: (jnp.minimum(u, local_blocks), 0))
    out_sib = pl.BlockSpec((2, BLOCK, width), lambda u, p, s, t: (0, jnp.maximum(u - local_blocks, 0), 0))
    kv_back = pl.BlockSpec((devices, 2 * tokens + TAIL, HD), lambda u, p, s, t: (0, 0, 0))
    kv_all = pl.BlockSpec((devices, 2, tokens, HD), lambda u, p, s, t: (0, 0, 0, 0))
    small = pl.BlockSpec((TAIL, HD), lambda u, p, s, t: (0, 0))
    bf = lambda *shape: jax.ShapeDtypeStruct(shape, jnp.bfloat16)
    keys_wide = listed * BLOCK
    macs = units * QPG * BLOCK * keys_wide * HD * 6
    return pl.pallas_call(
        functools.partial(group_kernel, gi, devices, local_blocks, listed, offsets),
        grid_spec=pltpu.PrefetchScalarGridSpec(
            num_scalar_prefetch=3,
            grid=(units,),
            in_specs=[block_own, qs, block_own, gs, kv_all, small],
            out_specs=[out_own, out_own, out_sib, small, kv_back],
            scratch_shapes=[pltpu.VMEM((blocks, BLOCK, HD), jnp.bfloat16)] * 4
            + [pltpu.VMEM((blocks, BLOCK, HD), jnp.float32)] * 2
            + [pltpu.VMEM((SPLIT, keys_wide, ROWS), jnp.float32)] * 3
            + [pltpu.VMEM((SPLIT, keys_wide, ROWS), jnp.bfloat16)] * 2
            + [pltpu.VMEM((SPLIT, 8, ROWS), jnp.float32)],
        ),
        out_shape=[bf(tokens + BLOCK, width), bf(tokens + BLOCK, width), bf(2, tokens, width)]
        + [jax.ShapeDtypeStruct((TAIL, HD), jnp.float32), bf(devices, 2 * tokens + TAIL, HD)],
        compiler_params=pltpu.CompilerParams(
            dimension_semantics=("arbitrary",), vmem_limit_bytes=60 * 2**20
        ),
        cost_estimate=pl.CostEstimate(
            flops=2 * macs, bytes_accessed=6 * 2**20, transcendentals=units * QPG * BLOCK * keys_wide
        ),
        name="group_attention",
    )(place, strides, tau, queries, qg_sib, out_grad, qg_sib, kv_in, tau_in)


def spread_kernel(k_ref, v_ref, out):
    for parity in range(2):
        cols = slice(parity * 2 * HD, parity * 2 * HD + HD)
        out[parity, 0] = k_ref[:, cols]
        out[parity, 1] = v_ref[:, cols]


def spread(gi, devices, keys, values):
    tokens, width = keys.shape
    cols = width - HD
    taken = pl.BlockSpec((tokens, width), lambda d: (0, 0))

    def kernel(k_ref, v_ref, out):
        at = gi * HD
        spread_kernel(k_ref.at[:, at : at + cols], v_ref.at[:, at : at + cols], out)

    return pl.pallas_call(
        kernel,
        grid=(devices // 2,),
        in_specs=[taken, taken],
        out_specs=pl.BlockSpec((2, 2, tokens, HD), lambda d: (d, 0, 0, 0)),
        out_shape=jax.ShapeDtypeStruct((devices, 2, tokens, HD), jnp.bfloat16),
        compiler_params=pltpu.CompilerParams(vmem_limit_bytes=60 * 2**20),
        name="spread_keys_values",
    )(keys, values)


def total_over(x, axis):
    size = lax.axis_size(axis)
    if size & (size - 1):
        return lax.psum(x, axis)

    def partner(distance):
        return lax.ppermute(x, axis, [(i, i ^ distance) for i in range(size)])

    step = 1
    while step < size:
        if size // step % 4 == 0 and size // step != 8:
            x = (x + partner(step)) + (partner(2 * step) + partner(3 * step))
            step *= 4
        else:
            x = x + partner(step)
            step *= 2
    return x


def body(queries, keys, values, tau, out_grad, key_blocks):
    ctx = lax.axis_size("ctx")
    me = lax.axis_index("ctx").astype(jnp.int32)
    core = me % 2
    tokens = queries.shape[1]
    local_blocks = tokens // BLOCK
    block_count = ctx * local_blocks
    listed_count = key_blocks.shape[2]
    offsets = distinct_offsets(block_count, listed_count)
    swap = [(d, d ^ 1) for d in range(ctx)]
    wide = 2 * QPG * HD

    q0, k0, v0, g0 = queries[0], keys[0], values[0], out_grad[0]
    place = me[None]
    strides = ((key_blocks[:, :, 3] - jnp.arange(block_count, dtype=jnp.int32)) % block_count).reshape(-1)

    def kv_for(gi):
        return lax.all_to_all(spread(gi, ctx, k0, v0), "ctx", 0, 0)

    def theirs(x):
        return lax.dynamic_slice_in_dim(x, (1 - core) * wide, wide, 1)

    kv_in = [kv_for(gi) for gi in range(2)]
    qg_sib = lax.ppermute(jnp.stack([theirs(q0), theirs(g0)]), "ctx", swap)

    att_parts, dq_parts, grads = [], [], []
    tau_rows = jnp.zeros((TAIL, HD), jnp.float32)
    for gi in range(2):
        att_own, dq_own, sib, tau_rows, kv_grads = run_group(
            gi, ctx, place, strides, tau, q0, g0, qg_sib, kv_in[gi], tau_rows, offsets
        )
        sib = lax.ppermute(sib, "ctx", swap)
        att_parts.append((att_own[:tokens], sib[0]))
        dq_parts.append((dq_own[:tokens], sib[1]))
        grads.append(lax.all_to_all(kv_grads, "ctx", 0, 0))

    def by_group(parts):
        return jnp.concatenate(
            [jnp.where(core == c // 2, parts[c % 2][0], parts[c % 2][1]) for c in range(4)], axis=1
        )

    attended = by_group(att_parts)[None]
    query_grad = by_group(dq_parts)[None]

    def summed(which):
        cols = []
        for c in range(4):
            total = None
            for src in range(c // 2, ctx, 2):
                term = grads[c % 2][src, which * tokens : (which + 1) * tokens].astype(jnp.float32)
                total = term if total is None else total + term
            cols.append(total.astype(jnp.bfloat16))
        return jnp.concatenate(cols, axis=1)[None]

    key_grad, value_grad = summed(0), summed(1)
    tails = grads[1][:, 2 * tokens : 2 * tokens + 3, :HEADS].astype(jnp.float32)
    scale_total = total_over(jnp.sum(tails, axis=(0, 1))[None], "batch")[0]
    tau_grad = scale_total / math.sqrt(lax.axis_size("batch") * ctx * tokens)
    return (attended, query_grad, key_grad, value_grad, tau_grad)


def solution(mesh):
    rows = P("batch", "ctx", None)
    return jax.shard_map(
        body,
        mesh=mesh,
        in_specs=(rows, rows, rows, P(), rows, P()),
        out_specs=(rows, rows, rows, rows, P()),
        check_vma=False,
    )
```

```python
import functools
import math

import jax
import jax.numpy as jnp
from jax import lax
from jax.experimental import pallas as pl
from jax.experimental.pallas import tpu as pltpu
from jax.sharding import PartitionSpec as P

HEADS = 16
KV_HEADS = 4
HD = 128
BLOCK = 128
QPG = HEADS // KV_HEADS
SPLIT = 2
CHUNK = 4
HEADS_EACH = QPG // SPLIT
ROWS = HEADS_EACH * BLOCK
TAIL = 16
STRIDES = (2, 3)
LOG2E = math.log2(math.e)
NEVER = -1e30


def distinct_offsets(block_count, listed_count):
    tables = []
    for stride in STRIDES:
        steps = range(1, (listed_count - 3) // 2 + 1)
        listed = [-1, 0, 1] + [stride * m for m in steps] + [-stride * m for m in steps]
        times = {}
        for o in listed:
            times[o % block_count] = times.get(o % block_count, 0) + 1
        tables.append(sorted(times.items()))
    most = max(len(t) for t in tables)
    return [t + [(0, 0)] * (most - len(t)) for t in tables]


def nt(a, b):
    return jnp.dot(a, b, preferred_element_type=jnp.float32)


def group_kernel(gi, devices, local_blocks, listed, offsets, *refs):
    place, strides, taus = refs[:3]
    q_own, q_sib, g_own, g_sib, kv_in, tau_in = refs[3:9]
    att_own, dq_own, sib_out, tau_out, kv_out = refs[9:14]
    k_s, v_s, kt_s, vt_s, dk_s, dv_s, s_s, e_s, tau_s = refs[14:]
    unit = pl.program_id(0)
    blocks = devices * local_blocks
    tokens = local_blocks * BLOCK
    me = place[0]
    core = me % 2
    group = 2 * core + gi

    @pl.when(unit == 0)
    def _():
        def fill(b, carry):
            for half in range(local_blocks):
                rows = slice(half * BLOCK, (half + 1) * BLOCK)
                k_block = kv_in[b, 0, rows, :]
                v_block = kv_in[b, 1, rows, :]
                at = b * local_blocks + half
                k_s[at] = k_block
                v_s[at] = v_block
                kt_s[at] = k_block.T
                vt_s[at] = v_block.T
            return carry

        lax.fori_loop(0, devices, fill, 0, unroll=2)
        dk_s[...] = jnp.zeros_like(dk_s)
        dv_s[...] = jnp.zeros_like(dv_s)
        tau_s[...] = jnp.zeros_like(tau_s)

    own = unit < local_blocks
    query_block = (me ^ (unit // local_blocks)) * local_blocks + unit % local_blocks
    wide = strides[group * blocks + query_block] == STRIDES[1]
    ids, bias = [], []
    for (narrow_off, narrow_times), (wide_off, wide_times) in zip(*offsets):
        ids.append((query_block + jnp.where(wide, wide_off, narrow_off)) % blocks)
        bias.append(
            times_bias(narrow_times)
            if narrow_times == wide_times
            else jnp.where(wide, times_bias(wide_times), times_bias(narrow_times))
        )
    chunks = [range(c, min(c + CHUNK, listed)) for c in range(0, listed, CHUNK)]

    def rows_of(c):
        return slice(c[0] * BLOCK, (c[-1] + 1) * BLOCK)

    def picked(ref, c, axis):
        return jnp.concatenate([ref[ids[j]] for j in c], axis=axis)

    def in_rows(x):
        return x.reshape(-1, 8, ROWS)

    def part(n):
        cols = slice(n * HEADS_EACH * HD, (n + 1) * HEADS_EACH * HD)
        s_n, e_n = s_s.at[n], e_s.at[n]
        q_here = jnp.where(own, q_own[:, cols], q_sib[0, :, cols])
        g_here = jnp.where(own, g_own[:, cols], g_sib[0, :, cols])

        def per_head(x):
            return [x[:, h * HD : (h + 1) * HD] for h in range(HEADS_EACH)]

        q_rows = jnp.concatenate(per_head(q_here), axis=0)
        g_rows = jnp.concatenate(per_head(g_here), axis=0)
        q_t = jnp.concatenate([x.T for x in per_head(q_here)], axis=1)
        g_t = jnp.concatenate([x.T for x in per_head(g_here)], axis=1)
        first = group * QPG + n * HEADS_EACH
        scale = jnp.concatenate(
            [jnp.full((1, BLOCK), taus[first + h], jnp.float32) for h in range(HEADS_EACH)], axis=1
        ) / math.sqrt(HD)
        factor = scale * LOG2E

        most = None
        for c in chunks:
            raw = nt(picked(k_s, c, 0), q_t)
            s_n[rows_of(c), :] = raw
            top = jnp.max(in_rows(raw), axis=0)
            most = top if most is None else jnp.maximum(most, top)
            yield
        top_row = jnp.max(most, axis=0, keepdims=True) * factor
        total = jnp.zeros((8, ROWS), jnp.float32)
        for c in chunks:
            for j in c:
                rows = slice(j * BLOCK, (j + 1) * BLOCK)
                e = jnp.exp2(s_n[rows, :] * factor - (top_row - bias[j]))
                e_n[rows, :] = e
                total = total + jnp.sum(in_rows(e), axis=0)
            yield
        inverse = 1.0 / jnp.sum(total, axis=0, keepdims=True)
        o_t = jnp.zeros((HD, ROWS), jnp.float32)
        for c in chunks:
            probs = (e_n[rows_of(c), :] * inverse).astype(jnp.bfloat16)
            o_t = o_t + nt(picked(vt_s, c, 1), probs)
            add_blocks(dv_s, c, nt(probs, g_rows))
            yield
        row_dot = jnp.sum(g_t.astype(jnp.float32) * o_t, axis=0, keepdims=True)
        write(n, 0, o_t)
        weight_scale = inverse * scale
        tau_rows = jnp.zeros((8, ROWS), jnp.float32)
        dq_t = jnp.zeros((HD, ROWS), jnp.float32)
        for c in chunks:
            dweights = nt(picked(v_s, c, 0), g_t)
            scaled = e_n[rows_of(c), :] * weight_scale * (dweights - row_dot)
            tau_rows = tau_rows + jnp.sum(in_rows(scaled * s_n[rows_of(c), :]), axis=0)
            low = scaled.astype(jnp.bfloat16)
            dq_t = dq_t + nt(picked(kt_s, c, 1), low)
            add_blocks(dk_s, c, nt(low, q_rows))
            yield
        tau_s[n] += tau_rows
        write(n, 1, dq_t)

    def add_blocks(ref, c, x):
        for n, j in enumerate(c):
            ref[ids[j]] += x[n * BLOCK : (n + 1) * BLOCK, :]

    def write(n, which, x_t):
        low = x_t.astype(jnp.bfloat16)
        out = jnp.concatenate([low[:, h * HD : (h + 1) * HD].T for h in range(HEADS_EACH)], axis=1)
        cols = slice(n * HEADS_EACH * HD, (n + 1) * HEADS_EACH * HD)
        (att_own, dq_own)[which][:, cols] = out
        sib_out[which, :, cols] = out

    shares = [part(n) for n in range(SPLIT)]
    for turn in range((4 + SPLIT) * len(chunks)):
        for n, share in enumerate(shares):
            if turn >= n * len(chunks):
                next(share, None)

    @pl.when(unit == 2 * local_blocks - 1)
    def _():
        lane = lax.broadcasted_iota(jnp.int32, (TAIL, HD), 1)
        row = lax.broadcasted_iota(jnp.int32, (TAIL, HD), 0)
        sums = tau_in[...]
        for h in range(QPG):
            head = group * QPG + h
            rows = tau_s[h // HEADS_EACH, :, (h % HEADS_EACH) * BLOCK : (h % HEADS_EACH + 1) * BLOCK]
            sums = sums + jnp.where(lane == head, jnp.sum(rows) / taus[head], 0.0)
        tau_out[...] = sums
        high = sums.astype(jnp.bfloat16).astype(jnp.float32)
        mid = (sums - high).astype(jnp.bfloat16).astype(jnp.float32)
        low = sums - high - mid
        tail = jnp.where(
            row == 0, high, jnp.where(row == 1, mid, jnp.where(row == 2, low, 0.0))
        ).astype(jnp.bfloat16)

        def drain(b, carry):
            for half in range(local_blocks):
                at = b * local_blocks + half
                low, high = half * BLOCK, (half + 1) * BLOCK
                kv_out[b, low:high, :] = dk_s[at].astype(jnp.bfloat16)
                kv_out[b, tokens + low : tokens + high, :] = dv_s[at].astype(jnp.bfloat16)
            kv_out[b, 2 * tokens :, :] = tail
            return carry

        lax.fori_loop(0, devices, drain, 0, unroll=2)


def times_bias(times):
    return math.log2(times) if times else NEVER


def run_group(gi, devices, place, strides, tau, queries, out_grad, qg_sib, kv_in, tau_in, offsets):
    listed = len(offsets[0])
    tokens = queries.shape[0]
    local_blocks = tokens // BLOCK
    units = 2 * local_blocks
    blocks = devices * local_blocks
    width = QPG * HD
    last = local_blocks - 1
    mine = lambda u, p, s, t: (jnp.minimum(u, last), 2 * (p[0] % 2) + gi)
    qs = pl.BlockSpec((1, BLOCK, width), lambda u, p, s, t: (0, jnp.maximum(u - local_blocks, 0), gi))
    gs = pl.BlockSpec((1, BLOCK, width), lambda u, p, s, t: (1, jnp.maximum(u - local_blocks, 0), gi))
    block_own = pl.BlockSpec((BLOCK, width), mine)
    out_own = pl.BlockSpec((BLOCK, width), lambda u, p, s, t: (jnp.minimum(u, local_blocks), 0))
    out_sib = pl.BlockSpec((2, BLOCK, width), lambda u, p, s, t: (0, jnp.maximum(u - local_blocks, 0), 0))
    kv_back = pl.BlockSpec((devices, 2 * tokens + TAIL, HD), lambda u, p, s, t: (0, 0, 0))
    kv_all = pl.BlockSpec((devices, 2, tokens, HD), lambda u, p, s, t: (0, 0, 0, 0))
    small = pl.BlockSpec((TAIL, HD), lambda u, p, s, t: (0, 0))
    bf = lambda *shape: jax.ShapeDtypeStruct(shape, jnp.bfloat16)
    keys_wide = listed * BLOCK
    macs = units * QPG * BLOCK * keys_wide * HD * 6
    return pl.pallas_call(
        functools.partial(group_kernel, gi, devices, local_blocks, listed, offsets),
        grid_spec=pltpu.PrefetchScalarGridSpec(
            num_scalar_prefetch=3,
            grid=(units,),
            in_specs=[block_own, qs, block_own, gs, kv_all, small],
            out_specs=[out_own, out_own, out_sib, small, kv_back],
            scratch_shapes=[pltpu.VMEM((blocks, BLOCK, HD), jnp.bfloat16)] * 4
            + [pltpu.VMEM((blocks, BLOCK, HD), jnp.float32)] * 2
            + [pltpu.VMEM((SPLIT, keys_wide, ROWS), jnp.float32)] * 2
            + [pltpu.VMEM((SPLIT, 8, ROWS), jnp.float32)],
        ),
        out_shape=[bf(tokens + BLOCK, width), bf(tokens + BLOCK, width), bf(2, tokens, width)]
        + [jax.ShapeDtypeStruct((TAIL, HD), jnp.float32), bf(devices, 2 * tokens + TAIL, HD)],
        compiler_params=pltpu.CompilerParams(
            dimension_semantics=("arbitrary",), vmem_limit_bytes=60 * 2**20
        ),
        cost_estimate=pl.CostEstimate(
            flops=2 * macs, bytes_accessed=6 * 2**20, transcendentals=units * QPG * BLOCK * keys_wide
        ),
        name="group_attention",
    )(place, strides, tau, queries, qg_sib, out_grad, qg_sib, kv_in, tau_in)


def spread_kernel(k_ref, v_ref, out):
    for parity in range(2):
        cols = slice(parity * 2 * HD, parity * 2 * HD + HD)
        out[parity, 0] = k_ref[:, cols]
        out[parity, 1] = v_ref[:, cols]


def spread(gi, devices, keys, values):
    tokens, width = keys.shape
    cols = width - HD
    taken = pl.BlockSpec((tokens, width), lambda d: (0, 0))

    def kernel(k_ref, v_ref, out):
        at = gi * HD
        spread_kernel(k_ref.at[:, at : at + cols], v_ref.at[:, at : at + cols], out)

    return pl.pallas_call(
        kernel,
        grid=(devices // 2,),
        in_specs=[taken, taken],
        out_specs=pl.BlockSpec((2, 2, tokens, HD), lambda d: (d, 0, 0, 0)),
        out_shape=jax.ShapeDtypeStruct((devices, 2, tokens, HD), jnp.bfloat16),
        compiler_params=pltpu.CompilerParams(vmem_limit_bytes=60 * 2**20),
        name="spread_keys_values",
    )(keys, values)


def total_over(x, axis):
    size = lax.axis_size(axis)
    if size & (size - 1):
        return lax.psum(x, axis)

    def partner(distance):
        return lax.ppermute(x, axis, [(i, i ^ distance) for i in range(size)])

    step = 1
    while step < size:
        if size // step % 4 == 0 and size // step != 8:
            x = (x + partner(step)) + (partner(2 * step) + partner(3 * step))
            step *= 4
        else:
            x = x + partner(step)
            step *= 2
    return x


def body(queries, keys, values, tau, out_grad, key_blocks):
    ctx = lax.axis_size("ctx")
    me = lax.axis_index("ctx").astype(jnp.int32)
    core = me % 2
    tokens = queries.shape[1]
    local_blocks = tokens // BLOCK
    block_count = ctx * local_blocks
    listed_count = key_blocks.shape[2]
    offsets = distinct_offsets(block_count, listed_count)
    swap = [(d, d ^ 1) for d in range(ctx)]
    wide = 2 * QPG * HD

    q0, k0, v0, g0 = queries[0], keys[0], values[0], out_grad[0]
    place = me[None]
    strides = ((key_blocks[:, :, 3] - jnp.arange(block_count, dtype=jnp.int32)) % block_count).reshape(-1)

    def kv_for(gi):
        return lax.all_to_all(spread(gi, ctx, k0, v0), "ctx", 0, 0)

    def theirs(x):
        return lax.dynamic_slice_in_dim(x, (1 - core) * wide, wide, 1)

    kv_in = [kv_for(gi) for gi in range(2)]
    qg_sib = lax.ppermute(jnp.stack([theirs(q0), theirs(g0)]), "ctx", swap)

    att_parts, dq_parts, grads = [], [], []
    tau_rows = jnp.zeros((TAIL, HD), jnp.float32)
    for gi in range(2):
        att_own, dq_own, sib, tau_rows, kv_grads = run_group(
            gi, ctx, place, strides, tau, q0, g0, qg_sib, kv_in[gi], tau_rows, offsets
        )
        if grads:
            kv_grads, grads[0] = lax.optimization_barrier((kv_grads, grads[0]))
        sib = lax.ppermute(sib, "ctx", swap)
        att_parts.append((att_own[:tokens], sib[0]))
        dq_parts.append((dq_own[:tokens], sib[1]))
        grads.append(lax.all_to_all(kv_grads, "ctx", 0, 0))

    def by_group(parts):
        return jnp.concatenate(
            [jnp.where(core == c // 2, parts[c % 2][0], parts[c % 2][1]) for c in range(4)], axis=1
        )

    attended = by_group(att_parts)[None]
    query_grad = by_group(dq_parts)[None]

    def summed(which):
        cols = []
        for c in range(4):
            total = None
            for src in range(c // 2, ctx, 2):
                term = grads[c % 2][src, which * tokens : (which + 1) * tokens].astype(jnp.float32)
                total = term if total is None else total + term
            cols.append(total.astype(jnp.bfloat16))
        return jnp.concatenate(cols, axis=1)[None]

    key_grad, value_grad = summed(0), summed(1)
    tails = grads[1][:, 2 * tokens : 2 * tokens + 3, :HEADS].astype(jnp.float32)
    scale_total = total_over(jnp.sum(tails, axis=(0, 1))[None], "batch")[0]
    tau_grad = scale_total / math.sqrt(lax.axis_size("batch") * ctx * tokens)
    return (attended, query_grad, key_grad, value_grad, tau_grad)


def solution(mesh):
    rows = P("batch", "ctx", None)
    return jax.shard_map(
        body,
        mesh=mesh,
        in_specs=(rows, rows, rows, P(), rows, P()),
        out_specs=(rows, rows, rows, rows, P()),
        check_vma=False,
    )
```

```python
import functools
import math

import jax
import jax.numpy as jnp
from jax import lax
from jax.experimental import pallas as pl
from jax.experimental.pallas import tpu as pltpu
from jax.sharding import PartitionSpec as P

HEADS = 16
KV_HEADS = 4
HD = 128
BLOCK = 128
QPG = HEADS // KV_HEADS
CHUNK = 4
ROWS = QPG * BLOCK
TAIL = 8
STRIDES = (2, 3)
LOG2E = math.log2(math.e)
NEVER = -1e30


def distinct_offsets(block_count, listed_count):
    tables = []
    for stride in STRIDES:
        steps = range(1, (listed_count - 3) // 2 + 1)
        listed = [-1, 0, 1] + [stride * m for m in steps] + [-stride * m for m in steps]
        times = {}
        for o in listed:
            times[o % block_count] = times.get(o % block_count, 0) + 1
        tables.append(sorted(times.items()))
    most = max(len(t) for t in tables)
    return [t + [(0, 0)] * (most - len(t)) for t in tables]


def nt(a, b):
    return jnp.dot(a, b, preferred_element_type=jnp.float32)


def group_kernel(gi, devices, local_blocks, listed, offsets, *refs):
    place, key_blocks, taus = refs[:3]
    inputs, rest = refs[3 : 8 + gi], refs[8 + gi :]
    q_own, q_sib, g_own, g_sib, kv_in = inputs[:5]
    att_own, dq_own, sib_out, tau_out, kv_out = rest[:5]
    k_s, v_s, kt_s, vt_s, dk_s, dv_s, s_s, e_s, tau_s = rest[5:]
    step = pl.program_id(0)
    blocks = devices * local_blocks
    me = place[0]
    group = 2 * (me % 2) + gi

    @pl.when(step == 0)
    def _():
        def fill(b, carry):
            for half in range(local_blocks):
                rows = slice(half * BLOCK, (half + 1) * BLOCK)
                k_block = kv_in[b, 0, rows, :]
                v_block = kv_in[b, 1, rows, :]
                at = b * local_blocks + half
                k_s[at] = k_block
                v_s[at] = v_block
                kt_s[at] = k_block.T
                vt_s[at] = v_block.T
            return carry

        lax.fori_loop(0, devices, fill, 0, unroll=2)
        dk_s[...] = jnp.zeros_like(dk_s)
        dv_s[...] = jnp.zeros_like(dv_s)
        tau_s[...] = jnp.zeros_like(tau_s)

    chunks = [range(c, min(c + CHUNK, listed)) for c in range(0, listed, CHUNK)]
    scale = jnp.concatenate(
        [jnp.full((1, BLOCK), taus[group * QPG + h], jnp.float32) for h in range(QPG)], axis=1
    ) / math.sqrt(HD)
    factor = scale * LOG2E

    def rows_of(c):
        return slice(c[0] * BLOCK, (c[-1] + 1) * BLOCK)

    def per_head(x):
        return [x[:, h * HD : (h + 1) * HD] for h in range(QPG)]

    def in_rows(x):
        return x.reshape(-1, 8, ROWS)

    def part(n):
        s_n, e_n = s_s.at[n], e_s.at[n]
        query_block = (me ^ n) * local_blocks + step
        wide = (key_blocks[group, query_block, 3] - query_block) % blocks == STRIDES[1]
        ids, bias = [], []
        for (narrow_off, narrow_times), (wide_off, wide_times) in zip(*offsets):
            ids.append((query_block + jnp.where(wide, wide_off, narrow_off)) % blocks)
            bias.append(
                times_bias(narrow_times)
                if narrow_times == wide_times
                else jnp.where(wide, times_bias(wide_times), times_bias(narrow_times))
            )

        def picked(ref, c, axis):
            return jnp.concatenate([ref[ids[j]] for j in c], axis=axis)

        def add_blocks(ref, c, x):
            for n, j in enumerate(c):
                ref[ids[j]] += x[n * BLOCK : (n + 1) * BLOCK, :]

        q_here = q_sib[0] if n else q_own[...]
        g_here = g_sib[0] if n else g_own[...]
        q_rows = jnp.concatenate(per_head(q_here), axis=0)
        g_rows = jnp.concatenate(per_head(g_here), axis=0)
        q_t = jnp.concatenate([x.T for x in per_head(q_here)], axis=1)
        g_t = jnp.concatenate([x.T for x in per_head(g_here)], axis=1)
        most = None
        for c in chunks:
            raw = nt(picked(k_s, c, 0), q_t)
            s_n[rows_of(c), :] = raw
            top = jnp.max(in_rows(raw), axis=0)
            most = top if most is None else jnp.maximum(most, top)
            yield
        top_row = jnp.max(most, axis=0, keepdims=True) * factor
        total = jnp.zeros((8, ROWS), jnp.float32)
        for c in chunks:
            for j in c:
                rows = slice(j * BLOCK, (j + 1) * BLOCK)
                e = jnp.exp2(s_n[rows, :] * factor - (top_row - bias[j]))
                e_n[rows, :] = e
                total = total + jnp.sum(in_rows(e), axis=0)
            yield
        inverse = 1.0 / jnp.sum(total, axis=0, keepdims=True)
        o_t = jnp.zeros((HD, ROWS), jnp.float32)
        for c in chunks:
            probs = (e_n[rows_of(c), :] * inverse).astype(jnp.bfloat16)
            o_t = o_t + nt(picked(vt_s, c, 1), probs)
            add_blocks(dv_s, c, nt(probs, g_rows))
            yield
        row_dot = jnp.sum(g_t.astype(jnp.float32) * o_t, axis=0, keepdims=True)
        write(n, 0, o_t)
        weight_scale = inverse * scale
        tau_rows = jnp.zeros((8, ROWS), jnp.float32)
        dq_t = jnp.zeros((HD, ROWS), jnp.float32)
        for c in chunks:
            dweights = nt(picked(v_s, c, 0), g_t)
            scaled = e_n[rows_of(c), :] * weight_scale * (dweights - row_dot)
            tau_rows = tau_rows + jnp.sum(in_rows(scaled * s_n[rows_of(c), :]), axis=0)
            low = scaled.astype(jnp.bfloat16)
            dq_t = dq_t + nt(picked(kt_s, c, 1), low)
            add_blocks(dk_s, c, nt(low, q_rows))
            yield
        tau_s[n] += tau_rows
        write(n, 1, dq_t)

    def write(n, which, x_t):
        low = x_t.astype(jnp.bfloat16)
        out = jnp.concatenate([x.T for x in per_head(low)], axis=1)
        if n:
            sib_out[which] = out
        else:
            (att_own, dq_own)[which][...] = out

    shares = [part(n) for n in range(2)]
    for turn in range(6 * len(chunks)):
        for n, share in enumerate(shares):
            if turn >= n * len(chunks):
                next(share, None)

    @pl.when(step == local_blocks - 1)
    def _():
        lane = lax.broadcasted_iota(jnp.int32, (TAIL, HD), 1)
        sums = inputs[5][...] if gi else jnp.zeros((TAIL, HD), jnp.float32)
        for h in range(QPG):
            head = group * QPG + h
            rows = tau_s[:, :, h * BLOCK : (h + 1) * BLOCK]
            sums = sums + jnp.where(lane == head, jnp.sum(rows) / taus[head], 0.0)
        tau_out[...] = sums

        def drain(b, carry):
            for half in range(local_blocks):
                at = b * local_blocks + half
                rows = slice(half * BLOCK, (half + 1) * BLOCK)
                kv_out[b, 0, rows, :] = dk_s[at].astype(jnp.bfloat16)
                kv_out[b, 1, rows, :] = dv_s[at].astype(jnp.bfloat16)
            return carry

        lax.fori_loop(0, devices, drain, 0, unroll=2)


def times_bias(times):
    return math.log2(times) if times else NEVER


def run_group(gi, devices, place, key_blocks, tau, queries, out_grad, qg_sib, kv_in, tau_in, offsets):
    listed = len(offsets[0])
    tokens = queries.shape[0]
    local_blocks = tokens // BLOCK
    blocks = devices * local_blocks
    width = QPG * HD
    block_own = pl.BlockSpec((BLOCK, width), lambda u, p, s, t: (u, 2 * (p[0] % 2) + gi))
    qs = pl.BlockSpec((1, BLOCK, width), lambda u, p, s, t: (0, u, gi))
    gs = pl.BlockSpec((1, BLOCK, width), lambda u, p, s, t: (1, u, gi))
    out_own = pl.BlockSpec((BLOCK, width), lambda u, p, s, t: (u, 0))
    out_sib = pl.BlockSpec((2, BLOCK, width), lambda u, p, s, t: (0, u, 0))
    kv_all = pl.BlockSpec((devices, 2, tokens, HD), lambda u, p, s, t: (0, 0, 0, 0))
    small = pl.BlockSpec((TAIL, HD), lambda u, p, s, t: (0, 0))
    bf = lambda *shape: jax.ShapeDtypeStruct(shape, jnp.bfloat16)
    keys_wide = listed * BLOCK
    cells = 2 * local_blocks * ROWS * keys_wide
    return pl.pallas_call(
        functools.partial(group_kernel, gi, devices, local_blocks, listed, offsets),
        grid_spec=pltpu.PrefetchScalarGridSpec(
            num_scalar_prefetch=3,
            grid=(local_blocks,),
            in_specs=[block_own, qs, block_own, gs, kv_all] + [small] * gi,
            out_specs=[out_own, out_own, out_sib, small, kv_all],
            scratch_shapes=[pltpu.VMEM((blocks, BLOCK, HD), jnp.bfloat16)] * 4
            + [pltpu.VMEM((blocks, BLOCK, HD), jnp.float32)] * 2
            + [pltpu.VMEM((2, keys_wide, ROWS), jnp.float32)] * 2
            + [pltpu.VMEM((2, 8, ROWS), jnp.float32)],
        ),
        out_shape=[bf(tokens, width), bf(tokens, width), bf(2, tokens, width)]
        + [jax.ShapeDtypeStruct((TAIL, HD), jnp.float32), bf(devices, 2, tokens, HD)],
        compiler_params=pltpu.CompilerParams(
            dimension_semantics=("arbitrary",), vmem_limit_bytes=60 * 2**20
        ),
        cost_estimate=pl.CostEstimate(
            flops=12 * HD * cells, bytes_accessed=6 * 2**20, transcendentals=cells
        ),
        name="group_attention",
    )(place, key_blocks, tau, queries, qg_sib, out_grad, qg_sib, kv_in, *tau_in[:gi])


def total_over(x, axis):
    size = lax.axis_size(axis)
    if size & (size - 1):
        return lax.psum(x, axis)
    step = 1
    while step < size:
        radix = min(8, size // step)
        terms = [x] + [
            lax.ppermute(x, axis, [(i, i ^ (step * d)) for i in range(size)]) for d in range(1, radix)
        ]
        while len(terms) > 1:
            terms = [a + b for a, b in zip(terms[::2], terms[1::2])]
        x = terms[0]
        step *= radix
    return x


def spread(gi, devices, keys, values):
    tokens = keys.shape[0]

    def kernel(k_ref, v_ref, out, sems):
        copies = []
        for d in range(devices):
            group = 2 * (d % 2) + gi
            for which, ref in enumerate((k_ref, v_ref)):
                source = ref.at[:, group * HD : (group + 1) * HD]
                copies.append(pltpu.make_async_copy(source, out.at[d, which], sems.at[d, which]))
        for copy in copies:
            copy.start()
        for copy in copies:
            copy.wait()

    anywhere = pl.BlockSpec(memory_space=pl.ANY)
    return pl.pallas_call(
        kernel,
        in_specs=[anywhere, anywhere],
        out_specs=anywhere,
        out_shape=jax.ShapeDtypeStruct((devices, 2, tokens, HD), jnp.bfloat16),
        scratch_shapes=[pltpu.SemaphoreType.DMA((devices, 2))],
        compiler_params=pltpu.CompilerParams(vmem_limit_bytes=60 * 2**20),
        name="spread_keys_values",
    )(keys, values)


def body(queries, keys, values, tau, out_grad, key_blocks):
    ctx = lax.axis_size("ctx")
    me = lax.axis_index("ctx").astype(jnp.int32)
    core = me % 2
    tokens = queries.shape[1]
    local_blocks = tokens // BLOCK
    block_count = ctx * local_blocks
    listed_count = key_blocks.shape[2]
    offsets = distinct_offsets(block_count, listed_count)
    swap = [(d, d ^ 1) for d in range(ctx)]
    wide = 2 * QPG * HD

    q0, k0, v0, g0 = queries[0], keys[0], values[0], out_grad[0]
    place = me[None]

    def kv_for(gi):
        return lax.all_to_all(spread(gi, ctx, k0, v0), "ctx", 0, 0)

    def theirs(x):
        return lax.dynamic_slice_in_dim(x, (1 - core) * wide, wide, 1)

    kv_in = [kv_for(gi) for gi in range(2)]
    qg_sib = lax.ppermute(jnp.stack([theirs(q0), theirs(g0)]), "ctx", swap)

    sibs, owns, grads, tau_rows = [], [], [], []
    for gi in range(2):
        att_own, dq_own, sib, tau_here, kv_grads = run_group(
            gi, ctx, place, key_blocks, tau, q0, g0, qg_sib, kv_in[gi], tau_rows, offsets
        )
        tau_rows.append(tau_here)
        if gi:
            kv_grads, grads[0] = lax.optimization_barrier((kv_grads, grads[0]))
        owns.append((att_own, dq_own))
        sibs.append(lax.ppermute(sib, "ctx", swap))
        grads.append(lax.all_to_all(kv_grads, "ctx", 0, 0))
    tau_all, sibs = lax.optimization_barrier((tau_rows[1], sibs))
    att_parts, dq_parts = (
        [(own[which], sib[which]) for own, sib in zip(owns, sibs)] for which in range(2)
    )

    def by_group(parts):
        return jnp.concatenate(
            [jnp.where(core == c // 2, parts[c % 2][0], parts[c % 2][1]) for c in range(4)], axis=1
        )

    attended = by_group(att_parts)[None]
    query_grad = by_group(dq_parts)[None]

    def summed(which):
        cols = []
        for c in range(4):
            total = None
            for src in range(c // 2, ctx, 2):
                term = grads[c % 2][src, which].astype(jnp.float32)
                total = term if total is None else total + term
            cols.append(total.astype(jnp.bfloat16))
        return jnp.concatenate(cols, axis=1)[None]

    key_grad, value_grad = summed(0), summed(1)
    scale_total = total_over(total_over(tau_all[:1], "batch"), "ctx")[0, :HEADS]
    tau_grad = scale_total / math.sqrt(lax.axis_size("batch") * ctx * tokens)
    return (attended, query_grad, key_grad, value_grad, tau_grad)


def solution(mesh):
    rows = P("batch", "ctx", None)
    return jax.shard_map(
        body,
        mesh=mesh,
        in_specs=(rows, rows, rows, P(), rows, P()),
        out_specs=(rows, rows, rows, rows, P()),
        check_vma=False,
    )
```

```python
import functools
import math

import jax
import jax.numpy as jnp
from jax import lax
from jax.experimental import pallas as pl
from jax.experimental.pallas import tpu as pltpu
from jax.sharding import PartitionSpec as P

HEADS = 16
KV_HEADS = 4
HD = 128
BLOCK = 128
QPG = HEADS // KV_HEADS
CHUNK = 4
ROWS = QPG * BLOCK
TAIL = 16
STRIDES = (2, 3)
LOG2E = math.log2(math.e)
NEVER = -1e30


def distinct_offsets(block_count, listed_count):
    tables = []
    for stride in STRIDES:
        steps = range(1, (listed_count - 3) // 2 + 1)
        listed = [-1, 0, 1] + [stride * m for m in steps] + [-stride * m for m in steps]
        times = {}
        for o in listed:
            times[o % block_count] = times.get(o % block_count, 0) + 1
        tables.append(sorted(times.items()))
    most = max(len(t) for t in tables)
    return [t + [(0, 0)] * (most - len(t)) for t in tables]


def nt(a, b):
    return jnp.dot(a, b, preferred_element_type=jnp.float32)


def group_kernel(gi, devices, local_blocks, listed, offsets, *refs):
    place, key_blocks, taus = refs[:3]
    inputs, rest = refs[3 : 8 + gi], refs[8 + gi :]
    q_own, q_sib, g_own, g_sib, kv_in = inputs[:5]
    att_own, dq_own, sib_out, tau_out, kv_out = rest[:5]
    kt_s, vt_s, dk_s, dv_s, s_s, e_s = rest[5:]
    blocks = devices * local_blocks
    me = place[0]
    group = 2 * (me % 2) + gi
    units = 2 * local_blocks

    chunks = [range(c, min(c + CHUNK, listed)) for c in range(0, listed, CHUNK)]
    scale = jnp.concatenate(
        [jnp.full((1, BLOCK), taus[group * QPG + h], jnp.float32) for h in range(QPG)], axis=1
    ) / math.sqrt(HD)
    factor = scale * LOG2E

    def rows_of(c):
        return slice(c[0] * BLOCK, (c[-1] + 1) * BLOCK)

    def per_head(x):
        return [x[:, h * HD : (h + 1) * HD] for h in range(QPG)]

    def in_rows(x):
        return x.reshape(-1, 8, ROWS)

    tau_totals = []

    def part(n):
        s_n, e_n = s_s.at[n], e_s.at[n]
        side, at = n // local_blocks, n % local_blocks
        here = slice(at * BLOCK, (at + 1) * BLOCK)
        query_block = (me ^ side) * local_blocks + at
        wide = (key_blocks[group, query_block, 3] - query_block) % blocks == STRIDES[1]
        ids, bias = [], []
        for (narrow_off, narrow_times), (wide_off, wide_times) in zip(*offsets):
            ids.append((query_block + jnp.where(wide, wide_off, narrow_off)) % blocks)
            bias.append(
                times_bias(narrow_times)
                if narrow_times == wide_times
                else jnp.where(wide, times_bias(wide_times), times_bias(narrow_times))
            )

        def taken(which, c):
            return jnp.concatenate([kv_in[ids[j], which] for j in c], axis=0)

        def picked(ref, c, axis):
            return jnp.concatenate([ref[ids[j]] for j in c], axis=axis)

        def add_blocks(ref, c, x):
            for n, j in enumerate(c):
                ref[ids[j]] += x[n * BLOCK : (n + 1) * BLOCK, :]

        q_here = q_sib[0, here, :] if side else q_own[here, :]
        g_here = g_sib[0, here, :] if side else g_own[here, :]
        q_rows = jnp.concatenate(per_head(q_here), axis=0)
        g_rows = jnp.concatenate(per_head(g_here), axis=0)
        q_t = jnp.concatenate([x.T for x in per_head(q_here)], axis=1)
        g_t = jnp.concatenate([x.T for x in per_head(g_here)], axis=1)
        most = None
        for c in chunks:
            raw = nt(taken(0, c), q_t)
            s_n[rows_of(c), :] = raw
            top = jnp.max(in_rows(raw), axis=0)
            most = top if most is None else jnp.maximum(most, top)
            yield
        top_row = jnp.max(most, axis=0, keepdims=True) * factor
        total = jnp.zeros((8, ROWS), jnp.float32)
        for c in chunks:
            for j in c:
                rows = slice(j * BLOCK, (j + 1) * BLOCK)
                e = jnp.exp2(s_n[rows, :] * factor - (top_row - bias[j]))
                e_n[rows, :] = e
                total = total + jnp.sum(in_rows(e), axis=0)
            yield
        inverse = 1.0 / jnp.sum(total, axis=0, keepdims=True)
        o_t = jnp.zeros((HD, ROWS), jnp.float32)
        for c in chunks:
            probs = (e_n[rows_of(c), :] * inverse).astype(jnp.bfloat16)
            o_t = o_t + nt(picked(vt_s, c, 1), probs)
            add_blocks(dv_s, c, nt(probs, g_rows))
            yield
        row_dot = jnp.sum(g_t.astype(jnp.float32) * o_t, axis=0, keepdims=True)
        write(side, here, 0, o_t)
        weight_scale = inverse * scale
        tau_rows = jnp.zeros((8, ROWS), jnp.float32)
        dq_t = jnp.zeros((HD, ROWS), jnp.float32)
        for c in chunks:
            dweights = nt(taken(1, c), g_t)
            scaled = e_n[rows_of(c), :] * weight_scale * (dweights - row_dot)
            tau_rows = tau_rows + jnp.sum(in_rows(scaled * s_n[rows_of(c), :]), axis=0)
            low = scaled.astype(jnp.bfloat16)
            dq_t = dq_t + nt(picked(kt_s, c, 1), low)
            add_blocks(dk_s, c, nt(low, q_rows))
            yield
        tau_totals.append(tau_rows)
        write(side, here, 1, dq_t)

    def write(side, here, which, x_t):
        low = x_t.astype(jnp.bfloat16)
        out = jnp.concatenate([x.T for x in per_head(low)], axis=1)
        if side:
            sib_out[which, here, :] = out
        else:
            (att_own, dq_own)[which][here, :] = out

    def turned(which, ref, wait):
        turns = 2 * len(chunks)
        for turn in range(wait):
            yield
        for turn in range(turns):
            for b in range(blocks * turn // turns, blocks * (turn + 1) // turns):
                ref[b] = kv_in[b, which].T
            yield

    dk_s[...] = jnp.zeros_like(dk_s)
    dv_s[...] = jnp.zeros_like(dv_s)
    shares = [(0, turned(1, vt_s, 0)), (0, turned(0, kt_s, len(chunks)))]
    shares += [(n * len(chunks), part(n)) for n in range(units)]
    for turn in range((4 + units) * len(chunks)):
        for begin, share in shares:
            if turn >= begin:
                next(share, None)

    lane = lax.broadcasted_iota(jnp.int32, (TAIL, HD), 1)
    row = lax.broadcasted_iota(jnp.int32, (TAIL, HD), 0)
    sums = inputs[5][...] if gi else jnp.zeros((TAIL, HD), jnp.float32)
    tau_rows = functools.reduce(jnp.add, tau_totals)
    for h in range(QPG):
        head = group * QPG + h
        total = jnp.sum(tau_rows[:, h * BLOCK : (h + 1) * BLOCK])
        sums = sums + jnp.where(lane == head, total / taus[head], 0.0)
    tau_out[...] = sums
    high = sums.astype(jnp.bfloat16).astype(jnp.float32)
    mid = (sums - high).astype(jnp.bfloat16).astype(jnp.float32)
    low = sums - high - mid
    tail = jnp.where(row == 0, high, jnp.where(row == 1, mid, jnp.where(row == 2, low, 0.0)))

    def drain(d, carry):
        for half in range(local_blocks):
            for which, ref in enumerate((dk_s, dv_s)):
                at = (2 * half + which) * BLOCK
                kv_out[d, at : at + BLOCK, :] = ref[d * local_blocks + half].astype(jnp.bfloat16)
        kv_out[d, 2 * local_blocks * BLOCK :, :] = tail.astype(jnp.bfloat16)
        return carry

    lax.fori_loop(0, devices, drain, 0, unroll=2)


def times_bias(times):
    return math.log2(times) if times else NEVER


def run_group(gi, devices, place, key_blocks, tau, queries, out_grad, qg_sib, kv_in, tau_in, offsets):
    listed = len(offsets[0])
    tokens = queries.shape[0]
    local_blocks = tokens // BLOCK
    blocks = devices * local_blocks
    width = QPG * HD
    block_own = pl.BlockSpec((tokens, width), lambda u, p, s, t: (0, 2 * (p[0] % 2) + gi))
    qs = pl.BlockSpec((1, tokens, width), lambda u, p, s, t: (0, 0, gi))
    gs = pl.BlockSpec((1, tokens, width), lambda u, p, s, t: (1, 0, gi))
    out_own = pl.BlockSpec((tokens, width), lambda u, p, s, t: (0, 0))
    out_sib = pl.BlockSpec((2, tokens, width), lambda u, p, s, t: (0, 0, 0))
    kv_all = pl.BlockSpec((blocks, 2, BLOCK, HD), lambda u, p, s, t: (0, 0, 0, 0))
    kv_back = pl.BlockSpec((devices, 2 * tokens + TAIL, HD), lambda u, p, s, t: (0, 0, 0))
    small = pl.BlockSpec((TAIL, HD), lambda u, p, s, t: (0, 0))
    bf = lambda *shape: jax.ShapeDtypeStruct(shape, jnp.bfloat16)
    keys_wide = listed * BLOCK
    cells = 2 * local_blocks * ROWS * keys_wide
    return pl.pallas_call(
        functools.partial(group_kernel, gi, devices, local_blocks, listed, offsets),
        grid_spec=pltpu.PrefetchScalarGridSpec(
            num_scalar_prefetch=3,
            grid=(1,),
            in_specs=[block_own, qs, block_own, gs, kv_all] + [small] * gi,
            out_specs=[out_own, out_own, out_sib, small, kv_back],
            scratch_shapes=[pltpu.VMEM((blocks, HD, BLOCK), jnp.bfloat16)] * 2
            + [pltpu.VMEM((blocks, BLOCK, HD), jnp.float32)] * 2
            + [pltpu.VMEM((2 * local_blocks, keys_wide, ROWS), jnp.float32)] * 2,
        ),
        out_shape=[bf(tokens, width), bf(tokens, width), bf(2, tokens, width)]
        + [jax.ShapeDtypeStruct((TAIL, HD), jnp.float32), bf(devices, 2 * tokens + TAIL, HD)],
        compiler_params=pltpu.CompilerParams(
            dimension_semantics=("arbitrary",), vmem_limit_bytes=60 * 2**20
        ),
        cost_estimate=pl.CostEstimate(
            flops=12 * HD * cells, bytes_accessed=6 * 2**20, transcendentals=cells
        ),
        name="group_attention",
    )(place, key_blocks, tau, queries, qg_sib, out_grad, qg_sib, kv_in, *tau_in[:gi])


def spread(gi, devices, keys, values):
    tokens, width = keys.shape
    local_blocks = tokens // BLOCK

    def kernel(k_ref, v_ref, out):
        for parity in range(2):
            cols = slice((2 * parity + gi) * HD, (2 * parity + gi + 1) * HD)
            for half in range(local_blocks):
                rows = slice(half * BLOCK, (half + 1) * BLOCK)
                out[parity, half, 0] = k_ref[rows, cols]
                out[parity, half, 1] = v_ref[rows, cols]

    taken = pl.BlockSpec((tokens, width), lambda d: (0, 0))
    block = (2, local_blocks, 2, BLOCK, HD)
    return pl.pallas_call(
        kernel,
        grid=(devices // 2,),
        in_specs=[taken, taken],
        out_specs=pl.BlockSpec(block, lambda d: (d, 0, 0, 0, 0)),
        out_shape=jax.ShapeDtypeStruct((devices, *block[1:]), jnp.bfloat16),
        compiler_params=pltpu.CompilerParams(vmem_limit_bytes=60 * 2**20),
        name="spread_keys_values",
    )(keys, values)


def body(queries, keys, values, tau, out_grad, key_blocks):
    ctx = lax.axis_size("ctx")
    me = lax.axis_index("ctx").astype(jnp.int32)
    core = me % 2
    tokens = queries.shape[1]
    local_blocks = tokens // BLOCK
    block_count = ctx * local_blocks
    listed_count = key_blocks.shape[2]
    offsets = distinct_offsets(block_count, listed_count)
    swap = [(d, d ^ 1) for d in range(ctx)]
    wide = 2 * QPG * HD

    q0, k0, v0, g0 = queries[0], keys[0], values[0], out_grad[0]
    place = me[None]

    def kv_for(gi):
        arrived = lax.all_to_all(spread(gi, ctx, k0, v0), "ctx", 0, 0)
        return arrived.reshape(block_count, 2, BLOCK, HD)

    def theirs(x):
        return lax.dynamic_slice_in_dim(x, (1 - core) * wide, wide, 1)

    kv_in = [kv_for(gi) for gi in range(2)]
    qg_sib = lax.ppermute(jnp.stack([theirs(q0), theirs(g0)]), "ctx", swap)

    sibs, owns, grads, tau_rows = [], [], [], []
    for gi in range(2):
        att_own, dq_own, sib, tau_here, kv_grads = run_group(
            gi, ctx, place, key_blocks, tau, q0, g0, qg_sib, kv_in[gi], tau_rows, offsets
        )
        tau_rows.append(tau_here)
        if gi:
            kv_grads, grads[0] = lax.optimization_barrier((kv_grads, grads[0]))
        owns.append((att_own, dq_own))
        sibs.append(lax.ppermute(sib, "ctx", swap))
        grads.append(lax.all_to_all(kv_grads, "ctx", 0, 0))
    sibs = lax.optimization_barrier(sibs)
    att_parts, dq_parts = (
        [(own[which], sib[which]) for own, sib in zip(owns, sibs)] for which in range(2)
    )

    def by_group(parts):
        return jnp.concatenate(
            [jnp.where(core == c // 2, parts[c % 2][0], parts[c % 2][1]) for c in range(4)], axis=1
        )

    attended = by_group(att_parts)[None]
    query_grad = by_group(dq_parts)[None]

    def summed(which):
        cols = []
        for c in range(4):
            total = None
            for src in range(c // 2, ctx, 2):
                term = grads[c % 2][src, : 2 * tokens].reshape(local_blocks, 2, BLOCK, HD)[:, which]
                term = term.astype(jnp.float32)
                total = term if total is None else total + term
            cols.append(total.reshape(tokens, HD).astype(jnp.bfloat16))
        return jnp.concatenate(cols, axis=1)[None]

    key_grad, value_grad = summed(0), summed(1)
    tails = grads[1][:, 2 * tokens : 2 * tokens + 3].astype(jnp.float32)
    here = jnp.sum(tails, axis=(0, 1))
    batch = lax.axis_size("batch")
    over_batch = lax.all_to_all(jnp.broadcast_to(here, (batch, 1, HD)), "batch", 0, 0)
    scale_total = jnp.sum(over_batch, axis=(0, 1))[:HEADS]
    tau_grad = scale_total / math.sqrt(lax.axis_size("batch") * ctx * tokens)
    return (attended, query_grad, key_grad, value_grad, tau_grad)


def solution(mesh):
    rows = P("batch", "ctx", None)
    return jax.shard_map(
        body,
        mesh=mesh,
        in_specs=(rows, rows, rows, P(), rows, P()),
        out_specs=(rows, rows, rows, rows, P()),
        check_vma=False,
    )
```

```python
import functools
import math

import jax
import jax.numpy as jnp
from jax import lax
from jax.experimental import pallas as pl
from jax.experimental.pallas import tpu as pltpu
from jax.sharding import PartitionSpec as P

HEADS = 16
KV_HEADS = 4
HD = 128
BLOCK = 128
QPG = HEADS // KV_HEADS
CHUNK = 4
ROWS = QPG * BLOCK
TAIL = 8
VMEM_BYTES = 63 * 2**20
STRIDES = (2, 3)
LOG2E = math.log2(math.e)
NEVER = -1e30


def distinct_offsets(block_count, listed_count):
    tables = []
    for stride in STRIDES:
        steps = range(1, (listed_count - 3) // 2 + 1)
        listed = [-1, 0, 1] + [stride * m for m in steps] + [-stride * m for m in steps]
        times = {}
        for o in listed:
            times[o % block_count] = times.get(o % block_count, 0) + 1
        tables.append(sorted(times.items()))
    most = max(len(t) for t in tables)
    return [t + [(0, 0)] * (most - len(t)) for t in tables]


def nt(a, b):
    return jnp.dot(a, b, preferred_element_type=jnp.float32)


def group_kernel(gi, devices, local_blocks, listed, offsets, *refs):
    place, strides, taus = refs[:3]
    inputs, rest = refs[3 : 8 + gi], refs[8 + gi :]
    q_own, q_sib, g_own, g_sib, kv_in = inputs[:5]
    att_own, dq_own, sib_out, tau_out, kv_out = rest[:5]
    kt_s, vt_s, dk_s, dv_s, s_s, e_s = rest[5:]
    blocks = devices * local_blocks
    me = place[0]
    group = 2 * (me % 2) + gi
    units = 2 * local_blocks

    chunks = [range(c, min(c + CHUNK, listed)) for c in range(0, listed, CHUNK)]
    scale = jnp.concatenate(
        [jnp.full((1, BLOCK), taus[group * QPG + h], jnp.float32) for h in range(QPG)], axis=1
    ) / math.sqrt(HD)
    factor = scale * LOG2E

    def rows_of(c):
        return slice(c[0] * BLOCK, (c[-1] + 1) * BLOCK)

    def per_head(x):
        return [x[:, h * HD : (h + 1) * HD] for h in range(QPG)]

    def in_rows(x):
        return x.reshape(-1, 8, ROWS)

    tau_totals = []

    def part(n):
        s_n, e_n = s_s.at[n], e_s.at[n]
        side, at = n // local_blocks, n % local_blocks
        here = slice(at * BLOCK, (at + 1) * BLOCK)
        query_block = (me ^ side) * local_blocks + at
        wide = strides[group * blocks + query_block] == STRIDES[1]
        ids, bias = [], []
        for (narrow_off, narrow_times), (wide_off, wide_times) in zip(*offsets):
            ids.append((query_block + jnp.where(wide, wide_off, narrow_off)) % blocks)
            bias.append(
                times_bias(narrow_times)
                if narrow_times == wide_times
                else jnp.where(wide, times_bias(wide_times), times_bias(narrow_times))
            )

        def taken(which, c):
            return jnp.concatenate([kv_in[ids[j], which] for j in c], axis=0)

        def picked(ref, c, axis):
            return jnp.concatenate([ref[ids[j]] for j in c], axis=axis)

        def add_blocks(ref, c, x):
            for n, j in enumerate(c):
                ref[ids[j]] += x[n * BLOCK : (n + 1) * BLOCK, :]

        q_here = q_sib[0, here, :] if side else q_own[here, :]
        g_here = g_sib[0, here, :] if side else g_own[here, :]
        q_rows = jnp.concatenate(per_head(q_here), axis=0)
        g_rows = jnp.concatenate(per_head(g_here), axis=0)
        q_t = jnp.concatenate([x.T for x in per_head(q_here)], axis=1)
        g_t = jnp.concatenate([x.T for x in per_head(g_here)], axis=1)
        most = None
        for c in chunks:
            raw = nt(taken(0, c), q_t)
            s_n[rows_of(c), :] = raw
            top = jnp.max(in_rows(raw), axis=0)
            most = top if most is None else jnp.maximum(most, top)
            yield
        top_row = jnp.max(most, axis=0, keepdims=True) * factor
        total = jnp.zeros((8, ROWS), jnp.float32)
        for c in chunks:
            for j in c:
                rows = slice(j * BLOCK, (j + 1) * BLOCK)
                e = jnp.exp2(s_n[rows, :] * factor - (top_row - bias[j]))
                e_n[rows, :] = e
                total = total + jnp.sum(in_rows(e), axis=0)
            yield
        inverse = 1.0 / jnp.sum(total, axis=0, keepdims=True)
        o_t = jnp.zeros((HD, ROWS), jnp.float32)
        for c in chunks:
            probs = (e_n[rows_of(c), :] * inverse).astype(jnp.bfloat16)
            o_t = o_t + nt(picked(vt_s, c, 1), probs)
            add_blocks(dv_s, c, nt(probs, g_rows))
            yield
        row_dot = jnp.sum(g_t.astype(jnp.float32) * o_t, axis=0, keepdims=True)
        write(side, here, 0, o_t)
        weight_scale = inverse * scale
        tau_rows = jnp.zeros((8, ROWS), jnp.float32)
        dq_t = jnp.zeros((HD, ROWS), jnp.float32)
        for c in chunks:
            dweights = nt(taken(1, c), g_t)
            scaled = e_n[rows_of(c), :] * weight_scale * (dweights - row_dot)
            tau_rows = tau_rows + jnp.sum(in_rows(scaled * s_n[rows_of(c), :]), axis=0)
            low = scaled.astype(jnp.bfloat16)
            dq_t = dq_t + nt(picked(kt_s, c, 1), low)
            add_blocks(dk_s, c, nt(low, q_rows))
            yield
        tau_totals.append(tau_rows)
        write(side, here, 1, dq_t)

    def write(side, here, which, x_t):
        low = x_t.astype(jnp.bfloat16)
        out = jnp.concatenate([x.T for x in per_head(low)], axis=1)
        if side:
            sib_out[which, here, :] = out
        else:
            (att_own, dq_own)[which][here, :] = out

    def turned(which, ref, wait):
        turns = 2 * len(chunks)
        for turn in range(wait):
            yield
        for turn in range(turns):
            for b in range(blocks * turn // turns, blocks * (turn + 1) // turns):
                ref[b] = kv_in[b, which].T
            yield

    dk_s[...] = jnp.zeros_like(dk_s)
    dv_s[...] = jnp.zeros_like(dv_s)
    shares = [(0, turned(1, vt_s, 0)), (0, turned(0, kt_s, len(chunks)))]
    shares += [(n * len(chunks), part(n)) for n in range(units)]
    for turn in range((4 + units) * len(chunks)):
        for begin, share in shares:
            if turn >= begin:
                next(share, None)

    lane = lax.broadcasted_iota(jnp.int32, (TAIL, HD), 1)
    sums = inputs[5][...] if gi else jnp.zeros((TAIL, HD), jnp.float32)
    tau_rows = functools.reduce(jnp.add, tau_totals)
    for h in range(QPG):
        head = group * QPG + h
        total = jnp.sum(tau_rows[:, h * BLOCK : (h + 1) * BLOCK])
        sums = sums + jnp.where(lane == head, total / taus[head], 0.0)
    tau_out[...] = sums

    def drain(d, carry):
        for half in range(local_blocks):
            for which, ref in enumerate((dk_s, dv_s)):
                at = (2 * half + which) * BLOCK
                kv_out[d, at : at + BLOCK, :] = ref[d * local_blocks + half].astype(jnp.bfloat16)
        return carry

    lax.fori_loop(0, devices, drain, 0, unroll=2)


def times_bias(times):
    return math.log2(times) if times else NEVER


def run_group(gi, devices, place, strides, tau, queries, out_grad, qg_sib, kv_in, tau_in, offsets):
    listed = len(offsets[0])
    tokens = queries.shape[0]
    local_blocks = tokens // BLOCK
    blocks = devices * local_blocks
    width = QPG * HD
    block_own = pl.BlockSpec((tokens, width), lambda u, p, s, t: (0, 2 * (p[0] % 2) + gi))
    qs = pl.BlockSpec((1, tokens, width), lambda u, p, s, t: (0, 0, gi))
    gs = pl.BlockSpec((1, tokens, width), lambda u, p, s, t: (1, 0, gi))
    out_own = pl.BlockSpec((tokens, width), lambda u, p, s, t: (0, 0))
    out_sib = pl.BlockSpec((2, tokens, width), lambda u, p, s, t: (0, 0, 0))
    kv_all = pl.BlockSpec((blocks, 2, BLOCK, HD), lambda u, p, s, t: (0, 0, 0, 0))
    kv_back = pl.BlockSpec((devices, 2 * tokens, HD), lambda u, p, s, t: (0, 0, 0))
    small = pl.BlockSpec((TAIL, HD), lambda u, p, s, t: (0, 0))
    bf = lambda *shape: jax.ShapeDtypeStruct(shape, jnp.bfloat16)
    keys_wide = listed * BLOCK
    cells = 2 * local_blocks * ROWS * keys_wide
    return pl.pallas_call(
        functools.partial(group_kernel, gi, devices, local_blocks, listed, offsets),
        grid_spec=pltpu.PrefetchScalarGridSpec(
            num_scalar_prefetch=3,
            grid=(1,),
            in_specs=[block_own, qs, block_own, gs, kv_all] + [small] * gi,
            out_specs=[out_own, out_own, out_sib, small, kv_back],
            scratch_shapes=[pltpu.VMEM((blocks, HD, BLOCK), jnp.bfloat16)] * 2
            + [pltpu.VMEM((blocks, BLOCK, HD), jnp.float32)] * 2
            + [pltpu.VMEM((2 * local_blocks, keys_wide, ROWS), jnp.float32)] * 2,
        ),
        out_shape=[bf(tokens, width), bf(tokens, width), bf(2, tokens, width)]
        + [jax.ShapeDtypeStruct((TAIL, HD), jnp.float32), bf(devices, 2 * tokens, HD)],
        compiler_params=pltpu.CompilerParams(
            dimension_semantics=("arbitrary",), vmem_limit_bytes=VMEM_BYTES
        ),
        cost_estimate=pl.CostEstimate(
            flops=12 * HD * cells, bytes_accessed=6 * 2**20, transcendentals=cells
        ),
        name="group_attention",
    )(place, strides, tau, queries, qg_sib, out_grad, qg_sib, kv_in, *tau_in[:gi])


def total_over(x, axis):
    size = lax.axis_size(axis)
    if size & (size - 1):
        return lax.psum(x, axis)

    def partner(distance):
        return lax.ppermute(x, axis, [(i, i ^ distance) for i in range(size)])

    step = 1
    while step < size:
        if size // step % 4 == 0 and size // step != 8:
            x = (x + partner(step)) + (partner(2 * step) + partner(3 * step))
            step *= 4
        else:
            x = x + partner(step)
            step *= 2
    return x


def spread(gi, devices, keys, values):
    tokens, width = keys.shape
    local_blocks = tokens // BLOCK

    def kernel(k_ref, v_ref, out):
        for parity in range(2):
            cols = slice((2 * parity + gi) * HD, (2 * parity + gi + 1) * HD)
            for half in range(local_blocks):
                rows = slice(half * BLOCK, (half + 1) * BLOCK)
                out[parity, half, 0] = k_ref[rows, cols]
                out[parity, half, 1] = v_ref[rows, cols]

    taken = pl.BlockSpec((tokens, width), lambda d: (0, 0))
    block = (2, local_blocks, 2, BLOCK, HD)
    return pl.pallas_call(
        kernel,
        grid=(devices // 2,),
        in_specs=[taken, taken],
        out_specs=pl.BlockSpec(block, lambda d: (d, 0, 0, 0, 0)),
        out_shape=jax.ShapeDtypeStruct((devices, *block[1:]), jnp.bfloat16),
        compiler_params=pltpu.CompilerParams(vmem_limit_bytes=VMEM_BYTES),
        name="spread_keys_values",
    )(keys, values)


def body(queries, keys, values, tau, out_grad, key_blocks):
    ctx = lax.axis_size("ctx")
    me = lax.axis_index("ctx").astype(jnp.int32)
    core = me % 2
    tokens = queries.shape[1]
    local_blocks = tokens // BLOCK
    block_count = ctx * local_blocks
    listed_count = key_blocks.shape[2]
    offsets = distinct_offsets(block_count, listed_count)
    swap = [(d, d ^ 1) for d in range(ctx)]
    wide = 2 * QPG * HD

    q0, k0, v0, g0 = queries[0], keys[0], values[0], out_grad[0]
    place = me[None]

    def kv_for(gi):
        arrived = lax.all_to_all(spread(gi, ctx, k0, v0), "ctx", 0, 0)
        return arrived.reshape(block_count, 2, BLOCK, HD)

    def theirs(x):
        return lax.dynamic_slice_in_dim(x, (1 - core) * wide, wide, 1)

    kv_in = [kv_for(gi) for gi in range(2)]
    strides = (key_blocks[:, :, 3] - jnp.arange(block_count, dtype=jnp.int32)) % block_count
    rows, strides = lax.optimization_barrier((jnp.stack([theirs(q0), theirs(g0)]), strides.reshape(-1)))
    qg_sib = lax.ppermute(rows, "ctx", swap)

    sibs, owns, grads, tau_rows = [], [], [], []
    for gi in range(2):
        att_own, dq_own, sib, tau_here, kv_grads = run_group(
            gi, ctx, place, strides, tau, q0, g0, qg_sib, kv_in[gi], tau_rows, offsets
        )
        tau_rows.append(tau_here)
        owns.append((att_own, dq_own))
        sibs.append(sib)
        grads.append(kv_grads)
        if gi == 0:
            grads[0] = lax.all_to_all(kv_grads, "ctx", 0, 0)
    grads, sibs, tau_last = lax.optimization_barrier((grads, sibs, tau_rows[1]))
    grads[1] = lax.all_to_all(grads[1], "ctx", 0, 0)
    sibs = lax.optimization_barrier([lax.ppermute(sib, "ctx", swap) for sib in sibs])
    att_parts, dq_parts = (
        [(own[which], sib[which]) for own, sib in zip(owns, sibs)] for which in range(2)
    )

    def by_group(parts):
        return jnp.concatenate(
            [jnp.where(core == c // 2, parts[c % 2][0], parts[c % 2][1]) for c in range(4)], axis=1
        )

    attended = by_group(att_parts)[None]
    query_grad = by_group(dq_parts)[None]

    def summed(which):
        cols = []
        for c in range(4):
            total = None
            for src in range(c // 2, ctx, 2):
                term = grads[c % 2][src].reshape(local_blocks, 2, BLOCK, HD)[:, which]
                term = term.astype(jnp.float32)
                total = term if total is None else total + term
            cols.append(total.reshape(tokens, HD).astype(jnp.bfloat16))
        return jnp.concatenate(cols, axis=1)[None]

    key_grad, value_grad = summed(0), summed(1)
    scale_total = total_over(total_over(tau_last[:1], "ctx"), "batch")[0, :HEADS]
    tau_grad = scale_total / math.sqrt(lax.axis_size("batch") * ctx * tokens)
    return (attended, query_grad, key_grad, value_grad, tau_grad)


def solution(mesh):
    rows = P("batch", "ctx", None)
    return jax.shard_map(
        body,
        mesh=mesh,
        in_specs=(rows, rows, rows, P(), rows, P()),
        out_specs=(rows, rows, rows, rows, P()),
        check_vma=False,
    )
```

```python
import functools
import math

import jax
import jax.numpy as jnp
from jax import lax
from jax.experimental import pallas as pl
from jax.experimental.pallas import tpu as pltpu
from jax.sharding import PartitionSpec as P

HEADS = 16
KV_HEADS = 4
HD = 128
BLOCK = 128
QPG = HEADS // KV_HEADS
CHUNK = 4
ROWS = QPG * BLOCK
TAIL = 8
VMEM_BYTES = 63 * 2**20
STRIDES = (2, 3)
LOG2E = math.log2(math.e)
NEVER = -1e30


def distinct_offsets(block_count, listed_count):
    tables = []
    for stride in STRIDES:
        steps = range(1, (listed_count - 3) // 2 + 1)
        listed = [-1, 0, 1] + [stride * m for m in steps] + [-stride * m for m in steps]
        times = {}
        for o in listed:
            times[o % block_count] = times.get(o % block_count, 0) + 1
        tables.append(sorted(times.items()))
    most = max(len(t) for t in tables)
    return [t + [(0, 0)] * (most - len(t)) for t in tables]


def nt(a, b):
    return jnp.dot(a, b, preferred_element_type=jnp.float32)


def group_kernel(gi, devices, local_blocks, listed, offsets, *refs):
    place, strides, taus = refs[:3]
    inputs, rest = refs[3 : 6 + gi], refs[6 + gi :]
    rows_in, turned_in, kv_in = inputs[:3]
    tau_out, kv_out, o_out, ds_out = rest[:4]
    vt_s, dk_s, dv_s, s_s, e_s, ds_s, sems = rest[4:]
    blocks = devices * local_blocks
    me = place[0]
    group = 2 * (me % 2) + gi
    units = 2 * local_blocks

    chunks = [range(c, min(c + CHUNK, listed)) for c in range(0, listed, CHUNK)]
    scale = jnp.concatenate(
        [jnp.full((1, BLOCK), taus[group * QPG + h], jnp.float32) for h in range(QPG)], axis=1
    ) / math.sqrt(HD)
    factor = scale * LOG2E

    def rows_of(c):
        return slice(c[0] * BLOCK, (c[-1] + 1) * BLOCK)

    def in_rows(x):
        return x.reshape(-1, 8, ROWS)

    tau_totals = []

    def part(n):
        s_n, e_n = s_s.at[n], e_s.at[n]
        query_block, ids, bias = listing(offsets, strides, me, group, n, local_blocks, blocks)

        def taken(which, c):
            return jnp.concatenate([kv_in[ids[j], which] for j in c], axis=0)

        def picked(ref, c, axis):
            return jnp.concatenate([ref[ids[j]] for j in c], axis=axis)

        def add_blocks(ref, c, x):
            for n, j in enumerate(c):
                ref[ids[j]] += x[n * BLOCK : (n + 1) * BLOCK, :]

        most = None
        for c in chunks:
            raw = nt(taken(0, c), turned_in[0, n, 0])
            s_n[rows_of(c), :] = raw
            top = jnp.max(in_rows(raw), axis=0)
            most = top if most is None else jnp.maximum(most, top)
            yield
        top_row = jnp.max(most, axis=0, keepdims=True) * factor
        total = jnp.zeros((8, ROWS), jnp.float32)
        for c in chunks:
            for j in c:
                rows = slice(j * BLOCK, (j + 1) * BLOCK)
                e = jnp.exp2(s_n[rows, :] * factor - (top_row - bias[j]))
                e_n[rows, :] = e
                total = total + jnp.sum(in_rows(e), axis=0)
            yield
        inverse = 1.0 / jnp.sum(total, axis=0, keepdims=True)
        o_t = jnp.zeros((HD, ROWS), jnp.float32)
        for c in chunks:
            probs = (e_n[rows_of(c), :] * inverse).astype(jnp.bfloat16)
            o_t = o_t + nt(picked(vt_s, c, 1), probs)
            add_blocks(dv_s, c, nt(probs, rows_in[0, n, 1]))
            yield
        row_dot = jnp.sum(turned_in[0, n, 1].astype(jnp.float32) * o_t, axis=0, keepdims=True)
        o_out[n] = o_t.astype(jnp.bfloat16)
        weight_scale = inverse * scale
        tau_rows = jnp.zeros((8, ROWS), jnp.float32)
        for c in chunks:
            dweights = nt(taken(1, c), turned_in[0, n, 1])
            scaled = e_n[rows_of(c), :] * weight_scale * (dweights - row_dot)
            tau_rows = tau_rows + jnp.sum(in_rows(scaled * s_n[rows_of(c), :]), axis=0)
            low = scaled.astype(jnp.bfloat16)
            ds_s[n, rows_of(c), :] = low
            add_blocks(dk_s, c, nt(low, rows_in[0, n, 0]))
            yield
        tau_totals.append(tau_rows)
        pltpu.make_async_copy(ds_s.at[n], ds_out.at[n], sems.at[n]).start()

    def turned(which, ref):
        turns = 2 * len(chunks)
        for turn in range(turns):
            for b in range(blocks * turn // turns, blocks * (turn + 1) // turns):
                ref[b] = kv_in[b, which].T
            yield

    dk_s[...] = jnp.zeros_like(dk_s)
    dv_s[...] = jnp.zeros_like(dv_s)
    shares = [(0, turned(1, vt_s))]
    shares += [(n * len(chunks), part(n)) for n in range(units)]
    for turn in range((4 + units) * len(chunks)):
        for begin, share in shares:
            if turn >= begin:
                next(share, None)

    lane = lax.broadcasted_iota(jnp.int32, (TAIL, HD), 1)
    sums = inputs[3][...] if gi else jnp.zeros((TAIL, HD), jnp.float32)
    tau_rows = functools.reduce(jnp.add, tau_totals)
    for h in range(QPG):
        head = group * QPG + h
        total = jnp.sum(tau_rows[:, h * BLOCK : (h + 1) * BLOCK])
        sums = sums + jnp.where(lane == head, total / taus[head], 0.0)
    tau_out[...] = sums

    def drain(d, carry):
        for half in range(local_blocks):
            for which, ref in enumerate((dk_s, dv_s)):
                at = (2 * half + which) * BLOCK
                kv_out[d, at : at + BLOCK, :] = ref[d * local_blocks + half].astype(jnp.bfloat16)
        return carry

    lax.fori_loop(0, devices, drain, 0, unroll=2)
    for n in range(units):
        pltpu.make_async_copy(ds_s.at[n], ds_out.at[n], sems.at[n]).wait()


def times_bias(times):
    return math.log2(times) if times else NEVER


def listing(offsets, strides, me, group, n, local_blocks, blocks):
    query_block = (me ^ (n // local_blocks)) * local_blocks + n % local_blocks
    wide = strides[group * blocks + query_block] == STRIDES[1]
    ids, bias = [], []
    for (narrow_off, narrow_times), (wide_off, wide_times) in zip(*offsets):
        ids.append((query_block + jnp.where(wide, wide_off, narrow_off)) % blocks)
        bias.append(
            times_bias(narrow_times)
            if narrow_times == wide_times
            else jnp.where(wide, times_bias(wide_times), times_bias(narrow_times))
        )
    return query_block, ids, bias


def per_head(x):
    return [x[:, h * HD : (h + 1) * HD] for h in range(QPG)]


def once(shape, index=None):
    at = index or (lambda *_: (0,) * len(shape))
    return pl.BlockSpec(shape, at, pipeline_mode=pl.Buffered(1))


def run_group(gi, devices, place, strides, tau, rows, turned, kv_in, tau_in, offsets):
    listed = len(offsets[0])
    units = rows.shape[1]
    local_blocks = units // 2
    blocks = devices * local_blocks
    bf = lambda *shape: jax.ShapeDtypeStruct(shape, jnp.bfloat16)
    keys_wide = listed * BLOCK
    cells = units * ROWS * keys_wide
    small = once((TAIL, HD))
    kv_back = (devices, 2 * local_blocks * BLOCK, HD)
    return pl.pallas_call(
        functools.partial(group_kernel, gi, devices, local_blocks, listed, offsets),
        grid_spec=pltpu.PrefetchScalarGridSpec(
            num_scalar_prefetch=3,
            grid=(1,),
            in_specs=[
                once((1, units, 2, ROWS, HD), lambda *_: (gi, 0, 0, 0, 0)),
                once((1, units, 2, HD, ROWS), lambda *_: (gi, 0, 0, 0, 0)),
                once((blocks, 2, BLOCK, HD)),
            ]
            + [small] * gi,
            out_specs=[small, once(kv_back), once((units, HD, ROWS)), pl.BlockSpec(memory_space=pl.ANY)],
            scratch_shapes=[pltpu.VMEM((blocks, HD, BLOCK), jnp.bfloat16)]
            + [pltpu.VMEM((blocks, BLOCK, HD), jnp.float32)] * 2
            + [pltpu.VMEM((units, keys_wide, ROWS), jnp.float32)] * 2
            + [pltpu.VMEM((units, keys_wide, ROWS), jnp.bfloat16), pltpu.SemaphoreType.DMA((units,))],
        ),
        out_shape=[jax.ShapeDtypeStruct((TAIL, HD), jnp.float32), bf(*kv_back), bf(units, HD, ROWS)]
        + [bf(units, keys_wide, ROWS)],
        compiler_params=pltpu.CompilerParams(
            dimension_semantics=("arbitrary",), vmem_limit_bytes=VMEM_BYTES
        ),
        cost_estimate=pl.CostEstimate(
            flops=10 * HD * cells, bytes_accessed=6 * 2**20, transcendentals=cells
        ),
        name="group_attention",
    )(place, strides, tau, rows, turned, kv_in, *tau_in[:gi])


def turn(place, queries, out_grad, qg_sib):
    tokens = queries.shape[0]
    local_blocks = tokens // BLOCK
    units = 2 * local_blocks
    width = QPG * HD

    def kernel(place, q_own, g_own, q_sib, g_sib, rows, turned):
        own = pl.program_id(1) < local_blocks
        for which, (a, b) in enumerate(((q_own, q_sib), (g_own, g_sib))):
            heads = per_head(jnp.where(own, a[...], b[0]))
            rows[0, 0, which] = jnp.concatenate(heads, axis=0)
            turned[0, 0, which] = jnp.concatenate([x.T for x in heads], axis=1)

    mine = pl.BlockSpec(
        (BLOCK, width), lambda gi, u, p: (jnp.minimum(u, local_blocks - 1), 2 * (p[0] % 2) + gi)
    )

    def theirs(which):
        return pl.BlockSpec(
            (1, BLOCK, width), lambda gi, u, p: (which, jnp.maximum(u - local_blocks, 0), gi)
        )

    shapes = [(2, units, 2, ROWS, HD), (2, units, 2, HD, ROWS)]
    return pl.pallas_call(
        kernel,
        grid_spec=pltpu.PrefetchScalarGridSpec(
            num_scalar_prefetch=1,
            grid=(2, units),
            in_specs=[mine, mine, theirs(0), theirs(1)],
            out_specs=[pl.BlockSpec((1, 1, *x[2:]), lambda gi, u, p: (gi, u, 0, 0, 0)) for x in shapes],
        ),
        out_shape=[jax.ShapeDtypeStruct(x, jnp.bfloat16) for x in shapes],
        compiler_params=pltpu.CompilerParams(vmem_limit_bytes=VMEM_BYTES),
        name="turn_queries",
    )(place, queries, out_grad, qg_sib, qg_sib)


def finish(devices, place, strides, parts, offsets):
    units, keys_wide, _ = parts[0][0].shape
    local_blocks = units // 2
    blocks = devices * local_blocks
    tokens = local_blocks * BLOCK
    last = local_blocks - 1
    wide = 2 * QPG * HD

    def kernel(place, strides, *refs):
        ins, (own_out, sib_out, kt_s) = (refs[:3], refs[3:6]), refs[6:]
        n = pl.program_id(0)
        me = place[0]

        @pl.when(n == 0)
        def _():
            for gi in range(2):
                for b in range(blocks):
                    kt_s[gi, b] = ins[gi][1][b, 0].T

        results = [[], []]
        for gi, (ds, _, o_t) in enumerate(ins):
            _, ids, _ = listing(offsets, strides, me, 2 * (me % 2) + gi, n, local_blocks, blocks)
            dq_t = nt(jnp.concatenate([kt_s[gi, b] for b in ids], axis=1), ds[0])
            results[0] += [x.T for x in per_head(o_t[0])]
            results[1] += [x.T for x in per_head(dq_t.astype(jnp.bfloat16))]
        results = [jnp.concatenate(x, axis=1) for x in results]

        @pl.when(n < local_blocks)
        def _():
            for which in range(2):
                own_out[which] = results[which]

        @pl.when(n >= local_blocks)
        def _():
            for which in range(2):
                sib_out[which] = results[which]

    each = [
        pl.BlockSpec((1, keys_wide, ROWS), lambda n, p, s: (n, 0, 0)),
        pl.BlockSpec((blocks, 1, BLOCK, HD), lambda n, p, s: (0, 0, 0, 0)),
        pl.BlockSpec((1, HD, ROWS), lambda n, p, s: (n, 0, 0)),
    ]
    return pl.pallas_call(
        kernel,
        grid_spec=pltpu.PrefetchScalarGridSpec(
            num_scalar_prefetch=2,
            grid=(units,),
            in_specs=each * 2,
            out_specs=[
                pl.BlockSpec((2, BLOCK, wide), lambda n, p, s: (0, jnp.minimum(n, last), 0)),
                pl.BlockSpec((2, BLOCK, wide), lambda n, p, s: (0, jnp.maximum(n - local_blocks, 0), 0)),
            ],
            scratch_shapes=[pltpu.VMEM((2, blocks, HD, BLOCK), jnp.bfloat16)],
        ),
        out_shape=[jax.ShapeDtypeStruct((2, tokens, wide), jnp.bfloat16)] * 2,
        compiler_params=pltpu.CompilerParams(vmem_limit_bytes=VMEM_BYTES),
        cost_estimate=pl.CostEstimate(flops=2**20, bytes_accessed=2**20, transcendentals=0),
        name="finish_rows",
    )(place, strides, *parts[0], *parts[1])


def partners(x, axis, distances):
    size = lax.axis_size(axis)
    a, b, c = (lax.ppermute(x, axis, [(i, i ^ d) for i in range(size)]) for d in distances)
    return (x + a) + (b + c)


def total_everywhere(x):
    ctx, batch = lax.axis_size("ctx"), lax.axis_size("batch")
    if batch != 4 or ctx not in (8, 32):
        return x, lambda y: lax.psum(y, ("ctx", "batch"))

    def rest(y):
        y = partners(y, "batch", (1, 2, 3))
        step = 2
        while step < ctx:
            y = partners(y, "ctx", (step, 2 * step, 3 * step))
            step *= 4
        return y

    return x + lax.ppermute(x, "ctx", [(i, i ^ 1) for i in range(ctx)]), rest


def spread(gi, devices, keys, values):
    tokens, width = keys.shape
    local_blocks = tokens // BLOCK

    def kernel(k_ref, v_ref, out):
        for parity in range(2):
            cols = slice((2 * parity + gi) * HD, (2 * parity + gi + 1) * HD)
            for half in range(local_blocks):
                rows = slice(half * BLOCK, (half + 1) * BLOCK)
                out[parity, half, 0] = k_ref[rows, cols]
                out[parity, half, 1] = v_ref[rows, cols]

    taken = pl.BlockSpec((tokens, width), lambda d: (0, 0))
    block = (2, local_blocks, 2, BLOCK, HD)
    return pl.pallas_call(
        kernel,
        grid=(devices // 2,),
        in_specs=[taken, taken],
        out_specs=pl.BlockSpec(block, lambda d: (d, 0, 0, 0, 0)),
        out_shape=jax.ShapeDtypeStruct((devices, *block[1:]), jnp.bfloat16),
        compiler_params=pltpu.CompilerParams(vmem_limit_bytes=VMEM_BYTES),
        name="spread_keys_values",
    )(keys, values)


def body(queries, keys, values, tau, out_grad, key_blocks):
    ctx = lax.axis_size("ctx")
    me = lax.axis_index("ctx").astype(jnp.int32)
    core = me % 2
    tokens = queries.shape[1]
    local_blocks = tokens // BLOCK
    block_count = ctx * local_blocks
    listed_count = key_blocks.shape[2]
    offsets = distinct_offsets(block_count, listed_count)
    swap = [(d, d ^ 1) for d in range(ctx)]
    wide = 2 * QPG * HD

    q0, k0, v0, g0 = queries[0], keys[0], values[0], out_grad[0]
    place = me[None]

    def kv_for(gi):
        arrived = lax.all_to_all(spread(gi, ctx, k0, v0), "ctx", 0, 0)
        return arrived.reshape(block_count, 2, BLOCK, HD)

    def theirs(x):
        return lax.dynamic_slice_in_dim(x, (1 - core) * wide, wide, 1)

    kv_in = [kv_for(gi) for gi in range(2)]
    strides = (key_blocks[:, :, 3] - jnp.arange(block_count, dtype=jnp.int32)) % block_count
    rows, strides = lax.optimization_barrier((jnp.stack([theirs(q0), theirs(g0)]), strides.reshape(-1)))
    qg_sib = lax.ppermute(rows, "ctx", swap)

    rows, turned = turn(place, q0, g0, qg_sib)
    grads, tau_rows, parts = [], [], []
    for gi in range(2):
        tau_here, kv_grads, o_t, ds = run_group(
            gi, ctx, place, strides, tau, rows, turned, kv_in[gi], tau_rows, offsets
        )
        tau_rows.append(tau_here)
        parts.append((ds, kv_in[gi], o_t))
        grads.append(kv_grads)
        if gi == 0:
            grads[0] = lax.all_to_all(kv_grads, "ctx", 0, 0)
    grads, parts, tau_last = lax.optimization_barrier((grads, parts, tau_rows[1]))
    grads[1] = lax.all_to_all(grads[1], "ctx", 0, 0)
    tau_pair, over_rest = total_everywhere(tau_last)
    tau_pair, parts, grads[0] = lax.optimization_barrier((tau_pair, parts, grads[0]))
    own, sib = finish(ctx, place, strides, parts, offsets)
    sib = lax.ppermute(sib, "ctx", swap)

    def both(which):
        a = jnp.where(core == 0, own[which], sib[which])
        b = jnp.where(core == 0, sib[which], own[which])
        return jnp.concatenate([a, b], axis=1)[None]

    attended, query_grad = both(0), both(1)

    def summed(which):
        cols = []
        for c in range(4):
            total = None
            for src in range(c // 2, ctx, 2):
                term = grads[c % 2][src].reshape(local_blocks, 2, BLOCK, HD)[:, which]
                term = term.astype(jnp.float32)
                total = term if total is None else total + term
            cols.append(total.reshape(tokens, HD).astype(jnp.bfloat16))
        return jnp.concatenate(cols, axis=1)[None]

    key_grad, value_grad = summed(0), summed(1)
    scale_total = over_rest(tau_pair)[0, :HEADS]
    tau_grad = scale_total / math.sqrt(lax.axis_size("batch") * ctx * tokens)
    return (attended, query_grad, key_grad, value_grad, tau_grad)


def solution(mesh):
    rows = P("batch", "ctx", None)
    return jax.shard_map(
        body,
        mesh=mesh,
        in_specs=(rows, rows, rows, P(), rows, P()),
        out_specs=(rows, rows, rows, rows, P()),
        check_vma=False,
    )
```

```python
import functools
import math

import jax
import jax.numpy as jnp
from jax import lax
from jax.experimental import pallas as pl
from jax.experimental.pallas import tpu as pltpu
from jax.sharding import PartitionSpec as P

HEADS = 16
KV_HEADS = 4
HD = 128
BLOCK = 128
QPG = HEADS // KV_HEADS
CHUNK = 2
ROWS = QPG * BLOCK
TAIL = 8
VMEM_BYTES = 63 * 2**20
STRIDES = (2, 3)
LOG2E = math.log2(math.e)
NEVER = -1e30


def distinct_offsets(block_count, listed_count):
    tables = []
    for stride in STRIDES:
        steps = range(1, (listed_count - 3) // 2 + 1)
        listed = [-1, 0, 1] + [stride * m for m in steps] + [-stride * m for m in steps]
        times = {}
        for o in listed:
            times[o % block_count] = times.get(o % block_count, 0) + 1
        tables.append(sorted(times.items()))
    most = max(len(t) for t in tables)
    return [t + [(0, 0)] * (most - len(t)) for t in tables]


def nt(a, b):
    return jnp.dot(a, b, preferred_element_type=jnp.float32)


def group_kernel(gi, devices, local_blocks, listed, offsets, *refs):
    place, strides, taus = refs[:3]
    inputs, rest = refs[3 : 8 + gi], refs[8 + gi :]
    q_own, q_sib, g_own, g_sib, kv_in = inputs[:5]
    att_own, dq_own, sib_out, tau_out, kv_out = rest[:5]
    kt_s, vt_s, dk_s, dv_s, s_s, e_s, qt_s, gt_s = rest[5:]
    blocks = devices * local_blocks
    me = place[0]
    group = 2 * (me % 2) + gi
    units = 2 * local_blocks

    chunks = [range(c, min(c + CHUNK, listed)) for c in range(0, listed, CHUNK)]
    scale = jnp.concatenate(
        [jnp.full((1, BLOCK), taus[group * QPG + h], jnp.float32) for h in range(QPG)], axis=1
    ) / math.sqrt(HD)
    factor = scale * LOG2E

    def rows_of(c):
        return slice(c[0] * BLOCK, (c[-1] + 1) * BLOCK)

    def per_head(x):
        return [x[:, h * HD : (h + 1) * HD] for h in range(QPG)]

    def in_rows(x):
        return x.reshape(-1, 8, ROWS)

    tau_totals = []

    def part(n):
        s_n, e_n = s_s.at[n], e_s.at[n]
        side, at = n // local_blocks, n % local_blocks
        here = slice(at * BLOCK, (at + 1) * BLOCK)
        query_block = (me ^ side) * local_blocks + at
        wide = strides[group * blocks + query_block] == STRIDES[1]
        ids, bias = [], []
        for (narrow_off, narrow_times), (wide_off, wide_times) in zip(*offsets):
            ids.append((query_block + jnp.where(wide, wide_off, narrow_off)) % blocks)
            bias.append(
                times_bias(narrow_times)
                if narrow_times == wide_times
                else jnp.where(wide, times_bias(wide_times), times_bias(narrow_times))
            )

        def taken(which, c):
            return jnp.concatenate([kv_in[ids[j], which] for j in c], axis=0)

        def picked(ref, c, axis):
            return jnp.concatenate([ref[ids[j]] for j in c], axis=axis)

        def add_blocks(ref, c, x):
            for n, j in enumerate(c):
                ref[ids[j]] += x[n * BLOCK : (n + 1) * BLOCK, :]


        def rows_of_heads(own, sib):
            return jnp.concatenate(per_head(sib[0, here, :] if side else own[here, :]), axis=0)

        for own, sib, ref in ((q_own, q_sib, qt_s), (g_own, g_sib, gt_s)):
            heads = per_head(sib[0, here, :] if side else own[here, :])
            for h, x in enumerate(heads):
                ref[n, :, h * BLOCK : (h + 1) * BLOCK] = x.T
        most = None
        for c in chunks:
            raw = nt(taken(0, c), qt_s[n])
            s_n[rows_of(c), :] = raw
            top = jnp.max(in_rows(raw), axis=0)
            most = top if most is None else jnp.maximum(most, top)
            yield
        top_row = jnp.max(most, axis=0, keepdims=True) * factor
        total = jnp.zeros((8, ROWS), jnp.float32)
        for c in chunks:
            for j in c:
                rows = slice(j * BLOCK, (j + 1) * BLOCK)
                e = jnp.exp2(s_n[rows, :] * factor - (top_row - bias[j]))
                e_n[rows, :] = e
                total = total + jnp.sum(in_rows(e), axis=0)
            yield
        inverse = 1.0 / jnp.sum(total, axis=0, keepdims=True)
        o_t = jnp.zeros((HD, ROWS), jnp.float32)
        for c in chunks:
            probs = (e_n[rows_of(c), :] * inverse).astype(jnp.bfloat16)
            o_t = o_t + nt(picked(vt_s, c, 1), probs)
            add_blocks(dv_s, c, nt(probs, rows_of_heads(g_own, g_sib)))
            yield
        row_dot = jnp.sum(gt_s[n].astype(jnp.float32) * o_t, axis=0, keepdims=True)
        write(side, here, 0, o_t)
        weight_scale = inverse * scale
        tau_rows = jnp.zeros((8, ROWS), jnp.float32)
        dq_t = jnp.zeros((HD, ROWS), jnp.float32)
        for c in chunks:
            dweights = nt(taken(1, c), gt_s[n])
            scaled = e_n[rows_of(c), :] * weight_scale * (dweights - row_dot)
            tau_rows = tau_rows + jnp.sum(in_rows(scaled * s_n[rows_of(c), :]), axis=0)
            low = scaled.astype(jnp.bfloat16)
            dq_t = dq_t + nt(picked(kt_s, c, 1), low)
            add_blocks(dk_s, c, nt(low, rows_of_heads(q_own, q_sib)))
            yield
        tau_totals.append(tau_rows)
        write(side, here, 1, dq_t)

    def write(side, here, which, x_t):
        low = x_t.astype(jnp.bfloat16)
        out = jnp.concatenate([x.T for x in per_head(low)], axis=1)
        if side:
            sib_out[which, here, :] = out
        else:
            (att_own, dq_own)[which][here, :] = out

    def turned(which, ref, wait):
        turns = 2 * len(chunks)
        for turn in range(wait):
            yield
        for turn in range(turns):
            for b in range(blocks * turn // turns, blocks * (turn + 1) // turns):
                ref[b] = kv_in[b, which].T
            yield

    dk_s[...] = jnp.zeros_like(dk_s)
    dv_s[...] = jnp.zeros_like(dv_s)
    shares = [(0, turned(1, vt_s, 0)), (0, turned(0, kt_s, len(chunks)))]
    shares += [(n * len(chunks), part(n)) for n in range(units)]
    for turn in range((4 + units) * len(chunks)):
        for begin, share in shares:
            if turn >= begin:
                next(share, None)

    lane = lax.broadcasted_iota(jnp.int32, (TAIL, HD), 1)
    sums = inputs[5][...] if gi else jnp.zeros((TAIL, HD), jnp.float32)
    tau_rows = functools.reduce(jnp.add, tau_totals)
    for h in range(QPG):
        head = group * QPG + h
        total = jnp.sum(tau_rows[:, h * BLOCK : (h + 1) * BLOCK])
        sums = sums + jnp.where(lane == head, total / taus[head], 0.0)
    tau_out[...] = sums

    def drain(d, carry):
        for half in range(local_blocks):
            for which, ref in enumerate((dk_s, dv_s)):
                at = (2 * half + which) * BLOCK
                kv_out[d, at : at + BLOCK, :] = ref[d * local_blocks + half].astype(jnp.bfloat16)
        return carry

    lax.fori_loop(0, devices, drain, 0, unroll=2)


def times_bias(times):
    return math.log2(times) if times else NEVER


def run_group(gi, devices, place, strides, tau, queries, out_grad, qg_sib, kv_in, tau_in, offsets):
    listed = len(offsets[0])
    tokens = queries.shape[0]
    local_blocks = tokens // BLOCK
    blocks = devices * local_blocks
    width = QPG * HD
    block_own = pl.BlockSpec((tokens, width), lambda u, p, s, t: (0, 2 * (p[0] % 2) + gi), pipeline_mode=pl.Buffered(1))
    qs = pl.BlockSpec((1, tokens, width), lambda u, p, s, t: (0, 0, gi), pipeline_mode=pl.Buffered(1))
    gs = pl.BlockSpec((1, tokens, width), lambda u, p, s, t: (1, 0, gi), pipeline_mode=pl.Buffered(1))
    out_own = pl.BlockSpec((tokens, width), lambda u, p, s, t: (0, 0), pipeline_mode=pl.Buffered(1))
    out_sib = pl.BlockSpec((2, tokens, width), lambda u, p, s, t: (0, 0, 0), pipeline_mode=pl.Buffered(1))
    kv_all = pl.BlockSpec((blocks, 2, BLOCK, HD), lambda u, p, s, t: (0, 0, 0, 0), pipeline_mode=pl.Buffered(1))
    kv_back = pl.BlockSpec((devices, 2 * tokens, HD), lambda u, p, s, t: (0, 0, 0), pipeline_mode=pl.Buffered(1))
    small = pl.BlockSpec((TAIL, HD), lambda u, p, s, t: (0, 0), pipeline_mode=pl.Buffered(1))
    bf = lambda *shape: jax.ShapeDtypeStruct(shape, jnp.bfloat16)
    keys_wide = listed * BLOCK
    cells = 2 * local_blocks * ROWS * keys_wide
    return pl.pallas_call(
        functools.partial(group_kernel, gi, devices, local_blocks, listed, offsets),
        grid_spec=pltpu.PrefetchScalarGridSpec(
            num_scalar_prefetch=3,
            grid=(1,),
            in_specs=[block_own, qs, block_own, gs, kv_all] + [small] * gi,
            out_specs=[out_own, out_own, out_sib, small, kv_back],
            scratch_shapes=[pltpu.VMEM((blocks, HD, BLOCK), jnp.bfloat16)] * 2
            + [pltpu.VMEM((blocks, BLOCK, HD), jnp.float32)] * 2
            + [pltpu.VMEM((2 * local_blocks, keys_wide, ROWS), jnp.float32)] * 2
            + [pltpu.VMEM((2 * local_blocks, HD, ROWS), jnp.bfloat16)] * 2,
        ),
        out_shape=[bf(tokens, width), bf(tokens, width), bf(2, tokens, width)]
        + [jax.ShapeDtypeStruct((TAIL, HD), jnp.float32), bf(devices, 2 * tokens, HD)],
        compiler_params=pltpu.CompilerParams(
            dimension_semantics=("arbitrary",), vmem_limit_bytes=VMEM_BYTES
        ),
        cost_estimate=pl.CostEstimate(
            flops=12 * HD * cells, bytes_accessed=6 * 2**20, transcendentals=cells
        ),
        name="group_attention",
    )(place, strides, tau, queries, qg_sib, out_grad, qg_sib, kv_in, *tau_in[:gi])


def partners(x, axis, distances):
    size = lax.axis_size(axis)
    a, b, c = (lax.ppermute(x, axis, [(i, i ^ d) for i in range(size)]) for d in distances)
    return (x + a) + (b + c)


def total_everywhere(x):
    ctx, batch = lax.axis_size("ctx"), lax.axis_size("batch")
    if batch != 4 or ctx not in (8, 32):
        return lax.psum(x, ("ctx", "batch"))
    x = x + lax.ppermute(x, "ctx", [(i, i ^ 1) for i in range(ctx)])
    x = partners(x, "batch", (1, 2, 3))
    step = 2
    while step < ctx:
        x = partners(x, "ctx", (step, 2 * step, 3 * step))
        step *= 4
    return x


def spread(gi, devices, keys, values):
    tokens, width = keys.shape
    local_blocks = tokens // BLOCK

    def kernel(k_ref, v_ref, out):
        for parity in range(2):
            cols = slice((2 * parity + gi) * HD, (2 * parity + gi + 1) * HD)
            for half in range(local_blocks):
                rows = slice(half * BLOCK, (half + 1) * BLOCK)
                out[parity, half, 0] = k_ref[rows, cols]
                out[parity, half, 1] = v_ref[rows, cols]

    taken = pl.BlockSpec((tokens, width), lambda d: (0, 0))
    block = (2, local_blocks, 2, BLOCK, HD)
    return pl.pallas_call(
        kernel,
        grid=(devices // 2,),
        in_specs=[taken, taken],
        out_specs=pl.BlockSpec(block, lambda d: (d, 0, 0, 0, 0)),
        out_shape=jax.ShapeDtypeStruct((devices, *block[1:]), jnp.bfloat16),
        compiler_params=pltpu.CompilerParams(vmem_limit_bytes=VMEM_BYTES),
        name="spread_keys_values",
    )(keys, values)


def body(queries, keys, values, tau, out_grad, key_blocks):
    ctx = lax.axis_size("ctx")
    me = lax.axis_index("ctx").astype(jnp.int32)
    core = me % 2
    tokens = queries.shape[1]
    local_blocks = tokens // BLOCK
    block_count = ctx * local_blocks
    listed_count = key_blocks.shape[2]
    offsets = distinct_offsets(block_count, listed_count)
    swap = [(d, d ^ 1) for d in range(ctx)]
    wide = 2 * QPG * HD

    q0, k0, v0, g0 = queries[0], keys[0], values[0], out_grad[0]
    place = me[None]

    def kv_for(gi):
        arrived = lax.all_to_all(spread(gi, ctx, k0, v0), "ctx", 0, 0)
        return arrived.reshape(block_count, 2, BLOCK, HD)

    def theirs(x):
        return lax.dynamic_slice_in_dim(x, (1 - core) * wide, wide, 1)

    kv_in = [kv_for(gi) for gi in range(2)]
    strides = (key_blocks[:, :, 3] - jnp.arange(block_count, dtype=jnp.int32)) % block_count
    rows, strides = lax.optimization_barrier((jnp.stack([theirs(q0), theirs(g0)]), strides.reshape(-1)))
    qg_sib = lax.ppermute(rows, "ctx", swap)

    sibs, owns, grads, tau_rows = [], [], [], []
    for gi in range(2):
        att_own, dq_own, sib, tau_here, kv_grads = run_group(
            gi, ctx, place, strides, tau, q0, g0, qg_sib, kv_in[gi], tau_rows, offsets
        )
        tau_rows.append(tau_here)
        owns.append((att_own, dq_own))
        sibs.append(sib)
        grads.append(kv_grads)
        if gi == 0:
            grads[0] = lax.all_to_all(kv_grads, "ctx", 0, 0)
    grads, sibs, tau_last = lax.optimization_barrier((grads, sibs, tau_rows[1]))
    grads[1] = lax.all_to_all(grads[1], "ctx", 0, 0)
    sibs, grads[0] = lax.optimization_barrier(
        ([lax.ppermute(sib, "ctx", swap) for sib in sibs], grads[0])
    )
    att_parts, dq_parts = (
        [(own[which], sib[which]) for own, sib in zip(owns, sibs)] for which in range(2)
    )

    def by_group(parts):
        return jnp.concatenate(
            [jnp.where(core == c // 2, parts[c % 2][0], parts[c % 2][1]) for c in range(4)], axis=1
        )

    attended = by_group(att_parts)[None]
    query_grad = by_group(dq_parts)[None]

    def summed(which):
        cols = []
        for c in range(4):
            total = None
            for src in range(c // 2, ctx, 2):
                term = grads[c % 2][src].reshape(local_blocks, 2, BLOCK, HD)[:, which]
                term = term.astype(jnp.float32)
                total = term if total is None else total + term
            cols.append(total.reshape(tokens, HD).astype(jnp.bfloat16))
        return jnp.concatenate(cols, axis=1)[None]

    key_grad, value_grad = summed(0), summed(1)
    scale_total = total_everywhere(tau_last)[0, :HEADS]
    tau_grad = scale_total / math.sqrt(lax.axis_size("batch") * ctx * tokens)
    return (attended, query_grad, key_grad, value_grad, tau_grad)


def solution(mesh):
    rows = P("batch", "ctx", None)
    return jax.shard_map(
        body,
        mesh=mesh,
        in_specs=(rows, rows, rows, P(), rows, P()),
        out_specs=(rows, rows, rows, rows, P()),
        check_vma=False,
    )
```

```python
import functools
import math

import jax
import jax.numpy as jnp
from jax import lax
from jax.experimental import pallas as pl
from jax.experimental.pallas import tpu as pltpu
from jax.sharding import PartitionSpec as P

HEADS = 16
KV_HEADS = 4
HD = 128
BLOCK = 128
QPG = HEADS // KV_HEADS
CHUNK = 6
ROWS = QPG * BLOCK
TAIL = 8
VMEM_BYTES = 63 * 2**20
STRIDES = (2, 3)
LOG2E = math.log2(math.e)
NEVER = -1e30


def distinct_offsets(block_count, listed_count):
    tables = []
    for stride in STRIDES:
        steps = range(1, (listed_count - 3) // 2 + 1)
        listed = [-1, 0, 1] + [stride * m for m in steps] + [-stride * m for m in steps]
        times = {}
        for o in listed:
            times[o % block_count] = times.get(o % block_count, 0) + 1
        tables.append(sorted(times.items()))
    most = max(len(t) for t in tables)
    return [t + [(0, 0)] * (most - len(t)) for t in tables]


def nt(a, b):
    return jnp.dot(a, b, preferred_element_type=jnp.float32)


def group_kernel(gi, devices, local_blocks, listed, offsets, *refs):
    place, strides, taus = refs[:3]
    inputs, rest = refs[3 : 8 + gi], refs[8 + gi :]
    q_own, q_sib, g_own, g_sib, kv_in = inputs[:5]
    att_own, dq_own, sib_out, tau_out, kv_out = rest[:5]
    kt_s, vt_s, dk_s, dv_s, s_s, e_s, qt_s, gt_s = rest[5:]
    blocks = devices * local_blocks
    me = place[0]
    group = 2 * (me % 2) + gi
    units = 2 * local_blocks

    chunks = [range(c, min(c + CHUNK, listed)) for c in range(0, listed, CHUNK)]
    scale = jnp.concatenate(
        [jnp.full((1, BLOCK), taus[group * QPG + h], jnp.float32) for h in range(QPG)], axis=1
    ) / math.sqrt(HD)
    factor = scale * LOG2E

    def rows_of(c):
        return slice(c[0] * BLOCK, (c[-1] + 1) * BLOCK)

    def per_head(x):
        return [x[:, h * HD : (h + 1) * HD] for h in range(QPG)]

    def in_rows(x):
        return x.reshape(-1, 8, ROWS)

    tau_totals = []

    def part(n):
        s_n, e_n = s_s.at[n], e_s.at[n]
        side, at = n // local_blocks, n % local_blocks
        here = slice(at * BLOCK, (at + 1) * BLOCK)
        query_block = (me ^ side) * local_blocks + at
        wide = strides[group * blocks + query_block] == STRIDES[1]
        ids, bias = [], []
        for (narrow_off, narrow_times), (wide_off, wide_times) in zip(*offsets):
            ids.append((query_block + jnp.where(wide, wide_off, narrow_off)) % blocks)
            bias.append(
                times_bias(narrow_times)
                if narrow_times == wide_times
                else jnp.where(wide, times_bias(wide_times), times_bias(narrow_times))
            )

        def taken(which, c):
            return jnp.concatenate([kv_in[ids[j], which] for j in c], axis=0)

        def picked(ref, c, axis):
            return jnp.concatenate([ref[ids[j]] for j in c], axis=axis)

        def add_blocks(ref, c, x):
            for n, j in enumerate(c):
                ref[ids[j]] += x[n * BLOCK : (n + 1) * BLOCK, :]


        def rows_of_heads(own, sib):
            return jnp.concatenate(per_head(sib[0, here, :] if side else own[here, :]), axis=0)

        for own, sib, ref in ((q_own, q_sib, qt_s), (g_own, g_sib, gt_s)):
            heads = per_head(sib[0, here, :] if side else own[here, :])
            for h, x in enumerate(heads):
                ref[n, :, h * BLOCK : (h + 1) * BLOCK] = x.T
        most = None
        for c in chunks:
            raw = nt(taken(0, c), qt_s[n])
            s_n[rows_of(c), :] = raw
            top = jnp.max(in_rows(raw), axis=0)
            most = top if most is None else jnp.maximum(most, top)
            yield
        top_row = jnp.max(most, axis=0, keepdims=True) * factor
        total = jnp.zeros((8, ROWS), jnp.float32)
        for c in chunks:
            for j in c:
                rows = slice(j * BLOCK, (j + 1) * BLOCK)
                e = jnp.exp2(s_n[rows, :] * factor - (top_row - bias[j]))
                e_n[rows, :] = e
                total = total + jnp.sum(in_rows(e), axis=0)
            yield
        inverse = 1.0 / jnp.sum(total, axis=0, keepdims=True)
        o_t = jnp.zeros((HD, ROWS), jnp.float32)
        for c in chunks:
            probs = (e_n[rows_of(c), :] * inverse).astype(jnp.bfloat16)
            o_t = o_t + nt(picked(vt_s, c, 1), probs)
            add_blocks(dv_s, c, nt(probs, rows_of_heads(g_own, g_sib)))
            yield
        row_dot = jnp.sum(gt_s[n].astype(jnp.float32) * o_t, axis=0, keepdims=True)
        write(side, here, 0, o_t)
        weight_scale = inverse * scale
        tau_rows = jnp.zeros((8, ROWS), jnp.float32)
        dq_t = jnp.zeros((HD, ROWS), jnp.float32)
        for c in chunks:
            dweights = nt(taken(1, c), gt_s[n])
            scaled = e_n[rows_of(c), :] * weight_scale * (dweights - row_dot)
            tau_rows = tau_rows + jnp.sum(in_rows(scaled * s_n[rows_of(c), :]), axis=0)
            low = scaled.astype(jnp.bfloat16)
            dq_t = dq_t + nt(picked(kt_s, c, 1), low)
            add_blocks(dk_s, c, nt(low, rows_of_heads(q_own, q_sib)))
            yield
        tau_totals.append(tau_rows)
        write(side, here, 1, dq_t)

    def write(side, here, which, x_t):
        low = x_t.astype(jnp.bfloat16)
        out = jnp.concatenate([x.T for x in per_head(low)], axis=1)
        if side:
            sib_out[which, here, :] = out
        else:
            (att_own, dq_own)[which][here, :] = out

    def turned(which, ref, wait):
        turns = 2 * len(chunks)
        for turn in range(wait):
            yield
        for turn in range(turns):
            for b in range(blocks * turn // turns, blocks * (turn + 1) // turns):
                ref[b] = kv_in[b, which].T
            yield

    dk_s[...] = jnp.zeros_like(dk_s)
    dv_s[...] = jnp.zeros_like(dv_s)
    shares = [(0, turned(1, vt_s, 0)), (0, turned(0, kt_s, len(chunks)))]
    shares += [(n * len(chunks), part(n)) for n in range(units)]
    for turn in range((4 + units) * len(chunks)):
        for begin, share in shares:
            if turn >= begin:
                next(share, None)

    lane = lax.broadcasted_iota(jnp.int32, (TAIL, HD), 1)
    sums = inputs[5][...] if gi else jnp.zeros((TAIL, HD), jnp.float32)
    tau_rows = functools.reduce(jnp.add, tau_totals)
    for h in range(QPG):
        head = group * QPG + h
        total = jnp.sum(tau_rows[:, h * BLOCK : (h + 1) * BLOCK])
        sums = sums + jnp.where(lane == head, total / taus[head], 0.0)
    tau_out[...] = sums

    def drain(d, carry):
        for half in range(local_blocks):
            for which, ref in enumerate((dk_s, dv_s)):
                at = (2 * half + which) * BLOCK
                kv_out[d, at : at + BLOCK, :] = ref[d * local_blocks + half].astype(jnp.bfloat16)
        return carry

    lax.fori_loop(0, devices, drain, 0, unroll=2)


def times_bias(times):
    return math.log2(times) if times else NEVER


def run_group(gi, devices, place, strides, tau, queries, out_grad, qg_sib, kv_in, tau_in, offsets):
    listed = len(offsets[0])
    tokens = queries.shape[0]
    local_blocks = tokens // BLOCK
    blocks = devices * local_blocks
    width = QPG * HD
    block_own = pl.BlockSpec((tokens, width), lambda u, p, s, t: (0, 2 * (p[0] % 2) + gi), pipeline_mode=pl.Buffered(1))
    qs = pl.BlockSpec((1, tokens, width), lambda u, p, s, t: (0, 0, gi), pipeline_mode=pl.Buffered(1))
    gs = pl.BlockSpec((1, tokens, width), lambda u, p, s, t: (1, 0, gi), pipeline_mode=pl.Buffered(1))
    out_own = pl.BlockSpec((tokens, width), lambda u, p, s, t: (0, 0), pipeline_mode=pl.Buffered(1))
    out_sib = pl.BlockSpec((2, tokens, width), lambda u, p, s, t: (0, 0, 0), pipeline_mode=pl.Buffered(1))
    kv_all = pl.BlockSpec((blocks, 2, BLOCK, HD), lambda u, p, s, t: (0, 0, 0, 0), pipeline_mode=pl.Buffered(1))
    kv_back = pl.BlockSpec((devices, 2 * tokens, HD), lambda u, p, s, t: (0, 0, 0), pipeline_mode=pl.Buffered(1))
    small = pl.BlockSpec((TAIL, HD), lambda u, p, s, t: (0, 0), pipeline_mode=pl.Buffered(1))
    bf = lambda *shape: jax.ShapeDtypeStruct(shape, jnp.bfloat16)
    keys_wide = listed * BLOCK
    cells = 2 * local_blocks * ROWS * keys_wide
    return pl.pallas_call(
        functools.partial(group_kernel, gi, devices, local_blocks, listed, offsets),
        grid_spec=pltpu.PrefetchScalarGridSpec(
            num_scalar_prefetch=3,
            grid=(1,),
            in_specs=[block_own, qs, block_own, gs, kv_all] + [small] * gi,
            out_specs=[out_own, out_own, out_sib, small, kv_back],
            scratch_shapes=[pltpu.VMEM((blocks, HD, BLOCK), jnp.bfloat16)] * 2
            + [pltpu.VMEM((blocks, BLOCK, HD), jnp.float32)] * 2
            + [pltpu.VMEM((2 * local_blocks, keys_wide, ROWS), jnp.float32)] * 2
            + [pltpu.VMEM((2 * local_blocks, HD, ROWS), jnp.bfloat16)] * 2,
        ),
        out_shape=[bf(tokens, width), bf(tokens, width), bf(2, tokens, width)]
        + [jax.ShapeDtypeStruct((TAIL, HD), jnp.float32), bf(devices, 2 * tokens, HD)],
        compiler_params=pltpu.CompilerParams(
            dimension_semantics=("arbitrary",), vmem_limit_bytes=VMEM_BYTES
        ),
        cost_estimate=pl.CostEstimate(
            flops=12 * HD * cells, bytes_accessed=6 * 2**20, transcendentals=cells
        ),
        name="group_attention",
    )(place, strides, tau, queries, qg_sib, out_grad, qg_sib, kv_in, *tau_in[:gi])


def partners(x, axis, distances):
    size = lax.axis_size(axis)
    a, b, c = (lax.ppermute(x, axis, [(i, i ^ d) for i in range(size)]) for d in distances)
    return (x + a) + (b + c)


def total_everywhere(x):
    ctx, batch = lax.axis_size("ctx"), lax.axis_size("batch")
    if batch != 4 or ctx not in (8, 32):
        return lax.psum(x, ("ctx", "batch"))
    x = x + lax.ppermute(x, "ctx", [(i, i ^ 1) for i in range(ctx)])
    x = partners(x, "batch", (1, 2, 3))
    step = 2
    while step < ctx:
        x = partners(x, "ctx", (step, 2 * step, 3 * step))
        step *= 4
    return x


def spread(gi, devices, keys, values):
    tokens = keys.shape[0]
    local_blocks = tokens // BLOCK

    def kernel(*refs):
        columns, out, piece, sems = refs[:4], refs[4], refs[5], refs[6]
        for n, ref in enumerate(columns):
            for half in range(local_blocks):
                piece[n % 2, half, n // 2] = ref[half * BLOCK : (half + 1) * BLOCK, :]
        copies = [
            pltpu.make_async_copy(piece, out.at[pl.ds(2 * d, 2)], sems.at[d]) for d in range(devices // 2)
        ]
        for copy in copies:
            copy.start()
        for copy in copies:
            copy.wait()

    def column(group):
        return pl.BlockSpec((tokens, HD), lambda n: (0, group), pipeline_mode=pl.Buffered(1))

    block = (2, local_blocks, 2, BLOCK, HD)
    return pl.pallas_call(
        kernel,
        grid=(1,),
        in_specs=[column(gi), column(2 + gi)] * 2,
        out_specs=pl.BlockSpec(memory_space=pl.ANY),
        out_shape=jax.ShapeDtypeStruct((devices, *block[1:]), jnp.bfloat16),
        scratch_shapes=[pltpu.VMEM(block, jnp.bfloat16), pltpu.SemaphoreType.DMA((devices // 2,))],
        compiler_params=pltpu.CompilerParams(vmem_limit_bytes=VMEM_BYTES),
        name="spread_keys_values",
    )(keys, keys, values, values)


def body(queries, keys, values, tau, out_grad, key_blocks):
    ctx = lax.axis_size("ctx")
    me = lax.axis_index("ctx").astype(jnp.int32)
    core = me % 2
    tokens = queries.shape[1]
    local_blocks = tokens // BLOCK
    block_count = ctx * local_blocks
    listed_count = key_blocks.shape[2]
    offsets = distinct_offsets(block_count, listed_count)
    swap = [(d, d ^ 1) for d in range(ctx)]
    wide = 2 * QPG * HD

    q0, k0, v0, g0 = queries[0], keys[0], values[0], out_grad[0]
    place = me[None]

    def kv_for(gi):
        arrived = lax.all_to_all(spread(gi, ctx, k0, v0), "ctx", 0, 0)
        return arrived.reshape(block_count, 2, BLOCK, HD)

    def theirs(x):
        return lax.dynamic_slice_in_dim(x, (1 - core) * wide, wide, 1)

    kv_in = [kv_for(gi) for gi in range(2)]
    strides = (key_blocks[:, :, 3] - jnp.arange(block_count, dtype=jnp.int32)) % block_count
    rows, strides = lax.optimization_barrier((jnp.stack([theirs(q0), theirs(g0)]), strides.reshape(-1)))
    qg_sib = lax.ppermute(rows, "ctx", swap)

    sibs, owns, grads, tau_rows = [], [], [], []
    for gi in range(2):
        att_own, dq_own, sib, tau_here, kv_grads = run_group(
            gi, ctx, place, strides, tau, q0, g0, qg_sib, kv_in[gi], tau_rows, offsets
        )
        tau_rows.append(tau_here)
        owns.append((att_own, dq_own))
        sibs.append(sib)
        grads.append(kv_grads)
        if gi == 0:
            grads[0] = lax.all_to_all(kv_grads, "ctx", 0, 0)
    grads, sibs, tau_last = lax.optimization_barrier((grads, sibs, tau_rows[1]))
    grads[1] = lax.all_to_all(grads[1], "ctx", 0, 0)
    sibs = lax.optimization_barrier([lax.ppermute(sib, "ctx", swap) for sib in sibs])
    att_parts, dq_parts = (
        [(own[which], sib[which]) for own, sib in zip(owns, sibs)] for which in range(2)
    )

    def by_group(parts):
        return jnp.concatenate(
            [jnp.where(core == c // 2, parts[c % 2][0], parts[c % 2][1]) for c in range(4)], axis=1
        )

    attended = by_group(att_parts)[None]
    query_grad = by_group(dq_parts)[None]

    def summed(which):
        cols = []
        for c in range(4):
            total = None
            for src in range(c // 2, ctx, 2):
                term = grads[c % 2][src].reshape(local_blocks, 2, BLOCK, HD)[:, which]
                term = term.astype(jnp.float32)
                total = term if total is None else total + term
            cols.append(total.reshape(tokens, HD).astype(jnp.bfloat16))
        return jnp.concatenate(cols, axis=1)[None]

    key_grad, value_grad = summed(0), summed(1)
    scale_total = total_everywhere(tau_last)[0, :HEADS]
    tau_grad = scale_total / math.sqrt(lax.axis_size("batch") * ctx * tokens)
    return (attended, query_grad, key_grad, value_grad, tau_grad)


def solution(mesh):
    rows = P("batch", "ctx", None)
    return jax.shard_map(
        body,
        mesh=mesh,
        in_specs=(rows, rows, rows, P(), rows, P()),
        out_specs=(rows, rows, rows, rows, P()),
        check_vma=False,
    )
```

```python
import functools
import math

import jax
import jax.numpy as jnp
from jax import lax
from jax.experimental import pallas as pl
from jax.experimental.pallas import tpu as pltpu
from jax.sharding import PartitionSpec as P

HEADS = 16
KV_HEADS = 4
HD = 128
BLOCK = 128
QPG = HEADS // KV_HEADS
CHUNK = 11
ROWS = QPG * BLOCK
TAIL = 8
VMEM_BYTES = 63 * 2**20
STRIDES = (2, 3)
LOG2E = math.log2(math.e)
NEVER = -1e30


def distinct_offsets(block_count, listed_count):
    tables = []
    for stride in STRIDES:
        steps = range(1, (listed_count - 3) // 2 + 1)
        listed = [-1, 0, 1] + [stride * m for m in steps] + [-stride * m for m in steps]
        times = {}
        for o in listed:
            times[o % block_count] = times.get(o % block_count, 0) + 1
        tables.append(sorted(times.items()))
    most = max(len(t) for t in tables)
    return [t + [(0, 0)] * (most - len(t)) for t in tables]


def nt(a, b):
    return jnp.dot(a, b, preferred_element_type=jnp.float32)


def group_kernel(gi, devices, local_blocks, listed, offsets, *refs):
    place, strides, taus = refs[:3]
    inputs, rest = refs[3 : 8 + gi], refs[8 + gi :]
    q_own, q_sib, g_own, g_sib, kv_in = inputs[:5]
    att_own, dq_own, sib_out, tau_out, kv_out = rest[:5]
    kt_s, vt_s, dk_s, dv_s, s_s, e_s, qt_s, gt_s = rest[5:]
    blocks = devices * local_blocks
    me = place[0]
    group = 2 * (me % 2) + gi
    units = 2 * local_blocks

    chunks = [range(c, min(c + CHUNK, listed)) for c in range(0, listed, CHUNK)]
    scale = jnp.concatenate(
        [jnp.full((1, BLOCK), taus[group * QPG + h], jnp.float32) for h in range(QPG)], axis=1
    ) / math.sqrt(HD)
    factor = scale * LOG2E

    def rows_of(c):
        return slice(c[0] * BLOCK, (c[-1] + 1) * BLOCK)

    def per_head(x):
        return [x[:, h * HD : (h + 1) * HD] for h in range(QPG)]

    def in_rows(x):
        return x.reshape(-1, 8, ROWS)

    tau_totals = []

    def part(n):
        s_n, e_n = s_s.at[n], e_s.at[n]
        side, at = n // local_blocks, n % local_blocks
        here = slice(at * BLOCK, (at + 1) * BLOCK)
        query_block = (me ^ side) * local_blocks + at
        wide = strides[group * blocks + query_block] == STRIDES[1]
        ids, bias = [], []
        for (narrow_off, narrow_times), (wide_off, wide_times) in zip(*offsets):
            ids.append((query_block + jnp.where(wide, wide_off, narrow_off)) % blocks)
            bias.append(
                times_bias(narrow_times)
                if narrow_times == wide_times
                else jnp.where(wide, times_bias(wide_times), times_bias(narrow_times))
            )

        def taken(which, c):
            return jnp.concatenate([kv_in[ids[j], which] for j in c], axis=0)

        def picked(ref, c, axis):
            return jnp.concatenate([ref[ids[j]] for j in c], axis=axis)

        def add_blocks(ref, c, x):
            for n, j in enumerate(c):
                ref[ids[j]] += x[n * BLOCK : (n + 1) * BLOCK, :]


        def rows_of_heads(own, sib):
            return jnp.concatenate(per_head(sib[0, here, :] if side else own[here, :]), axis=0)

        for own, sib, ref in ((q_own, q_sib, qt_s), (g_own, g_sib, gt_s)):
            heads = per_head(sib[0, here, :] if side else own[here, :])
            for h, x in enumerate(heads):
                ref[n, :, h * BLOCK : (h + 1) * BLOCK] = x.T
        most = None
        for c in chunks:
            raw = nt(taken(0, c), qt_s[n])
            s_n[rows_of(c), :] = raw
            top = jnp.max(in_rows(raw), axis=0)
            most = top if most is None else jnp.maximum(most, top)
            yield
        top_row = jnp.max(most, axis=0, keepdims=True) * factor
        total = jnp.zeros((8, ROWS), jnp.float32)
        for c in chunks:
            for j in c:
                rows = slice(j * BLOCK, (j + 1) * BLOCK)
                e = jnp.exp2(s_n[rows, :] * factor - (top_row - bias[j]))
                e_n[rows, :] = e
                total = total + jnp.sum(in_rows(e), axis=0)
            yield
        inverse = 1.0 / jnp.sum(total, axis=0, keepdims=True)
        o_t = jnp.zeros((HD, ROWS), jnp.float32)
        for c in chunks:
            probs = (e_n[rows_of(c), :] * inverse).astype(jnp.bfloat16)
            o_t = o_t + nt(picked(vt_s, c, 1), probs)
            add_blocks(dv_s, c, nt(probs, rows_of_heads(g_own, g_sib)))
            yield
        row_dot = jnp.sum(gt_s[n].astype(jnp.float32) * o_t, axis=0, keepdims=True)
        write(side, here, 0, o_t)
        weight_scale = inverse * scale
        tau_rows = jnp.zeros((8, ROWS), jnp.float32)
        dq_t = jnp.zeros((HD, ROWS), jnp.float32)
        for c in chunks:
            dweights = nt(taken(1, c), gt_s[n])
            scaled = e_n[rows_of(c), :] * weight_scale * (dweights - row_dot)
            tau_rows = tau_rows + jnp.sum(in_rows(scaled * s_n[rows_of(c), :]), axis=0)
            low = scaled.astype(jnp.bfloat16)
            dq_t = dq_t + nt(picked(kt_s, c, 1), low)
            add_blocks(dk_s, c, nt(low, rows_of_heads(q_own, q_sib)))
            yield
        tau_totals.append(tau_rows)
        write(side, here, 1, dq_t)

    def write(side, here, which, x_t):
        low = x_t.astype(jnp.bfloat16)
        out = jnp.concatenate([x.T for x in per_head(low)], axis=1)
        if side:
            sib_out[which, here, :] = out
        else:
            (att_own, dq_own)[which][here, :] = out

    def turned(which, ref, wait):
        turns = 2 * len(chunks)
        for turn in range(wait):
            yield
        for turn in range(turns):
            for b in range(blocks * turn // turns, blocks * (turn + 1) // turns):
                ref[b] = kv_in[b, which].T
            yield

    dk_s[...] = jnp.zeros_like(dk_s)
    dv_s[...] = jnp.zeros_like(dv_s)
    shares = [(0, turned(1, vt_s, 0)), (0, turned(0, kt_s, len(chunks)))]
    shares += [(n * len(chunks), part(n)) for n in range(units)]
    for turn in range((4 + units) * len(chunks)):
        for begin, share in shares:
            if turn >= begin:
                next(share, None)

    lane = lax.broadcasted_iota(jnp.int32, (TAIL, HD), 1)
    sums = inputs[5][...] if gi else jnp.zeros((TAIL, HD), jnp.float32)
    tau_rows = functools.reduce(jnp.add, tau_totals)
    for h in range(QPG):
        head = group * QPG + h
        total = jnp.sum(tau_rows[:, h * BLOCK : (h + 1) * BLOCK])
        sums = sums + jnp.where(lane == head, total / taus[head], 0.0)
    tau_out[...] = sums

    def drain(d, carry):
        for half in range(local_blocks):
            for which, ref in enumerate((dk_s, dv_s)):
                at = (2 * half + which) * BLOCK
                kv_out[d, at : at + BLOCK, :] = ref[d * local_blocks + half].astype(jnp.bfloat16)
        return carry

    lax.fori_loop(0, devices, drain, 0, unroll=2)


def times_bias(times):
    return math.log2(times) if times else NEVER


def run_group(gi, devices, place, strides, tau, queries, out_grad, qg_sib, kv_in, tau_in, offsets):
    listed = len(offsets[0])
    tokens = queries.shape[0]
    local_blocks = tokens // BLOCK
    blocks = devices * local_blocks
    width = QPG * HD
    block_own = pl.BlockSpec((tokens, width), lambda u, p, s, t: (0, 2 * (p[0] % 2) + gi), pipeline_mode=pl.Buffered(1))
    qs = pl.BlockSpec((1, tokens, width), lambda u, p, s, t: (0, 0, gi), pipeline_mode=pl.Buffered(1))
    gs = pl.BlockSpec((1, tokens, width), lambda u, p, s, t: (1, 0, gi), pipeline_mode=pl.Buffered(1))
    out_own = pl.BlockSpec((tokens, width), lambda u, p, s, t: (0, 0), pipeline_mode=pl.Buffered(1))
    out_sib = pl.BlockSpec((2, tokens, width), lambda u, p, s, t: (0, 0, 0), pipeline_mode=pl.Buffered(1))
    kv_all = pl.BlockSpec((blocks, 2, BLOCK, HD), lambda u, p, s, t: (0, 0, 0, 0), pipeline_mode=pl.Buffered(1))
    kv_back = pl.BlockSpec((devices, 2 * tokens, HD), lambda u, p, s, t: (0, 0, 0), pipeline_mode=pl.Buffered(1))
    small = pl.BlockSpec((TAIL, HD), lambda u, p, s, t: (0, 0), pipeline_mode=pl.Buffered(1))
    bf = lambda *shape: jax.ShapeDtypeStruct(shape, jnp.bfloat16)
    keys_wide = listed * BLOCK
    cells = 2 * local_blocks * ROWS * keys_wide
    return pl.pallas_call(
        functools.partial(group_kernel, gi, devices, local_blocks, listed, offsets),
        grid_spec=pltpu.PrefetchScalarGridSpec(
            num_scalar_prefetch=3,
            grid=(1,),
            in_specs=[block_own, qs, block_own, gs, kv_all] + [small] * gi,
            out_specs=[out_own, out_own, out_sib, small, kv_back],
            scratch_shapes=[pltpu.VMEM((blocks, HD, BLOCK), jnp.bfloat16)] * 2
            + [pltpu.VMEM((blocks, BLOCK, HD), jnp.float32)] * 2
            + [pltpu.VMEM((2 * local_blocks, keys_wide, ROWS), jnp.float32)] * 2
            + [pltpu.VMEM((2 * local_blocks, HD, ROWS), jnp.bfloat16)] * 2,
        ),
        out_shape=[bf(tokens, width), bf(tokens, width), bf(2, tokens, width)]
        + [jax.ShapeDtypeStruct((TAIL, HD), jnp.float32), bf(devices, 2 * tokens, HD)],
        compiler_params=pltpu.CompilerParams(
            dimension_semantics=("arbitrary",), vmem_limit_bytes=VMEM_BYTES
        ),
        cost_estimate=pl.CostEstimate(
            flops=12 * HD * cells, bytes_accessed=6 * 2**20, transcendentals=cells
        ),
        name="group_attention",
    )(place, strides, tau, queries, qg_sib, out_grad, qg_sib, kv_in, *tau_in[:gi])


def partners(x, axis, distances):
    size = lax.axis_size(axis)
    a, b, c = (lax.ppermute(x, axis, [(i, i ^ d) for i in range(size)]) for d in distances)
    return (x + a) + (b + c)


def total_everywhere(x, ready):
    ctx, batch = lax.axis_size("ctx"), lax.axis_size("batch")
    if batch != 4 or ctx not in (8, 32):
        return lax.psum(x, ("ctx", "batch")), ready
    x = x + lax.ppermute(x, "ctx", [(i, i ^ 1) for i in range(ctx)])
    x = partners(x, "batch", (1, 2, 3))
    x, ready = lax.optimization_barrier((x, ready))
    step = 2
    while step < ctx:
        x = partners(x, "ctx", (step, 2 * step, 3 * step))
        step *= 4
    return x, ready


def spread(gi, devices, keys, values):
    tokens = keys.shape[0]
    local_blocks = tokens // BLOCK

    def kernel(*refs):
        columns, out, piece, sems = refs[:4], refs[4], refs[5], refs[6]
        for n, ref in enumerate(columns):
            for half in range(local_blocks):
                piece[n % 2, half, n // 2] = ref[half * BLOCK : (half + 1) * BLOCK, :]
        copies = [
            pltpu.make_async_copy(piece, out.at[pl.ds(2 * d, 2)], sems.at[d]) for d in range(devices // 2)
        ]
        for copy in copies:
            copy.start()
        for copy in copies:
            copy.wait()

    def column(group):
        return pl.BlockSpec((tokens, HD), lambda n: (0, group), pipeline_mode=pl.Buffered(1))

    block = (2, local_blocks, 2, BLOCK, HD)
    return pl.pallas_call(
        kernel,
        grid=(1,),
        in_specs=[column(gi), column(2 + gi)] * 2,
        out_specs=pl.BlockSpec(memory_space=pl.ANY),
        out_shape=jax.ShapeDtypeStruct((devices, *block[1:]), jnp.bfloat16),
        scratch_shapes=[pltpu.VMEM(block, jnp.bfloat16), pltpu.SemaphoreType.DMA((devices // 2,))],
        compiler_params=pltpu.CompilerParams(vmem_limit_bytes=VMEM_BYTES),
        name="spread_keys_values",
    )(keys, keys, values, values)


def body(queries, keys, values, tau, out_grad, key_blocks):
    ctx = lax.axis_size("ctx")
    me = lax.axis_index("ctx").astype(jnp.int32)
    core = me % 2
    tokens = queries.shape[1]
    local_blocks = tokens // BLOCK
    block_count = ctx * local_blocks
    listed_count = key_blocks.shape[2]
    offsets = distinct_offsets(block_count, listed_count)
    swap = [(d, d ^ 1) for d in range(ctx)]
    wide = 2 * QPG * HD

    q0, k0, v0, g0 = queries[0], keys[0], values[0], out_grad[0]
    place = me[None]

    def kv_for(gi):
        arrived = lax.all_to_all(spread(gi, ctx, k0, v0), "ctx", 0, 0)
        return arrived.reshape(block_count, 2, BLOCK, HD)

    def theirs(x):
        return lax.dynamic_slice_in_dim(x, (1 - core) * wide, wide, 1)

    kv_in = [kv_for(gi) for gi in range(2)]
    strides = (key_blocks[:, :, 3] - jnp.arange(block_count, dtype=jnp.int32)) % block_count
    rows, strides = lax.optimization_barrier((jnp.stack([theirs(q0), theirs(g0)]), strides.reshape(-1)))
    qg_sib = lax.ppermute(rows, "ctx", swap)

    sibs, owns, grads, tau_rows = [], [], [], []
    for gi in range(2):
        att_own, dq_own, sib, tau_here, kv_grads = run_group(
            gi, ctx, place, strides, tau, q0, g0, qg_sib, kv_in[gi], tau_rows, offsets
        )
        tau_rows.append(tau_here)
        owns.append((att_own, dq_own))
        sibs.append(sib)
        grads.append(kv_grads)
        if gi == 0:
            grads[0] = lax.all_to_all(kv_grads, "ctx", 0, 0)
    grads, sibs, tau_last = lax.optimization_barrier((grads, sibs, tau_rows[1]))
    grads[1] = lax.all_to_all(grads[1], "ctx", 0, 0)
    sibs, grads[0] = lax.optimization_barrier(
        ([lax.ppermute(sib, "ctx", swap) for sib in sibs], grads[0])
    )
    att_parts, dq_parts = (
        [(own[which], sib[which]) for own, sib in zip(owns, sibs)] for which in range(2)
    )

    def by_group(parts):
        return jnp.concatenate(
            [jnp.where(core == c // 2, parts[c % 2][0], parts[c % 2][1]) for c in range(4)], axis=1
        )

    attended = by_group(att_parts)[None]
    query_grad = by_group(dq_parts)[None]

    def summed(gi):
        columns = []
        for which in range(2):
            for parity in range(2):
                total = None
                for src in range(parity, ctx, 2):
                    term = grads[gi][src].reshape(local_blocks, 2, BLOCK, HD)[:, which]
                    term = term.astype(jnp.float32)
                    total = term if total is None else total + term
                columns.append(total.reshape(tokens, HD).astype(jnp.bfloat16))
        return columns

    scale_total, (attended, query_grad, first) = total_everywhere(
        tau_last, (attended, query_grad, summed(0))
    )
    second = summed(1)
    key_grad, value_grad = (
        jnp.concatenate([first[i], second[i], first[i + 1], second[i + 1]], axis=1)[None]
        for i in (0, 2)
    )
    scale_total = scale_total[0, :HEADS]
    tau_grad = scale_total / math.sqrt(lax.axis_size("batch") * ctx * tokens)
    return (attended, query_grad, key_grad, value_grad, tau_grad)


def solution(mesh):
    rows = P("batch", "ctx", None)
    return jax.shard_map(
        body,
        mesh=mesh,
        in_specs=(rows, rows, rows, P(), rows, P()),
        out_specs=(rows, rows, rows, rows, P()),
        check_vma=False,
    )
```

```python
import functools
import math

import jax
import jax.numpy as jnp
from jax import lax
from jax.experimental import pallas as pl
from jax.experimental.pallas import tpu as pltpu
from jax.sharding import PartitionSpec as P

HEADS = 16
KV_HEADS = 4
HD = 128
BLOCK = 128
QPG = HEADS // KV_HEADS
CHUNK = 6
ROWS = QPG * BLOCK
TAIL = 8
VMEM_BYTES = 63 * 2**20
STRIDES = (2, 3)
LOG2E = math.log2(math.e)
NEVER = -1e30


def distinct_offsets(block_count, listed_count):
    tables = []
    for stride in STRIDES:
        steps = range(1, (listed_count - 3) // 2 + 1)
        listed = [-1, 0, 1] + [stride * m for m in steps] + [-stride * m for m in steps]
        times = {}
        for o in listed:
            times[o % block_count] = times.get(o % block_count, 0) + 1
        tables.append(sorted(times.items()))
    most = max(len(t) for t in tables)
    return [t + [(0, 0)] * (most - len(t)) for t in tables]


def nt(a, b):
    return jnp.dot(a, b, preferred_element_type=jnp.float32)


def group_kernel(gi, devices, local_blocks, listed, offsets, *refs):
    place, strides, taus = refs[:3]
    inputs, rest = refs[3 : 8 + gi], refs[8 + gi :]
    q_own, q_sib, g_own, g_sib, kv_in = inputs[:5]
    att_own, dq_own, sib_out, tau_out, kv_out = rest[:5]
    kt_s, vt_s, dk_s, dv_s, s_s, e_s, qt_s, gt_s = rest[5:]
    blocks = devices * local_blocks
    me = place[0]
    group = 2 * (me % 2) + gi
    units = 2 * local_blocks

    chunks = [range(c, min(c + CHUNK, listed)) for c in range(0, listed, CHUNK)]
    scale = jnp.concatenate(
        [jnp.full((1, BLOCK), taus[group * QPG + h], jnp.float32) for h in range(QPG)], axis=1
    ) / math.sqrt(HD)
    factor = scale * LOG2E

    def rows_of(c):
        return slice(c[0] * BLOCK, (c[-1] + 1) * BLOCK)

    def per_head(x):
        return [x[:, h * HD : (h + 1) * HD] for h in range(QPG)]

    def in_rows(x):
        return x.reshape(-1, 8, ROWS)

    tau_totals = []

    def part(n):
        s_n, e_n = s_s.at[n], e_s.at[n]
        side, at = n // local_blocks, n % local_blocks
        here = slice(at * BLOCK, (at + 1) * BLOCK)
        query_block = (me ^ side) * local_blocks + at
        wide = strides[group * blocks + query_block] == STRIDES[1]
        ids, bias = [], []
        for (narrow_off, narrow_times), (wide_off, wide_times) in zip(*offsets):
            ids.append((query_block + jnp.where(wide, wide_off, narrow_off)) % blocks)
            bias.append(
                times_bias(narrow_times)
                if narrow_times == wide_times
                else jnp.where(wide, times_bias(wide_times), times_bias(narrow_times))
            )

        def taken(which, c):
            return jnp.concatenate([kv_in[ids[j], which] for j in c], axis=0)

        def picked(ref, c, axis):
            return jnp.concatenate([ref[ids[j]] for j in c], axis=axis)

        def add_blocks(ref, c, x):
            for n, j in enumerate(c):
                ref[ids[j]] += x[n * BLOCK : (n + 1) * BLOCK, :]


        def rows_of_heads(own, sib):
            return jnp.concatenate(per_head(sib[0, here, :] if side else own[here, :]), axis=0)

        for own, sib, ref in ((q_own, q_sib, qt_s), (g_own, g_sib, gt_s)):
            heads = per_head(sib[0, here, :] if side else own[here, :])
            for h, x in enumerate(heads):
                ref[n, :, h * BLOCK : (h + 1) * BLOCK] = x.T
        most = None
        for c in chunks:
            raw = nt(taken(0, c), qt_s[n])
            s_n[rows_of(c), :] = raw
            top = jnp.max(in_rows(raw), axis=0)
            most = top if most is None else jnp.maximum(most, top)
            yield
        top_row = jnp.max(most, axis=0, keepdims=True) * factor
        total = jnp.zeros((8, ROWS), jnp.float32)
        for c in chunks:
            for j in c:
                rows = slice(j * BLOCK, (j + 1) * BLOCK)
                e = jnp.exp2(s_n[rows, :] * factor - (top_row - bias[j]))
                e_n[rows, :] = e
                total = total + jnp.sum(in_rows(e), axis=0)
            yield
        inverse = 1.0 / jnp.sum(total, axis=0, keepdims=True)
        o_t = jnp.zeros((HD, ROWS), jnp.float32)
        for c in chunks:
            probs = (e_n[rows_of(c), :] * inverse).astype(jnp.bfloat16)
            o_t = o_t + nt(picked(vt_s, c, 1), probs)
            add_blocks(dv_s, c, nt(probs, rows_of_heads(g_own, g_sib)))
            yield
        row_dot = jnp.sum(gt_s[n].astype(jnp.float32) * o_t, axis=0, keepdims=True)
        write(side, here, 0, o_t)
        weight_scale = inverse * scale
        tau_rows = jnp.zeros((8, ROWS), jnp.float32)
        dq_t = jnp.zeros((HD, ROWS), jnp.float32)
        for c in chunks:
            dweights = nt(taken(1, c), gt_s[n])
            scaled = e_n[rows_of(c), :] * weight_scale * (dweights - row_dot)
            tau_rows = tau_rows + jnp.sum(in_rows(scaled * s_n[rows_of(c), :]), axis=0)
            low = scaled.astype(jnp.bfloat16)
            dq_t = dq_t + nt(picked(kt_s, c, 1), low)
            add_blocks(dk_s, c, nt(low, rows_of_heads(q_own, q_sib)))
            yield
        tau_totals.append(tau_rows)
        write(side, here, 1, dq_t)

    def write(side, here, which, x_t):
        low = x_t.astype(jnp.bfloat16)
        out = jnp.concatenate([x.T for x in per_head(low)], axis=1)
        if side:
            sib_out[which, here, :] = out
        else:
            (att_own, dq_own)[which][here, :] = out

    def turned(which, ref, wait):
        turns = 2 * len(chunks)
        for turn in range(wait):
            yield
        for turn in range(turns):
            for b in range(blocks * turn // turns, blocks * (turn + 1) // turns):
                ref[b] = kv_in[b, which].T
            yield

    dk_s[...] = jnp.zeros_like(dk_s)
    dv_s[...] = jnp.zeros_like(dv_s)
    shares = [(0, turned(1, vt_s, 0)), (0, turned(0, kt_s, len(chunks)))]
    shares += [(n * len(chunks), part(n)) for n in range(units)]
    for turn in range((4 + units) * len(chunks)):
        for begin, share in shares:
            if turn >= begin:
                next(share, None)

    lane = lax.broadcasted_iota(jnp.int32, (TAIL, HD), 1)
    sums = inputs[5][...] if gi else jnp.zeros((TAIL, HD), jnp.float32)
    tau_rows = functools.reduce(jnp.add, tau_totals)
    for h in range(QPG):
        head = group * QPG + h
        total = jnp.sum(tau_rows[:, h * BLOCK : (h + 1) * BLOCK])
        sums = sums + jnp.where(lane == head, total / taus[head], 0.0)
    tau_out[...] = sums

    def drain(d, carry):
        for half in range(local_blocks):
            for which, ref in enumerate((dk_s, dv_s)):
                at = (2 * half + which) * BLOCK
                kv_out[d, at : at + BLOCK, :] = ref[d * local_blocks + half].astype(jnp.bfloat16)
        return carry

    lax.fori_loop(0, devices, drain, 0, unroll=2)


def times_bias(times):
    return math.log2(times) if times else NEVER


def run_group(gi, devices, place, strides, tau, queries, out_grad, qg_sib, kv_in, tau_in, offsets):
    listed = len(offsets[0])
    tokens = queries.shape[0]
    local_blocks = tokens // BLOCK
    blocks = devices * local_blocks
    width = QPG * HD
    block_own = pl.BlockSpec((tokens, width), lambda u, p, s, t: (0, 2 * (p[0] % 2) + gi), pipeline_mode=pl.Buffered(1))
    qs = pl.BlockSpec((1, tokens, width), lambda u, p, s, t: (0, 0, gi), pipeline_mode=pl.Buffered(1))
    gs = pl.BlockSpec((1, tokens, width), lambda u, p, s, t: (1, 0, gi), pipeline_mode=pl.Buffered(1))
    out_own = pl.BlockSpec((tokens, width), lambda u, p, s, t: (0, 0), pipeline_mode=pl.Buffered(1))
    out_sib = pl.BlockSpec((2, tokens, width), lambda u, p, s, t: (0, 0, 0), pipeline_mode=pl.Buffered(1))
    kv_all = pl.BlockSpec((blocks, 2, BLOCK, HD), lambda u, p, s, t: (0, 0, 0, 0), pipeline_mode=pl.Buffered(1))
    kv_back = pl.BlockSpec((devices, 2 * tokens, HD), lambda u, p, s, t: (0, 0, 0), pipeline_mode=pl.Buffered(1))
    small = pl.BlockSpec((TAIL, HD), lambda u, p, s, t: (0, 0), pipeline_mode=pl.Buffered(1))
    bf = lambda *shape: jax.ShapeDtypeStruct(shape, jnp.bfloat16)
    keys_wide = listed * BLOCK
    cells = 2 * local_blocks * ROWS * keys_wide
    return pl.pallas_call(
        functools.partial(group_kernel, gi, devices, local_blocks, listed, offsets),
        grid_spec=pltpu.PrefetchScalarGridSpec(
            num_scalar_prefetch=3,
            grid=(1,),
            in_specs=[block_own, qs, block_own, gs, kv_all] + [small] * gi,
            out_specs=[out_own, out_own, out_sib, small, kv_back],
            scratch_shapes=[pltpu.VMEM((blocks, HD, BLOCK), jnp.bfloat16)] * 2
            + [pltpu.VMEM((blocks, BLOCK, HD), jnp.float32)] * 2
            + [pltpu.VMEM((2 * local_blocks, keys_wide, ROWS), jnp.float32)] * 2
            + [pltpu.VMEM((2 * local_blocks, HD, ROWS), jnp.bfloat16)] * 2,
        ),
        out_shape=[bf(tokens, width), bf(tokens, width), bf(2, tokens, width)]
        + [jax.ShapeDtypeStruct((TAIL, HD), jnp.float32), bf(devices, 2 * tokens, HD)],
        compiler_params=pltpu.CompilerParams(
            dimension_semantics=("arbitrary",), vmem_limit_bytes=VMEM_BYTES
        ),
        cost_estimate=pl.CostEstimate(
            flops=12 * HD * cells, bytes_accessed=6 * 2**20, transcendentals=cells
        ),
        name="group_attention",
    )(place, strides, tau, queries, qg_sib, out_grad, qg_sib, kv_in, *tau_in[:gi])


def partners(x, axis, distances):
    size = lax.axis_size(axis)
    a, b, c = (lax.ppermute(x, axis, [(i, i ^ d) for i in range(size)]) for d in distances)
    return (x + a) + (b + c)


def total_everywhere(x, ready):
    ctx, batch = lax.axis_size("ctx"), lax.axis_size("batch")
    if batch != 4 or ctx not in (8, 32):
        return lax.psum(x, ("ctx", "batch")), ready
    x = x + lax.ppermute(x, "ctx", [(i, i ^ 1) for i in range(ctx)])
    x = partners(x, "batch", (1, 2, 3))
    x, ready = lax.optimization_barrier((x, ready))
    step = 2
    while step < ctx:
        x = partners(x, "ctx", (step, 2 * step, 3 * step))
        step *= 4
    return x, ready


def spread(gi, devices, keys, values):
    tokens = keys.shape[0]
    local_blocks = tokens // BLOCK

    def kernel(*refs):
        columns, out, piece, sems = refs[:4], refs[4], refs[5], refs[6]
        for n, ref in enumerate(columns):
            for half in range(local_blocks):
                piece[n % 2, half, n // 2] = ref[half * BLOCK : (half + 1) * BLOCK, :]
        copies = [
            pltpu.make_async_copy(piece, out.at[pl.ds(2 * d, 2)], sems.at[d]) for d in range(devices // 2)
        ]
        for copy in copies:
            copy.start()
        for copy in copies:
            copy.wait()

    def column(group):
        return pl.BlockSpec((tokens, HD), lambda n: (0, group), pipeline_mode=pl.Buffered(1))

    block = (2, local_blocks, 2, BLOCK, HD)
    return pl.pallas_call(
        kernel,
        grid=(1,),
        in_specs=[column(gi), column(2 + gi)] * 2,
        out_specs=pl.BlockSpec(memory_space=pl.ANY),
        out_shape=jax.ShapeDtypeStruct((devices, *block[1:]), jnp.bfloat16),
        scratch_shapes=[pltpu.VMEM(block, jnp.bfloat16), pltpu.SemaphoreType.DMA((devices // 2,))],
        compiler_params=pltpu.CompilerParams(vmem_limit_bytes=VMEM_BYTES),
        name="spread_keys_values",
    )(keys, keys, values, values)


def body(queries, keys, values, tau, out_grad, key_blocks):
    ctx = lax.axis_size("ctx")
    me = lax.axis_index("ctx").astype(jnp.int32)
    core = me % 2
    tokens = queries.shape[1]
    local_blocks = tokens // BLOCK
    block_count = ctx * local_blocks
    listed_count = key_blocks.shape[2]
    offsets = distinct_offsets(block_count, listed_count)
    swap = [(d, d ^ 1) for d in range(ctx)]
    wide = 2 * QPG * HD

    q0, k0, v0, g0 = queries[0], keys[0], values[0], out_grad[0]
    place = me[None]

    def kv_for(gi):
        arrived = lax.all_to_all(spread(gi, ctx, k0, v0), "ctx", 0, 0)
        return arrived.reshape(block_count, 2, BLOCK, HD)

    def theirs(x):
        return lax.dynamic_slice_in_dim(x, (1 - core) * wide, wide, 1)

    kv_in = [kv_for(gi) for gi in range(2)]
    strides = (key_blocks[:, :, 3] - jnp.arange(block_count, dtype=jnp.int32)) % block_count
    rows, strides = lax.optimization_barrier((jnp.stack([theirs(q0), theirs(g0)]), strides.reshape(-1)))
    qg_sib = lax.ppermute(rows, "ctx", swap)

    sibs, owns, grads, tau_rows = [], [], [], []
    for gi in range(2):
        att_own, dq_own, sib, tau_here, kv_grads = run_group(
            gi, ctx, place, strides, tau, q0, g0, qg_sib, kv_in[gi], tau_rows, offsets
        )
        tau_rows.append(tau_here)
        owns.append((att_own, dq_own))
        sibs.append(sib)
        grads.append(kv_grads)
        if gi == 0:
            grads[0] = lax.all_to_all(kv_grads, "ctx", 0, 0)
    grads, sibs, tau_last = lax.optimization_barrier((grads, sibs, tau_rows[1]))
    grads[1] = lax.all_to_all(grads[1], "ctx", 0, 0)
    sibs = lax.optimization_barrier([lax.ppermute(sib, "ctx", swap) for sib in sibs])
    att_parts, dq_parts = (
        [(own[which], sib[which]) for own, sib in zip(owns, sibs)] for which in range(2)
    )

    def by_group(parts):
        return jnp.concatenate(
            [jnp.where(core == c // 2, parts[c % 2][0], parts[c % 2][1]) for c in range(4)], axis=1
        )

    attended = by_group(att_parts)[None]
    query_grad = by_group(dq_parts)[None]

    def summed(gi):
        columns = []
        for which in range(2):
            for parity in range(2):
                total = None
                for src in range(parity, ctx, 2):
                    term = grads[gi][src].reshape(local_blocks, 2, BLOCK, HD)[:, which]
                    term = term.astype(jnp.float32)
                    total = term if total is None else total + term
                columns.append(total.reshape(tokens, HD).astype(jnp.bfloat16))
        return columns

    scale_total, (attended, query_grad) = total_everywhere(tau_last, (attended, query_grad))
    first, second = summed(0), summed(1)
    key_grad, value_grad = (
        jnp.concatenate([first[i], second[i], first[i + 1], second[i + 1]], axis=1)[None]
        for i in (0, 2)
    )
    scale_total = scale_total[0, :HEADS]
    tau_grad = scale_total / math.sqrt(lax.axis_size("batch") * ctx * tokens)
    return (attended, query_grad, key_grad, value_grad, tau_grad)


def solution(mesh):
    rows = P("batch", "ctx", None)
    return jax.shard_map(
        body,
        mesh=mesh,
        in_specs=(rows, rows, rows, P(), rows, P()),
        out_specs=(rows, rows, rows, rows, P()),
        check_vma=False,
    )
```

```python
import functools
import math

import jax
import jax.numpy as jnp
from jax import lax
from jax.experimental import pallas as pl
from jax.experimental.pallas import tpu as pltpu
from jax.sharding import PartitionSpec as P

HEADS = 16
KV_HEADS = 4
HD = 128
BLOCK = 128
QPG = HEADS // KV_HEADS
CHUNK = 6
ROWS = QPG * BLOCK
TAIL = 8
VMEM_BYTES = 63 * 2**20
STRIDES = (2, 3)
LOG2E = math.log2(math.e)
NEVER = -1e30


def distinct_offsets(block_count, listed_count):
    tables = []
    for stride in STRIDES:
        steps = range(1, (listed_count - 3) // 2 + 1)
        listed = [-1, 0, 1] + [stride * m for m in steps] + [-stride * m for m in steps]
        times = {}
        for o in listed:
            times[o % block_count] = times.get(o % block_count, 0) + 1
        tables.append(sorted(times.items()))
    most = max(len(t) for t in tables)
    return [t + [(0, 0)] * (most - len(t)) for t in tables]


def nt(a, b):
    return jnp.dot(a, b, preferred_element_type=jnp.float32)


def group_kernel(gi, devices, local_blocks, listed, offsets, *refs):
    place, strides, taus = refs[:3]
    inputs, rest = refs[3 : 8 + gi], refs[8 + gi :]
    q_own, q_sib, g_own, g_sib, kv_in = inputs[:5]
    att_own, dq_own, sib_out, tau_out, kv_out = rest[:5]
    kt_s, vt_s, dk_s, dv_s, s_s, e_s, qt_s, gt_s = rest[5:]
    blocks = devices * local_blocks
    me = place[0]
    group = 2 * (me % 2) + gi
    units = 2 * local_blocks

    chunks = [range(c, min(c + CHUNK, listed)) for c in range(0, listed, CHUNK)]
    scale = jnp.concatenate(
        [jnp.full((1, BLOCK), taus[group * QPG + h], jnp.float32) for h in range(QPG)], axis=1
    ) / math.sqrt(HD)
    factor = scale * LOG2E

    def rows_of(c):
        return slice(c[0] * BLOCK, (c[-1] + 1) * BLOCK)

    def per_head(x):
        return [x[:, h * HD : (h + 1) * HD] for h in range(QPG)]

    def in_rows(x):
        return x.reshape(-1, 8, ROWS)

    tau_totals = []

    def part(n):
        s_n, e_n = s_s.at[n], e_s.at[n]
        side, at = n // local_blocks, n % local_blocks
        here = slice(at * BLOCK, (at + 1) * BLOCK)
        query_block = (me ^ side) * local_blocks + at
        wide = strides[group * blocks + query_block] == STRIDES[1]
        ids, bias = [], []
        for (narrow_off, narrow_times), (wide_off, wide_times) in zip(*offsets):
            ids.append((query_block + jnp.where(wide, wide_off, narrow_off)) % blocks)
            bias.append(
                times_bias(narrow_times)
                if narrow_times == wide_times
                else jnp.where(wide, times_bias(wide_times), times_bias(narrow_times))
            )

        def taken(which, c):
            return jnp.concatenate([kv_in[ids[j], which] for j in c], axis=0)

        def picked(ref, c, axis):
            return jnp.concatenate([ref[ids[j]] for j in c], axis=axis)

        def add_blocks(ref, c, x):
            for n, j in enumerate(c):
                ref[ids[j]] += x[n * BLOCK : (n + 1) * BLOCK, :]


        def rows_of_heads(own, sib):
            return jnp.concatenate(per_head(sib[0, here, :] if side else own[here, :]), axis=0)

        for own, sib, ref in ((q_own, q_sib, qt_s), (g_own, g_sib, gt_s)):
            heads = per_head(sib[0, here, :] if side else own[here, :])
            for h, x in enumerate(heads):
                ref[n, :, h * BLOCK : (h + 1) * BLOCK] = x.T
        most = None
        for c in chunks:
            raw = nt(taken(0, c), qt_s[n])
            s_n[rows_of(c), :] = raw
            top = jnp.max(in_rows(raw), axis=0)
            most = top if most is None else jnp.maximum(most, top)
            yield
        top_row = jnp.max(most, axis=0, keepdims=True) * factor
        total = jnp.zeros((8, ROWS), jnp.float32)
        for c in chunks:
            for j in c:
                rows = slice(j * BLOCK, (j + 1) * BLOCK)
                e = jnp.exp2(s_n[rows, :] * factor - (top_row - bias[j]))
                e_n[rows, :] = e
                total = total + jnp.sum(in_rows(e), axis=0)
            yield
        inverse = 1.0 / jnp.sum(total, axis=0, keepdims=True)
        o_t = jnp.zeros((HD, ROWS), jnp.float32)
        for c in chunks:
            probs = (e_n[rows_of(c), :] * inverse).astype(jnp.bfloat16)
            o_t = o_t + nt(picked(vt_s, c, 1), probs)
            add_blocks(dv_s, c, nt(probs, rows_of_heads(g_own, g_sib)))
            yield
        row_dot = jnp.sum(gt_s[n].astype(jnp.float32) * o_t, axis=0, keepdims=True)
        write(side, here, 0, o_t)
        weight_scale = inverse * scale
        tau_rows = jnp.zeros((8, ROWS), jnp.float32)
        dq_t = jnp.zeros((HD, ROWS), jnp.float32)
        for c in chunks:
            dweights = nt(taken(1, c), gt_s[n])
            scaled = e_n[rows_of(c), :] * weight_scale * (dweights - row_dot)
            tau_rows = tau_rows + jnp.sum(in_rows(scaled * s_n[rows_of(c), :]), axis=0)
            low = scaled.astype(jnp.bfloat16)
            dq_t = dq_t + nt(picked(kt_s, c, 1), low)
            add_blocks(dk_s, c, nt(low, rows_of_heads(q_own, q_sib)))
            yield
        tau_totals.append(tau_rows)
        write(side, here, 1, dq_t)

    def write(side, here, which, x_t):
        low = x_t.astype(jnp.bfloat16)
        out = jnp.concatenate([x.T for x in per_head(low)], axis=1)
        if side:
            sib_out[which, here, :] = out
        else:
            (att_own, dq_own)[which][here, :] = out

    def turned(which, ref, wait):
        turns = 2 * len(chunks)
        for turn in range(wait):
            yield
        for turn in range(turns):
            for b in range(blocks * turn // turns, blocks * (turn + 1) // turns):
                ref[b] = kv_in[b, which].T
            yield

    dk_s[...] = jnp.zeros_like(dk_s)
    dv_s[...] = jnp.zeros_like(dv_s)
    shares = [(0, turned(1, vt_s, 0)), (0, turned(0, kt_s, len(chunks)))]
    shares += [(n * len(chunks), part(n)) for n in range(units)]
    for turn in range((4 + units) * len(chunks)):
        for begin, share in shares:
            if turn >= begin:
                next(share, None)

    lane = lax.broadcasted_iota(jnp.int32, (TAIL, HD), 1)
    sums = inputs[5][...] if gi else jnp.zeros((TAIL, HD), jnp.float32)
    tau_rows = functools.reduce(jnp.add, tau_totals)
    for h in range(QPG):
        head = group * QPG + h
        total = jnp.sum(tau_rows[:, h * BLOCK : (h + 1) * BLOCK])
        sums = sums + jnp.where(lane == head, total / taus[head], 0.0)
    tau_out[...] = sums

    def drain(d, carry):
        for half in range(local_blocks):
            for which, ref in enumerate((dk_s, dv_s)):
                at = (2 * half + which) * BLOCK
                kv_out[d, at : at + BLOCK, :] = ref[d * local_blocks + half].astype(jnp.bfloat16)
        return carry

    lax.fori_loop(0, devices, drain, 0, unroll=2)


def times_bias(times):
    return math.log2(times) if times else NEVER


def run_group(gi, devices, place, strides, tau, queries, out_grad, qg_sib, kv_in, tau_in, offsets):
    listed = len(offsets[0])
    tokens = queries.shape[0]
    local_blocks = tokens // BLOCK
    blocks = devices * local_blocks
    width = QPG * HD
    block_own = pl.BlockSpec((tokens, width), lambda u, p, s, t: (0, 2 * (p[0] % 2) + gi), pipeline_mode=pl.Buffered(1))
    qs = pl.BlockSpec((1, tokens, width), lambda u, p, s, t: (0, 0, gi), pipeline_mode=pl.Buffered(1))
    gs = pl.BlockSpec((1, tokens, width), lambda u, p, s, t: (1, 0, gi), pipeline_mode=pl.Buffered(1))
    out_own = pl.BlockSpec((tokens, width), lambda u, p, s, t: (0, 0), pipeline_mode=pl.Buffered(1))
    out_sib = pl.BlockSpec((2, tokens, width), lambda u, p, s, t: (0, 0, 0), pipeline_mode=pl.Buffered(1))
    kv_all = pl.BlockSpec((blocks, 2, BLOCK, HD), lambda u, p, s, t: (0, 0, 0, 0), pipeline_mode=pl.Buffered(1))
    kv_back = pl.BlockSpec((devices, 2 * tokens, HD), lambda u, p, s, t: (0, 0, 0), pipeline_mode=pl.Buffered(1))
    small = pl.BlockSpec((TAIL, HD), lambda u, p, s, t: (0, 0), pipeline_mode=pl.Buffered(1))
    bf = lambda *shape: jax.ShapeDtypeStruct(shape, jnp.bfloat16)
    keys_wide = listed * BLOCK
    cells = 2 * local_blocks * ROWS * keys_wide
    return pl.pallas_call(
        functools.partial(group_kernel, gi, devices, local_blocks, listed, offsets),
        grid_spec=pltpu.PrefetchScalarGridSpec(
            num_scalar_prefetch=3,
            grid=(1,),
            in_specs=[block_own, qs, block_own, gs, kv_all] + [small] * gi,
            out_specs=[out_own, out_own, out_sib, small, kv_back],
            scratch_shapes=[pltpu.VMEM((blocks, HD, BLOCK), jnp.bfloat16)] * 2
            + [pltpu.VMEM((blocks, BLOCK, HD), jnp.float32)] * 2
            + [pltpu.VMEM((2 * local_blocks, keys_wide, ROWS), jnp.float32)] * 2
            + [pltpu.VMEM((2 * local_blocks, HD, ROWS), jnp.bfloat16)] * 2,
        ),
        out_shape=[bf(tokens, width), bf(tokens, width), bf(2, tokens, width)]
        + [jax.ShapeDtypeStruct((TAIL, HD), jnp.float32), bf(devices, 2 * tokens, HD)],
        compiler_params=pltpu.CompilerParams(
            dimension_semantics=("arbitrary",), vmem_limit_bytes=VMEM_BYTES
        ),
        cost_estimate=pl.CostEstimate(
            flops=12 * HD * cells, bytes_accessed=6 * 2**20, transcendentals=cells
        ),
        name="group_attention",
    )(place, strides, tau, queries, qg_sib, out_grad, qg_sib, kv_in, *tau_in[:gi])


def partners(x, axis, distances):
    size = lax.axis_size(axis)
    a, b, c = (lax.ppermute(x, axis, [(i, i ^ d) for i in range(size)]) for d in distances)
    return (x + a) + (b + c)


def total_everywhere(x, ready):
    ctx, batch = lax.axis_size("ctx"), lax.axis_size("batch")
    if batch != 4 or ctx not in (8, 32):
        return lax.psum(x, ("ctx", "batch")), ready
    x = x + lax.ppermute(x, "ctx", [(i, i ^ 1) for i in range(ctx)])
    a, b, c = (lax.ppermute(x, "batch", [(i, i ^ d) for i in range(batch)]) for d in (1, 2, 3))
    x, ready = lax.optimization_barrier((x + a, ready))
    x = x + (b + c)
    step = 2
    while step < ctx:
        x = partners(x, "ctx", (step, 2 * step, 3 * step))
        step *= 4
    return x, ready


def spread(gi, devices, keys, values):
    tokens = keys.shape[0]
    local_blocks = tokens // BLOCK

    def kernel(*refs):
        columns, out, piece, sems = refs[:4], refs[4], refs[5], refs[6]
        for n, ref in enumerate(columns):
            for half in range(local_blocks):
                piece[n % 2, half, n // 2] = ref[half * BLOCK : (half + 1) * BLOCK, :]
        copies = [
            pltpu.make_async_copy(piece, out.at[pl.ds(2 * d, 2)], sems.at[d]) for d in range(devices // 2)
        ]
        for copy in copies:
            copy.start()
        for copy in copies:
            copy.wait()

    def column(group):
        return pl.BlockSpec((tokens, HD), lambda n: (0, group), pipeline_mode=pl.Buffered(1))

    block = (2, local_blocks, 2, BLOCK, HD)
    return pl.pallas_call(
        kernel,
        grid=(1,),
        in_specs=[column(gi), column(2 + gi)] * 2,
        out_specs=pl.BlockSpec(memory_space=pl.ANY),
        out_shape=jax.ShapeDtypeStruct((devices, *block[1:]), jnp.bfloat16),
        scratch_shapes=[pltpu.VMEM(block, jnp.bfloat16), pltpu.SemaphoreType.DMA((devices // 2,))],
        compiler_params=pltpu.CompilerParams(vmem_limit_bytes=VMEM_BYTES),
        name="spread_keys_values",
    )(keys, keys, values, values)


def body(queries, keys, values, tau, out_grad, key_blocks):
    ctx = lax.axis_size("ctx")
    me = lax.axis_index("ctx").astype(jnp.int32)
    core = me % 2
    tokens = queries.shape[1]
    local_blocks = tokens // BLOCK
    block_count = ctx * local_blocks
    listed_count = key_blocks.shape[2]
    offsets = distinct_offsets(block_count, listed_count)
    swap = [(d, d ^ 1) for d in range(ctx)]
    wide = 2 * QPG * HD

    q0, k0, v0, g0 = queries[0], keys[0], values[0], out_grad[0]
    place = me[None]

    def kv_for(gi):
        arrived = lax.all_to_all(spread(gi, ctx, k0, v0), "ctx", 0, 0)
        return arrived.reshape(block_count, 2, BLOCK, HD)

    def theirs(x):
        return lax.dynamic_slice_in_dim(x, (1 - core) * wide, wide, 1)

    kv_in = [kv_for(gi) for gi in range(2)]
    strides = (key_blocks[:, :, 3] - jnp.arange(block_count, dtype=jnp.int32)) % block_count
    rows, strides = lax.optimization_barrier((jnp.stack([theirs(q0), theirs(g0)]), strides.reshape(-1)))
    qg_sib = lax.ppermute(rows, "ctx", swap)

    sibs, owns, grads, tau_rows = [], [], [], []
    for gi in range(2):
        att_own, dq_own, sib, tau_here, kv_grads = run_group(
            gi, ctx, place, strides, tau, q0, g0, qg_sib, kv_in[gi], tau_rows, offsets
        )
        tau_rows.append(tau_here)
        owns.append((att_own, dq_own))
        sibs.append(sib)
        grads.append(kv_grads)
        if gi == 0:
            grads[0] = lax.all_to_all(kv_grads, "ctx", 0, 0)
    grads, sibs, tau_last = lax.optimization_barrier((grads, sibs, tau_rows[1]))
    grads[1] = lax.all_to_all(grads[1], "ctx", 0, 0)
    sibs = lax.optimization_barrier([lax.ppermute(sib, "ctx", swap) for sib in sibs])
    att_parts, dq_parts = (
        [(own[which], sib[which]) for own, sib in zip(owns, sibs)] for which in range(2)
    )

    def by_group(parts):
        return jnp.concatenate(
            [jnp.where(core == c // 2, parts[c % 2][0], parts[c % 2][1]) for c in range(4)], axis=1
        )

    attended = by_group(att_parts)[None]
    query_grad = by_group(dq_parts)[None]

    def summed(gi):
        columns = []
        for which in range(2):
            for parity in range(2):
                total = None
                for src in range(parity, ctx, 2):
                    term = grads[gi][src].reshape(local_blocks, 2, BLOCK, HD)[:, which]
                    term = term.astype(jnp.float32)
                    total = term if total is None else total + term
                columns.append(total.reshape(tokens, HD).astype(jnp.bfloat16))
        return columns

    scale_total, (attended, query_grad) = total_everywhere(tau_last, (attended, query_grad))
    first, second = summed(0), summed(1)
    key_grad, value_grad = (
        jnp.concatenate([first[i], second[i], first[i + 1], second[i + 1]], axis=1)[None]
        for i in (0, 2)
    )
    scale_total = scale_total[0, :HEADS]
    tau_grad = scale_total / math.sqrt(lax.axis_size("batch") * ctx * tokens)
    return (attended, query_grad, key_grad, value_grad, tau_grad)


def solution(mesh):
    rows = P("batch", "ctx", None)
    return jax.shard_map(
        body,
        mesh=mesh,
        in_specs=(rows, rows, rows, P(), rows, P()),
        out_specs=(rows, rows, rows, rows, P()),
        check_vma=False,
    )
```
